256 devices in a mesh: prow: 8 (over y, core), pcol: 32 (over x, z).
Axes of the slice: x: 4, y: 4, z: 8, core: 2. Of those that a mesh axis runs over, the one named last changes fastest.
Arguments:
- trailing: float32 [16384, 16384], P('prow', 'pcol'), as said below
- panel: float32 [16384, 256], P('prow', 'pcol'), as said below
Outputs:
- updated: float32 [16384, 16384], P('prow', 'pcol')
- work_matrix: float32 [16384, 256], P('prow', 'pcol')
Inputs may be any that keep to these rules, and one draw needn't show every extreme that they name: trailing equals its transpose. panel has full column rank.
All inputs are finite; a program needn't handle non-finite values.
Results may differ from the reference program's by a relative error of at most 0.00016.
Values sent between devices are 32-bit elements; how exact they have to be, the bound alone decides.
A program may use at most 128 MiB of HBM per device.

```python
import math
import jax
import jax.numpy as jnp
from jax import lax

M = 16384
NB = 256


def draw_trailing(key, part):
    key = jax.random.fold_in(key, 11)
    base = jax.random.normal(key, (M, M), jnp.float32)
    return (base + base.T) * 0.7071


def row_ramp():
    return jnp.arange(M, dtype=jnp.float32)[:, None] / M


def draw_panel(key, part):
    key = jax.random.fold_in(key, 23)
    key_vals, key_cols = jax.random.split(key)
    ramp = 1.0 + 2.0 * row_ramp()
    col_scale = jnp.exp(jax.random.uniform(key_cols, (1, NB), jnp.float32, 0.0, math.log(10.0)))
    vals = jax.random.normal(key_vals, (M, NB), jnp.float32)
    return vals * ramp * col_scale


def setup_inputs(seed: int = 0) -> dict:
    arg_keys = jax.random.split(jax.random.key(seed), 3)
    return {
        "trailing": draw_trailing(jax.random.fold_in(arg_keys[2], 71), 0),
        "panel": draw_panel(jax.random.fold_in(arg_keys[2], 71), 0),
    }


HIGH = lax.Precision.HIGHEST

def matmul(left, right):
    return jnp.dot(left, right, precision=HIGH, preferred_element_type=jnp.float32)

def lower_pair(gram):
    size = gram.shape[0]
    if size == 1:
        root = jnp.sqrt(gram)
        return (root, 1.0 / root)
    half = size // 2
    l_top, i_top = lower_pair(gram[:half, :half])
    l_side = matmul(gram[half:, :half], i_top.T)
    l_bot, i_bot = lower_pair(gram[half:, half:] - matmul(l_side, l_side.T))
    zero_block = jnp.zeros((half, size - half), gram.dtype)
    lower = jnp.concatenate([jnp.concatenate([l_top, zero_block], 1), jnp.concatenate([l_side, l_bot], 1)], 0)
    i_side = -matmul(i_bot, matmul(l_side, i_top))
    inverse = jnp.concatenate([jnp.concatenate([i_top, zero_block], 1), jnp.concatenate([i_side, i_bot], 1)], 0)
    return (lower, inverse)

def upper_inverse(matrix):
    size = matrix.shape[0]
    if size == 1:
        return 1.0 / matrix
    half = size // 2
    i_top = upper_inverse(matrix[:half, :half])
    i_bot = upper_inverse(matrix[half:, half:])
    i_side = -matmul(i_top, matmul(matrix[:half, half:], i_bot))
    zero_block = jnp.zeros((size - half, half), matrix.dtype)
    return jnp.concatenate([jnp.concatenate([i_top, i_side], 1), jnp.concatenate([zero_block, i_bot], 1)], 0)

def reference(trailing, panel):
    gram = matmul(panel.T, panel)
    lower, lower_inv = lower_pair(gram)
    basis = matmul(panel, lower_inv.T)
    row_ids = lax.broadcasted_iota(jnp.int32, (M, NB), 0)
    col_ids = lax.broadcasted_iota(jnp.int32, (M, NB), 1)
    vectors = basis - (row_ids == col_ids).astype(jnp.float32)
    ygram = matmul(vectors.T, vectors)
    tinv = jnp.triu(ygram, 1) + 0.5 * jnp.diag(jnp.diag(ygram))
    tmat = upper_inverse(tinv)
    product = matmul(trailing, vectors)
    xmat = matmul(product, tmat)
    mproj = matmul(vectors.T, xmat)
    inner = matmul(tmat.T, mproj)
    work_matrix = xmat - 0.5 * matmul(vectors, inner)
    left = jnp.concatenate([vectors, work_matrix], axis=1)
    right = jnp.concatenate([work_matrix, vectors], axis=1)
    updated = trailing - matmul(left, right.T)
    return (updated, work_matrix)
```

```python
import functools

import jax
import jax.numpy as jnp
from jax import lax
from jax.experimental import pallas as pl
from jax.experimental.pallas import tpu as pltpu
from jax.sharding import PartitionSpec as P

HIGH = lax.Precision.HIGHEST
F32 = jnp.float32
NX, NZ, NY = 4, 8, 4
VMEM = pl.BlockSpec(memory_space=pltpu.VMEM)
ANY = pl.BlockSpec(memory_space=pl.ANY)
LIMIT = 48 << 20
NN, NT, TN = ((1,), (0,)), ((1,), (1,)), ((0,), (0,))


def mm(a, b, dims=NN):
    return lax.dot_general(a, b, (dims, ((), ())), precision=HIGH, preferred_element_type=F32)


def split(x):
    hi = x.astype(jnp.bfloat16)
    return hi, (x - hi.astype(F32)).astype(jnp.bfloat16)


def mm3(a, b, dims=NN):
    (ah, al), (bh, bl) = a, b

    def dot(l, r):
        return lax.dot_general(l, r, (dims, ((), ())), preferred_element_type=F32)

    return dot(ah, bh) + (dot(ah, bl) + dot(al, bh))


def iota(shape, dim):
    return lax.broadcasted_iota(jnp.int32, shape, dim)


BASE = 64


def base_inverse(block):
    n = BASE
    row = iota((8, 128), 0)
    eye = (iota((n, n), 0) == iota((n, n), 1)).astype(F32)
    x = jnp.concatenate([block, eye], axis=1)
    groups = [x[8 * g : 8 * g + 8, :] for g in range(n // 8)]
    zero = jnp.zeros((8, 128), F32)

    def column(vals):
        v = zero
        for i, e in enumerate(vals):
            if e is not None:
                v = jnp.where(row == i, e, v)
        return v

    out = []
    for k in range(n // 8):
        gk = groups[k]
        rows = [jnp.broadcast_to(gk[m : m + 1, :], (8, 128)) for m in range(8)]
        a = [[None] * 8 for _ in range(8)]
        for i in range(8):
            for j in range(i + 1):
                a[i][j] = jnp.broadcast_to(rows[j][:, 8 * k + i : 8 * k + i + 1], (8, 128))
        acols = {
            g: [jnp.broadcast_to(groups[g][:, 8 * k + m : 8 * k + m + 1], (8, 128)) for m in range(8)]
            for g in range(k + 1, n // 8)
        }
        l = [[None] * 8 for _ in range(8)]
        r = [None] * 8
        for j in range(8):
            r[j] = lax.rsqrt(a[j][j])
            for i in range(j + 1, 8):
                l[i][j] = a[i][j] * r[j]
            for i in range(j + 1, 8):
                for c in range(j + 1, i + 1):
                    a[i][c] = a[i][c] - l[i][j] * l[c][j]
        w = [[None] * 8 for _ in range(8)]
        for j in range(8):
            w[j][j] = r[j]
            for i in range(j + 1, 8):
                s = l[i][j] * w[j][j]
                for c in range(j + 1, i):
                    s = s + l[i][c] * w[c][j]
                w[i][j] = -(s * r[i])
        cols = [column([w[i][m] for i in range(8)]) for m in range(8)]
        u = cols[0] * rows[0]
        for m in range(1, 8):
            u = u + cols[m] * rows[m]
        out.append(u)
        if k + 1 < n // 8:
            cols_t = [column([w[j][m] for m in range(8)]) for j in range(8)]
            z = cols_t[0] * jnp.broadcast_to(u[0:1, :], (8, 128))
            for j in range(1, 8):
                z = z + cols_t[j] * jnp.broadcast_to(u[j : j + 1, :], (8, 128))
            z_rows = [jnp.broadcast_to(z[m : m + 1, :], (8, 128)) for m in range(8)]
            for g in range(k + 1, n // 8):
                s = acols[g][0] * z_rows[0]
                for m in range(1, 8):
                    s = s + acols[g][m] * z_rows[m]
                groups[g] = groups[g] - s
    inv = jnp.concatenate(out, axis=0)[:, n:]
    return jnp.where(iota((n, n), 1) <= iota((n, n), 0), inv, 0.0)


def lower_inverse(gram):
    size = gram.shape[0]
    if size == BASE:
        return base_inverse(gram)
    h = size // 2
    i_top = lower_inverse(gram[:h, :h])
    l_side = mm(gram[h:, :h], i_top, NT)
    i_bot = lower_inverse(gram[h:, h:] - mm(l_side, l_side, NT))
    i_side = -mm(i_bot, mm(l_side, i_top))
    top = jnp.concatenate([i_top, jnp.zeros((h, h), F32)], 1)
    return jnp.concatenate([top, jnp.concatenate([i_side, i_bot], 1)], 0)


def upper_inverse(y):
    n = y.shape[0]
    r, c = iota((n, n), 0), iota((n, n), 1)
    inv = jnp.where(r == c, 1.0 / y, 0.0)
    s = 1
    while s < n:
        off = (r // (2 * s) == c // (2 * s)) & (r // s != c // s) & (r < c)
        inv = inv - mm(inv, mm(jnp.where(off, y, 0.0), inv))
        s *= 2
    return inv


def meet(peers):
    barrier = pltpu.get_barrier_semaphore()
    for peer in peers:
        pl.semaphore_signal(barrier, inc=1, device_id=peer, device_id_type=pl.DeviceIdType.MESH)
    pl.semaphore_wait(barrier, len(peers))


def remote(src, dst, send, recv, peer):
    return pltpu.make_async_remote_copy(
        src_ref=src, dst_ref=dst, send_sem=send, recv_sem=recv, device_id=peer, device_id_type=pl.DeviceIdType.MESH
    )


def place():
    prow, pcol = lax.axis_index("prow"), lax.axis_index("pcol")
    return prow // 2, prow % 2, pcol // NZ, pcol % NZ


def gather_peers():
    _, _, x, z = place()
    peers = [{"pcol": x * NZ + (z + 1) % NZ}, {"pcol": x * NZ + (z + NZ - 1) % NZ}]
    return peers + [{"pcol": (x + dx) % NX * NZ + z} for dx in range(1, NX)]


def gather(rows, out, send, recv):
    _, core, x, z = place()

    def slab(xx, zz):
        start = (xx % NX * NZ + (zz + 2 * NZ) % NZ) * rows
        return out.at[pl.ds(pl.multiple_of(start, rows), rows)]

    def along_z(dx, dist):
        step = 1 if dist <= NZ // 2 else -1
        piece = slab(x + dx, z + step - dist)
        return remote(piece, piece, send.at[dx, dist], recv.at[dx, dist], {"pcol": x * NZ + (z + step + NZ) % NZ})

    def along_x(dx, dist):
        piece = slab(x, z - dist)
        return remote(piece, piece, send.at[dx, dist], recv.at[dx, dist], {"pcol": (x + NX - dx) % NX * NZ + z})

    def arrived(dx, dist):
        piece = slab(x + dx, z - dist)
        remote(piece, piece, send.at[dx, dist], recv.at[dx, dist], {"pcol": x * NZ + (z + 1) % NZ}).wait_recv()

    def passed_on(dx, dist):
        if dist < NZ // 2:
            along_z(dx, dist + 1).start()
        elif dist > NZ // 2 + 1:
            along_z(dx, dist - 1).start()

    order = (1, 7, 2, 6, 3, 5, 4)

    @pl.when(core == 0)
    def _():
        along_z(0, 1).start()
        along_z(0, NZ - 1).start()
        for dx in range(1, NX):
            along_x(dx, 0).start()
        for dist in order:
            arrived(0, dist)
            passed_on(0, dist)
            for dx in range(1, NX):
                along_x(dx, dist).start()
        for dist in (0,) + order:
            for dx in range(1, NX):
                arrived(dx, dist)

    @pl.when(core == 1)
    def _():
        for dx in range(1, NX):
            along_x(dx, 0).start()
        along_z(0, 1).start()
        along_z(0, NZ - 1).start()
        for dx in range(1, NX):
            arrived(dx, 0)
            along_z(dx, 1).start()
            along_z(dx, NZ - 1).start()
        for dist in order:
            for dx in range(NX):
                arrived(dx, dist)
                passed_on(dx, dist)

    for dx in range(NX):
        for dist in range(NZ):
            if dx or dist:
                piece = slab(x, z)
                remote(piece, piece, send.at[dx, dist], recv.at[dx, dist], {"pcol": x * NZ + (z + 1) % NZ}).wait_send()


def column_peers():
    y, core, _, _ = place()
    peers = [{"prow": (y + dy) % NY * 2 + core} for dy in range(1, NY)]
    return peers + [{"prow": y * 2 + 1 - core}]


class Broadcast:
    def __init__(self, y0, core0, src, out, send, recv):
        y, core, _, _ = place()
        self.owner = (y == y0) & (core == core0)
        self.relay = (y != y0) & (core == core0)
        self.leaf = core != core0
        self.along = [
            remote(src, out, send.at[dy], recv.at[0], {"prow": (y + dy) % NY * 2 + core}) for dy in range(1, NY)
        ]
        self.own = remote(src, out, send.at[0], recv.at[0], {"prow": y * 2 + 1 - core})
        self.pass_on = remote(out, out, send.at[0], recv.at[0], {"prow": y * 2 + 1 - core})
        self.keep = pltpu.make_async_copy(src, out, send.at[NY])

    def start(self):
        @pl.when(self.owner)
        def _():
            for copy in self.along:
                copy.start()
            self.own.start()
            self.keep.start()

    def finish(self):
        @pl.when(self.relay)
        def _():
            self.pass_on.wait_recv()
            self.pass_on.start()
            self.pass_on.wait_send()

        @pl.when(self.leaf)
        def _():
            self.pass_on.wait_recv()

        @pl.when(self.owner)
        def _():
            for copy in self.along:
                copy.wait_send()
            self.own.wait_send()
            self.keep.wait()


def panel_kernel(slab_ref, a_ref, out_ref, top_ref, send, recv, tsend, trecv):
    _, _, x, z = place()
    rows = slab_ref.shape[0]
    out_ref[pl.ds(pl.multiple_of((x * NZ + z) * rows, rows), rows), :] = slab_ref[...]
    meet(gather_peers() + column_peers())
    top = Broadcast(0, 0, a_ref.at[pl.ds(0, top_ref.shape[0])], top_ref, tsend, trecv)
    top.start()
    gather(rows, out_ref, send, recv)
    top.finish()


def rows_kernel(xc_ref, pt_ref, out_ref, pc_ref, first, send, recv, psend, precv, fsem):
    y, core, x, z = place()
    prow, pcol = y * 2 + core, x * NZ + z
    rows = first.shape[0]
    cols = pc_ref.shape[1]
    mine = xc_ref.at[pl.ds(pl.multiple_of(prow * rows, rows), rows)]
    to_row, to_col = pcol // 4, pcol % 4 * 8 + prow
    from_col, from_row = prow * 4 + pcol // 8, pcol % 8
    stays = (to_row == prow) & (to_col == pcol)
    target = {"prow": to_row, "pcol": to_col}
    source = {"prow": from_row, "pcol": from_col}

    barrier = pltpu.get_barrier_semaphore()
    peers = gather_peers() + column_peers()
    for peer in peers:
        pl.semaphore_signal(barrier, inc=1, device_id=peer, device_id_type=pl.DeviceIdType.MESH)

    @pl.when(jnp.logical_not(stays))
    def _():
        pl.semaphore_signal(barrier, inc=1, device_id=target, device_id_type=pl.DeviceIdType.MESH)
        pl.semaphore_signal(barrier, inc=1, device_id=source, device_id_type=pl.DeviceIdType.MESH)
        pl.semaphore_wait(barrier, len(peers) + 2)

    @pl.when(stays)
    def _():
        pl.semaphore_wait(barrier, len(peers))

    out_own = pl.ds(pl.multiple_of(pcol * rows, rows), rows)
    swap = remote(mine, first, fsem.at[0], fsem.at[1], target)

    @pl.when(jnp.logical_not(stays))
    def _():
        swap.start()

    offset = pl.multiple_of(pcol % 4 * cols, cols)
    part = Broadcast(x, z // 4, pt_ref.at[:, pl.ds(offset, cols)], pc_ref, psend, precv)
    part.start()

    @pl.when(jnp.logical_not(stays))
    def _():
        swap.wait_recv()
        out_ref[out_own, :] = first[...]

    @pl.when(stays)
    def _():
        out_ref[out_own, :] = xc_ref[pl.ds(pl.multiple_of(prow * rows, rows), rows), :]

    gather(rows, out_ref, send, recv)
    part.finish()

    @pl.when(jnp.logical_not(stays))
    def _():
        swap.wait_send()


def reduce_kernel(extra, *refs):
    if extra:
        s_ref, e_ref, out_ref, half, quarter, acc, send, recv, esend, erecv = refs
    else:
        s_ref, out_ref, half, quarter, acc, send, recv = refs
        e_ref = esend = erecv = None
    y, core, _, _ = place()
    prow = y * 2 + core
    width = s_ref.shape[1]
    q = s_ref.shape[0] // 8
    h = 4 * q
    mate = {"prow": y * 2 + 1 - core}

    def along(dy):
        return {"prow": (y + dy) % NY * 2 + core}

    meet([{"prow": (prow + d) % 8} for d in range(1, 8)])

    def rows(start, n):
        return pl.ds(pl.multiple_of(start, n), n)

    own = rows(core * h + y * q, q)
    exchange = remote(s_ref.at[rows((1 - core) * h, h)], half, send.at[0], recv.at[0], mate)
    exchange.start()
    handed = []
    if extra:
        for r in range(1, 8):
            piece = pl.ds(r % 2 * h + r // 2 * q, q)
            handed.append(
                remote(
                    e_ref.at[piece, pl.ds(0, extra)],
                    out_ref.at[piece, pl.ds(width, extra)],
                    esend.at[r],
                    erecv.at[0],
                    {"prow": r},
                )
            )

        @pl.when(prow == 0)
        def _():
            for copy in handed:
                copy.start()
            out_ref[pl.ds(0, q), pl.ds(width, extra)] = e_ref[pl.ds(0, q), pl.ds(0, extra)]

    exchange.wait_recv()
    acc[...] = s_ref[rows(core * h, h), :] + half[...]
    quarters = []
    for dy in range(1, NY):
        to = (y + dy) % NY
        quarters.append(remote(acc.at[rows(to * q, q)], quarter.at[dy], send.at[dy], recv.at[dy], along(dy)))
        quarters[-1].start()
    total = acc[rows(y * q, q), :]
    for copy, dy in zip(quarters, range(1, NY)):
        copy.wait_recv()
        total = total + quarter[dy]
    out_ref[own, pl.ds(0, width)] = total
    if extra:

        @pl.when(prow != 0)
        def _():
            remote(e_ref.at[own, pl.ds(0, extra)], out_ref.at[own, pl.ds(width, extra)], esend.at[0], erecv.at[0], mate).wait_recv()

    done = []
    for dy in range(1, NY):
        done.append(remote(out_ref.at[own], out_ref.at[own], send.at[3 + dy], recv.at[3 + dy], along(dy)))
        done[-1].start()
    passed = [remote(out_ref.at[own], out_ref.at[own], send.at[7], recv.at[7], mate)]
    passed[0].start()
    for dy in range(1, NY):
        theirs = rows(core * h + (y + NY - dy) % NY * q, q)
        remote(out_ref.at[theirs], out_ref.at[theirs], send.at[3 + dy], recv.at[3 + dy], mate).wait_recv()
        passed.append(remote(out_ref.at[theirs], out_ref.at[theirs], send.at[7 + dy], recv.at[7 + dy], mate))
        passed[-1].start()
    for dy in range(NY):
        theirs = rows((1 - core) * h + (y + NY - dy) % NY * q, q)
        remote(out_ref.at[theirs], out_ref.at[theirs], send.at[7 + dy], recv.at[7 + dy], mate).wait_recv()
    for copy in [exchange] + quarters + done + passed:
        copy.wait_send()
    if extra:

        @pl.when(prow == 0)
        def _():
            for copy in handed:
                copy.wait_send()


def params(cid):
    return pltpu.CompilerParams(collective_id=cid, has_side_effects=True, vmem_limit_bytes=LIMIT)


def plain(**kw):
    return pltpu.CompilerParams(vmem_limit_bytes=LIMIT, **kw)


def shape(*dims):
    return jax.ShapeDtypeStruct(dims, F32)


def all_reduce(s, e, extra, cid):
    n, width = s.shape
    dma = pltpu.SemaphoreType.DMA
    scratch = [pltpu.VMEM((n // 2, width), F32), pltpu.VMEM((4, n // 8, width), F32), pltpu.VMEM((n // 2, width), F32)]
    scratch += [dma((11,)), dma((11,))]
    args = [s]
    if extra:
        args.append(e)
        scratch += [dma((8,)), dma((1,))]
    return pl.pallas_call(
        functools.partial(reduce_kernel, extra),
        out_shape=shape(n, width + extra),
        in_specs=[VMEM] * len(args),
        out_specs=VMEM,
        scratch_shapes=scratch,
        compiler_params=params(cid),
    )(*args)


def products_kernel(pt_ref, a_ref, s_ref):
    pt = pt_ref[...]
    nb = pt.shape[0]
    s_ref[:, 0:nb] = mm(pt, pt, NT)
    s_ref[:, nb:] = mm3(split(pt), split(a_ref[...]))


def factor_kernel(s_ref, ae_ref, linv_ref, t_ref, xct_ref, xc_ref):
    nb = s_ref.shape[0]
    cols = ae_ref.shape[1]
    linv = lower_inverse(s_ref[:, 0:nb])
    linv_ref[...] = linv
    side = mm(linv, s_ref[:, nb + cols :])
    r, c = iota((nb, nb), 0), iota((nb, nb), 1)
    eye = (r == c).astype(F32)
    ygram = 2.0 * eye - side - mm(s_ref[:, nb + cols :], linv, ((0,), (1,)))
    t = upper_inverse(jnp.where(r < c, ygram, jnp.where(r == c, 0.5 * ygram, 0.0)))
    t_ref[...] = t
    avt = mm(linv, s_ref[:, nb : nb + cols]) - ae_ref[...]
    xct = mm(t, avt, TN)
    xct_ref[...] = xct
    xc_ref[...] = xct.T


def project_kernel(pt_ref, xr_ref, linv_ref, m_ref):
    nb = pt_ref.shape[0]
    m = mm(linv_ref[...], mm3(split(pt_ref[...]), split(xr_ref[...])))
    first = lax.axis_index("prow") == 0
    m_ref[...] = m - jnp.where(first, xr_ref[0:nb, :], 0.0)


def update_kernel(a_ref, pt_ref, xr_ref, pct_ref, xct_ref, linv_ref, t_ref, m_ref, o_ref, w_ref, bh, bl, vh, vl, bt, kl):
    nb, cols = pct_ref.shape
    step = pl.program_id(0)
    prow, pcol = lax.axis_index("prow"), lax.axis_index("pcol")
    at_top = (prow == 0) & (step == 0)

    @pl.when(step == 0)
    def _():
        linv = linv_ref[...]
        vct = mm(linv, pct_ref[...])
        e = (iota((nb, cols), 0) == iota((nb, cols), 1)) & (pcol == 0)
        vct = vct - e.astype(F32)
        k = mm(t_ref[...], m_ref[...], TN)
        wct = xct_ref[...] - 0.5 * mm(k, vct, TN)
        b = wct - 0.5 * mm(k, vct)
        bt[...] = b
        bh[...], bl[...] = split(mm(linv, b, TN))
        vh[...], vl[...] = split(vct)
        sel = (iota((8, nb), 1) == iota((8, nb), 0) + 8 * pcol).astype(F32)
        kt = mm(sel, k, NT)
        kl[0:8, :] = kt
        kl[8:16, :] = mm(kt, linv)
        kl[16:24, :] = sel

    p, x = pt_ref[...], xr_ref[...]
    ps, xs = split(p), split(x)
    both = mm3(ps, (bh[...], bl[...]), TN) + mm3(xs, (vh[...], vl[...]))
    o_ref[...] = a_ref[...] - both
    w_ref[...] = mm(kl[16:24, :], x, NT) - 0.5 * mm(kl[8:16, :], p)

    @pl.when(at_top)
    def _():
        o_ref[...] += bt[...]
        w_ref[...] += 0.5 * kl[0:8, :]


def shards(trailing, panel):
    rows, cols = trailing.shape
    pt_own = panel.T
    nc = pt_own.shape[0]
    nb = nc * lax.axis_size("pcol")
    dma = pltpu.SemaphoreType.DMA

    pt, ae = pl.pallas_call(
        panel_kernel,
        out_shape=(shape(nb, rows), shape(nb, cols)),
        in_specs=[VMEM, ANY],
        out_specs=(VMEM, VMEM),
        scratch_shapes=[dma((NX, NZ)), dma((NX, NZ)), dma((NY + 1,)), dma((1,))],
        compiler_params=params(1),
    )(pt_own, trailing)

    s = pl.pallas_call(
        products_kernel,
        out_shape=shape(nb, nb + cols),
        in_specs=[VMEM, VMEM],
        out_specs=VMEM,
        compiler_params=plain(),
    )(pt, trailing)

    s = all_reduce(s, pt, nb, 2)

    linv, t, xct, xc = pl.pallas_call(
        factor_kernel,
        out_shape=(shape(nb, nb), shape(nb, nb), shape(nb, cols), shape(cols, nb)),
        in_specs=[VMEM, VMEM],
        out_specs=(VMEM,) * 4,
        compiler_params=plain(),
    )(s, ae)

    xr, pct = pl.pallas_call(
        rows_kernel,
        out_shape=(shape(rows, nb), shape(nb, cols)),
        in_specs=[VMEM, VMEM],
        out_specs=(VMEM, VMEM),
        scratch_shapes=[
            pltpu.VMEM((cols // 8, nb), F32),
            dma((NX, NZ)),
            dma((NX, NZ)),
            dma((NY + 1,)),
            dma((1,)),
            dma((2,)),
        ],
        compiler_params=params(3),
    )(xc, pt)

    m = pl.pallas_call(
        project_kernel,
        out_shape=shape(nb, nb),
        in_specs=[VMEM] * 3,
        out_specs=VMEM,
        compiler_params=plain(),
    )(pt, xr, linv)
    m = all_reduce(m, None, 0, 4)

    tile = nb
    whole = lambda *dims: pl.BlockSpec(dims, lambda i: (0, 0))
    updated, wt = pl.pallas_call(
        update_kernel,
        grid=(rows // tile,),
        out_shape=(shape(rows, cols), shape(nc, rows)),
        in_specs=[
            pl.BlockSpec((tile, cols), lambda i: (i, 0)),
            pl.BlockSpec((nb, tile), lambda i: (0, i)),
            pl.BlockSpec((tile, nb), lambda i: (i, 0)),
            whole(nb, cols),
            whole(nb, cols),
            whole(nb, nb),
            whole(nb, nb),
            whole(nb, nb),
        ],
        out_specs=(pl.BlockSpec((tile, cols), lambda i: (i, 0)), pl.BlockSpec((nc, tile), lambda i: (0, i))),
        scratch_shapes=[pltpu.VMEM((nb, cols), jnp.bfloat16)] * 4 + [pltpu.VMEM((nb, cols), F32), pltpu.VMEM((24, nb), F32)],
        compiler_params=plain(dimension_semantics=("arbitrary",)),
    )(trailing, pt, xr, pct, xct, linv, t, m)
    return updated, wt.T


def solution(mesh):
    in_specs = (P("prow", "pcol"), P("prow", "pcol"))
    out_specs = (P("prow", "pcol"), P("prow", "pcol"))
    return jax.shard_map(shards, mesh=mesh, in_specs=in_specs, out_specs=out_specs, check_vma=False)
```

```python
import jax
import jax.numpy as jnp
from jax import lax
from jax.experimental import pallas as pl
from jax.experimental.pallas import tpu as pltpu
from jax.sharding import PartitionSpec as P

HIGH = lax.Precision.HIGHEST
F32 = jnp.float32
NX, NZ, NY = 4, 8, 4
VMEM = pl.BlockSpec(memory_space=pltpu.VMEM)
ANY = pl.BlockSpec(memory_space=pl.ANY)
LIMIT = 48 << 20
NN, NT, TN = ((1,), (0,)), ((1,), (1,)), ((0,), (0,))


def mm(a, b, dims=NN):
    return lax.dot_general(a, b, (dims, ((), ())), precision=HIGH, preferred_element_type=F32)


def split(x):
    hi = x.astype(jnp.bfloat16)
    return hi, (x - hi.astype(F32)).astype(jnp.bfloat16)


def mm3(a, b, dims=NN):
    (ah, al), (bh, bl) = a, b

    def dot(l, r):
        return lax.dot_general(l, r, (dims, ((), ())), preferred_element_type=F32)

    return dot(ah, bh) + (dot(ah, bl) + dot(al, bh))


def iota(shape, dim):
    return lax.broadcasted_iota(jnp.int32, shape, dim)


BASE = 64


def base_inverse(block):
    n = BASE
    row = iota((8, 128), 0)
    eye = (iota((n, n), 0) == iota((n, n), 1)).astype(F32)
    x = jnp.concatenate([block, eye], axis=1)
    groups = [x[8 * g : 8 * g + 8, :] for g in range(n // 8)]
    zero = jnp.zeros((8, 128), F32)

    def column(vals):
        v = zero
        for i, e in enumerate(vals):
            if e is not None:
                v = jnp.where(row == i, e, v)
        return v

    out = []
    for k in range(n // 8):
        gk = groups[k]
        rows = [jnp.broadcast_to(gk[m : m + 1, :], (8, 128)) for m in range(8)]
        a = [[None] * 8 for _ in range(8)]
        for i in range(8):
            for j in range(i + 1):
                a[i][j] = jnp.broadcast_to(rows[j][:, 8 * k + i : 8 * k + i + 1], (8, 128))
        acols = {
            g: [jnp.broadcast_to(groups[g][:, 8 * k + m : 8 * k + m + 1], (8, 128)) for m in range(8)]
            for g in range(k + 1, n // 8)
        }
        l = [[None] * 8 for _ in range(8)]
        r = [None] * 8
        for j in range(8):
            r[j] = lax.rsqrt(a[j][j])
            for i in range(j + 1, 8):
                l[i][j] = a[i][j] * r[j]
            for i in range(j + 1, 8):
                for c in range(j + 1, i + 1):
                    a[i][c] = a[i][c] - l[i][j] * l[c][j]
        w = [[None] * 8 for _ in range(8)]
        for j in range(8):
            w[j][j] = r[j]
            for i in range(j + 1, 8):
                s = l[i][j] * w[j][j]
                for c in range(j + 1, i):
                    s = s + l[i][c] * w[c][j]
                w[i][j] = -(s * r[i])
        cols = [column([w[i][m] for i in range(8)]) for m in range(8)]
        u = cols[0] * rows[0]
        for m in range(1, 8):
            u = u + cols[m] * rows[m]
        out.append(u)
        if k + 1 < n // 8:
            cols_t = [column([w[j][m] for m in range(8)]) for j in range(8)]
            z = cols_t[0] * jnp.broadcast_to(u[0:1, :], (8, 128))
            for j in range(1, 8):
                z = z + cols_t[j] * jnp.broadcast_to(u[j : j + 1, :], (8, 128))
            z_rows = [jnp.broadcast_to(z[m : m + 1, :], (8, 128)) for m in range(8)]
            for g in range(k + 1, n // 8):
                s = acols[g][0] * z_rows[0]
                for m in range(1, 8):
                    s = s + acols[g][m] * z_rows[m]
                groups[g] = groups[g] - s
    inv = jnp.concatenate(out, axis=0)[:, n:]
    return jnp.where(iota((n, n), 1) <= iota((n, n), 0), inv, 0.0)


def lower_inverse(gram, hook):
    size = gram.shape[0]
    if size == BASE:
        inv = base_inverse(gram)
        hook()
        return inv
    h = size // 2
    i_top = lower_inverse(gram[:h, :h], hook)
    l_side = mm(gram[h:, :h], i_top, NT)
    i_bot = lower_inverse(gram[h:, h:] - mm(l_side, l_side, NT), hook)
    i_side = -mm(i_bot, mm(l_side, i_top))
    top = jnp.concatenate([i_top, jnp.zeros((h, h), F32)], 1)
    return jnp.concatenate([top, jnp.concatenate([i_side, i_bot], 1)], 0)


def upper_base(y):
    n = y.shape[0]
    r, c = iota((n, n), 0), iota((n, n), 1)
    inv = jnp.where(r == c, 1.0 / y, 0.0)
    s = 1
    while s < n:
        off = (r // (2 * s) == c // (2 * s)) & (r // s != c // s) & (r < c)
        inv = inv - mm(inv, mm(jnp.where(off, y, 0.0), inv))
        s *= 2
    return inv


def upper_inverse(y):
    size = y.shape[0]
    if size == BASE:
        return upper_base(y)
    h = size // 2
    i_top = upper_inverse(y[:h, :h])
    i_bot = upper_inverse(y[h:, h:])
    i_side = -mm(i_top, mm(y[:h, h:], i_bot))
    bottom = jnp.concatenate([jnp.zeros((h, h), F32), i_bot], 1)
    return jnp.concatenate([jnp.concatenate([i_top, i_side], 1), bottom], 0)


def meet(peers):
    barrier = pltpu.get_barrier_semaphore()
    for peer in peers:
        pl.semaphore_signal(barrier, inc=1, device_id=peer, device_id_type=pl.DeviceIdType.MESH)
    pl.semaphore_wait(barrier, len(peers))


def remote(src, dst, send, recv, peer):
    return pltpu.make_async_remote_copy(
        src_ref=src, dst_ref=dst, send_sem=send, recv_sem=recv, device_id=peer, device_id_type=pl.DeviceIdType.MESH
    )


def place():
    prow, pcol = lax.axis_index("prow"), lax.axis_index("pcol")
    return prow // 2, prow % 2, pcol // NZ, pcol % NZ


def gather_peers():
    _, _, x, z = place()
    peers = [{"pcol": x * NZ + (z + 1) % NZ}, {"pcol": x * NZ + (z + NZ - 1) % NZ}]
    return peers + [{"pcol": (x + dx) % NX * NZ + z} for dx in range(1, NX)]


def gather(rows, out, send, recv, hooks=()):
    _, core, x, z = place()

    def slab(xx, zz):
        start = (xx % NX * NZ + (zz + 2 * NZ) % NZ) * rows
        return out.at[pl.ds(pl.multiple_of(start, rows), rows)]

    def along_z(dx, dist):
        step = 1 if dist <= NZ // 2 else -1
        piece = slab(x + dx, z + step - dist)
        return remote(piece, piece, send.at[dx, dist], recv.at[dx, dist], {"pcol": x * NZ + (z + step + NZ) % NZ})

    def along_x(dx, dist):
        piece = slab(x, z - dist)
        return remote(piece, piece, send.at[dx, dist], recv.at[dx, dist], {"pcol": (x + NX - dx) % NX * NZ + z})

    def arrived(dx, dist):
        piece = slab(x + dx, z - dist)
        remote(piece, piece, send.at[dx, dist], recv.at[dx, dist], {"pcol": x * NZ + (z + 1) % NZ}).wait_recv()

    def passed_on(dx, dist):
        if dist < NZ // 2:
            along_z(dx, dist + 1).start()
        elif dist > NZ // 2 + 1:
            along_z(dx, dist - 1).start()

    order = (1, 7, 2, 6, 3, 5, 4)

    @pl.when(core == 0)
    def _():
        along_z(0, 1).start()
        along_z(0, NZ - 1).start()
        for dx in range(1, NX):
            along_x(dx, 0).start()

    @pl.when(core == 1)
    def _():
        for dx in range(1, NX):
            along_x(dx, 0).start()
        along_z(0, 1).start()
        along_z(0, NZ - 1).start()
        for dx in range(1, NX):
            arrived(dx, 0)
            along_z(dx, 1).start()
            along_z(dx, NZ - 1).start()

    for i, dist in enumerate(order):

        @pl.when(core == 0)
        def _():
            arrived(0, dist)
            passed_on(0, dist)
            for dx in range(1, NX):
                along_x(dx, dist).start()

        @pl.when(core == 1)
        def _():
            for dx in range(NX):
                arrived(dx, dist)
                passed_on(dx, dist)

        if i < len(hooks):
            hooks[i]()

    @pl.when(core == 0)
    def _():
        for dist in (0,) + order:
            for dx in range(1, NX):
                arrived(dx, dist)

    for dx in range(NX):
        for dist in range(NZ):
            if dx or dist:
                piece = slab(x, z)
                remote(piece, piece, send.at[dx, dist], recv.at[dx, dist], {"pcol": x * NZ + (z + 1) % NZ}).wait_send()


def column_peers():
    y, core, _, _ = place()
    peers = [{"prow": (y + dy) % NY * 2 + core} for dy in range(1, NY)]
    return peers + [{"prow": y * 2 + 1 - core}]


class Broadcast:
    def __init__(self, y0, core0, src, out, send, recv):
        y, core, _, _ = place()
        self.owner = (y == y0) & (core == core0)
        self.relay = (y != y0) & (core == core0)
        self.leaf = core != core0
        self.along = [
            remote(src, out, send.at[dy], recv.at[0], {"prow": (y + dy) % NY * 2 + core}) for dy in range(1, NY)
        ]
        self.own = remote(src, out, send.at[0], recv.at[0], {"prow": y * 2 + 1 - core})
        self.pass_on = remote(out, out, send.at[0], recv.at[0], {"prow": y * 2 + 1 - core})
        self.keep = pltpu.make_async_copy(src, out, send.at[NY])

    def start(self):
        @pl.when(self.owner)
        def _():
            for copy in self.along:
                copy.start()
            self.own.start()
            self.keep.start()

    def forward(self):
        @pl.when(self.relay)
        def _():
            self.pass_on.wait_recv()
            self.pass_on.start()

    def finish(self):
        @pl.when(self.relay)
        def _():
            self.pass_on.wait_send()

        @pl.when(self.leaf)
        def _():
            self.pass_on.wait_recv()

        @pl.when(self.owner)
        def _():
            for copy in self.along:
                copy.wait_send()
            self.own.wait_send()
            self.keep.wait()


def panel_kernel(slab_ref, a_ref, out_ref, top_ref, send, recv, tsend, trecv):
    _, _, x, z = place()
    rows = slab_ref.shape[0]
    out_ref[pl.ds(pl.multiple_of((x * NZ + z) * rows, rows), rows), :] = slab_ref[...]
    meet(gather_peers() + column_peers())
    top = Broadcast(0, 0, a_ref.at[pl.ds(0, top_ref.shape[0])], top_ref, tsend, trecv)
    top.start()
    gather(rows, out_ref, send, recv)
    top.forward()
    top.finish()


class Sum:
    def __init__(self, s, out, half, quarter, acc, send, recv):
        y, core, _, _ = place()
        self.s, self.out, self.half, self.quarter, self.acc, self.send, self.recv = s, out, half, quarter, acc, send, recv
        self.y, self.core = y, core
        self.width = s.shape[1]
        self.q = s.shape[0] // 8
        self.h = 4 * self.q
        self.mate = {"prow": y * 2 + 1 - core}
        self.own = self.rows(core * self.h + y * self.q, self.q)
        self.sent = []

    def rows(self, start, n):
        return pl.ds(pl.multiple_of(start, n), n)

    def copy(self, src, dst, i, peer):
        return remote(src, dst, self.send.at[i], self.recv.at[i], peer)

    def go(self, *args):
        copy = self.copy(*args)
        copy.start()
        self.sent.append(copy)
        return copy

    def along(self, dy):
        return {"prow": (self.y + dy) % NY * 2 + self.core}

    def exchange(self):
        self.first = self.go(self.s.at[self.rows((1 - self.core) * self.h, self.h)], self.half, 0, self.mate)

    def quarters(self):
        self.first.wait_recv()
        self.acc[...] = self.s[self.rows(self.core * self.h, self.h), :] + self.half[...]
        for dy in range(1, NY):
            piece = self.rows((self.y + dy) % NY * self.q, self.q)
            self.go(self.acc.at[piece], self.quarter.at[dy], dy, self.along(dy))

    def total(self):
        total = self.acc[self.rows(self.y * self.q, self.q), :]
        for dy in range(1, NY):
            self.copy(self.quarter.at[dy], self.quarter.at[dy], dy, self.mate).wait_recv()
            total = total + self.quarter[dy]
        self.out[self.own, pl.ds(0, self.width)] = total

    def spread(self):
        piece = self.out.at[self.own]
        for dy in range(1, NY):
            self.go(piece, piece, 3 + dy, self.along(dy))
        self.go(piece, piece, 7, self.mate)

    def forward(self):
        for dy in range(1, NY):
            piece = self.out.at[self.rows(self.core * self.h + (self.y + NY - dy) % NY * self.q, self.q)]
            self.copy(piece, piece, 3 + dy, self.mate).wait_recv()
            self.go(piece, piece, 7 + dy, self.mate)

    def finish(self):
        for dy in range(NY):
            piece = self.out.at[self.rows((1 - self.core) * self.h + (self.y + NY - dy) % NY * self.q, self.q)]
            self.copy(piece, piece, 7 + dy, self.mate).wait_recv()

    def flush(self):
        for copy in self.sent:
            copy.wait_send()


def main_kernel(
    pt_ref,
    ae_ref,
    a_ref,
    out_ref,
    c_ref,
    d_ref,
    b_ref,
    l_ref,
    a_buf,
    gram,
    gtop,
    ghalf,
    gquarter,
    gacc,
    aps,
    apt,
    ahalf,
    aquarter,
    aacc,
    av,
    avt,
    linv_s,
    t_s,
    vct_s,
    pct,
    mpart,
    mx,
    mz,
    mown,
    mraw,
    acopy,
    gsend,
    grecv,
    hsend,
    hrecv,
    asend,
    arecv,
    psend,
    precv,
    fsem,
    send,
    recv,
    xsend,
    xrecv,
    zsend,
    zrecv,
    xgsend,
    xgrecv,
    wsend,
    wrecv,
):
    y, core, x, z = place()
    prow, pcol = y * 2 + core, x * NZ + z
    nb = pt_ref.shape[0]
    cols = ae_ref.shape[1]
    h, q = nb // 2, nb // 8
    rows = cols // 8

    load = pltpu.make_async_copy(a_ref, a_buf, acopy.at[0])
    load.start()

    to_row, to_col = pcol // 4, pcol % 4 * 8 + prow
    from_col, from_row = prow * 4 + pcol // 8, pcol % 8
    stays = (to_row == prow) & (to_col == pcol)
    moves = jnp.logical_not(stays)
    target = {"prow": to_row, "pcol": to_col}
    source = {"prow": from_row, "pcol": from_col}
    barrier = pltpu.get_barrier_semaphore()
    peers = [{"prow": (prow + d) % 8} for d in range(1, 8)]
    peers += [{"pcol": (x + dx) % NX * NZ + z} for dx in range(1, NX)]
    peers += [{"pcol": x * NZ + (z + dz) % NZ} for dz in range(1, NZ)]

    def greet(peer):
        pl.semaphore_signal(barrier, inc=1, device_id=peer, device_id_type=pl.DeviceIdType.MESH)

    for peer in peers:
        greet(peer)

    @pl.when(moves)
    def _():
        greet(target)
        greet(source)

    gram[...] = mm(pt_ref[...], pt_ref[...], NT)

    @pl.when(moves)
    def _():
        pl.semaphore_wait(barrier, len(peers) + 2)

    @pl.when(stays)
    def _():
        pl.semaphore_wait(barrier, len(peers))

    gsum = Sum(gram, gtop, ghalf, gquarter, gacc, gsend, grecv)
    asum = Sum(aps, apt, ahalf, aquarter, aacc, asend, arecv)
    gsum.exchange()
    handed = []
    for r in range(1, 8):
        piece = pl.ds(r % 2 * h + r // 2 * q, q)
        src, dst = pt_ref.at[piece, pl.ds(0, nb)], gtop.at[piece, pl.ds(nb, nb)]
        handed.append(remote(src, dst, hsend.at[r], hrecv.at[0], {"prow": r}))

    @pl.when(prow == 0)
    def _():
        for copy in handed:
            copy.start()
        gtop[pl.ds(0, q), pl.ds(nb, nb)] = pt_ref[pl.ds(0, q), pl.ds(0, nb)]

    load.wait()

    def product(half):
        mine = gsum.rows(half * h, h)
        aps[mine, :] = mm3(split(pt_ref[mine, :]), split(a_buf[...]))

    product(1 - core)
    asum.exchange()
    gsum.quarters()
    product(core)
    gsum.total()

    @pl.when(prow != 0)
    def _():
        piece = gtop.at[gsum.own, pl.ds(nb, nb)]
        remote(piece, piece, hsend.at[0], hrecv.at[0], gsum.mate).wait_recv()

    gsum.spread()
    asum.quarters()
    gsum.forward()
    gsum.finish()

    offset = pl.multiple_of(pcol % 4 * cols, cols)
    part = Broadcast(x, z // 4, pt_ref.at[:, pl.ds(offset, cols)], pct, psend, precv)

    def first():
        asum.total()
        asum.spread()
        part.start()

    stages = iter([first, asum.forward, lambda: None, lambda: None])
    linv = lower_inverse(gtop[:, 0:nb], lambda: next(stages)())
    linv_s[...] = linv
    asum.finish()
    avt[...] = mm(linv, apt[...]) - ae_ref[...]
    av[...] = avt[...].T

    mine = pl.ds(pl.multiple_of(prow * rows, rows), rows)
    swap = remote(
        av.at[mine], out_ref.at[pl.ds(pl.multiple_of(to_col * rows, rows), rows)], fsem.at[0], fsem.at[1], target
    )

    @pl.when(moves)
    def _():
        swap.start()

    @pl.when(stays)
    def _():
        out_ref[pl.ds(pl.multiple_of(pcol * rows, rows), rows), :] = av[mine, :]

    part.forward()
    part.finish()

    @pl.when(moves)
    def _():
        swap.wait_recv()

    def along_x(src, dst, sends, recvs, dx):
        return remote(src, dst, sends.at[dx], recvs.at[dx], {"pcol": (x + dx) % NX * NZ + z})

    def m_first():
        e = (iota((nb, cols), 0) == iota((nb, cols), 1)) & (pcol == 0)
        vct_s[...] = mm(linv_s[...], pct[...]) - e.astype(F32)
        mpart[...] = mm(vct_s[pl.ds(pl.multiple_of(prow * q, q), q), :], av[...])
        for dx in range(1, NX):
            piece = pl.ds(pl.multiple_of((x + dx) % NX * 8, 8), 8)
            along_x(mpart.at[piece], mx.at[dx], xsend, xrecv, dx).start()

    def factor():
        linv = linv_s[...]
        side = mm(linv, gtop[:, nb:])
        r, c = iota((nb, nb), 0), iota((nb, nb), 1)
        ygram = 2.0 * (r == c).astype(F32) - side - mm(gtop[:, nb:], linv, ((0,), (1,)))
        t_s[...] = upper_inverse(jnp.where(r < c, ygram, jnp.where(r == c, 0.5 * ygram, 0.0)))

    def m_second():
        total = mpart[pl.ds(pl.multiple_of(x * 8, 8), 8), :]
        for dx in range(1, NX):
            along_x(mx.at[dx], mx.at[dx], xsend, xrecv, dx).wait_recv()
            total = total + mx[dx]
        mown[...] = total
        for dz in range(1, NZ):
            remote(mown, mz.at[dz], zsend.at[dz], zrecv.at[dz], {"pcol": x * NZ + (z + dz) % NZ}).start()

    m_own = mraw.at[pl.ds(pl.multiple_of(prow * q + x * 8, 8), 8)]
    m_rows = mraw.at[pl.ds(pl.multiple_of(prow * q, q), q)]

    def m_third():
        total = mown[...]
        for dz in range(1, NZ):
            remote(mown, mz.at[dz], zsend.at[dz], zrecv.at[dz], {"pcol": x * NZ + (z + dz) % NZ}).wait_recv()
            total = total + mz[dz]
        mraw[pl.ds(pl.multiple_of(prow * q + x * 8, 8), 8), :] = total
        for dx in range(1, NX):
            along_x(m_own, m_own, xgsend, xgrecv, dx).start()

    def m_fourth():
        for dx in range(1, NX):
            along_x(m_own, m_own, xgsend, xgrecv, dx).wait_recv()
        for d in range(1, 8):
            remote(m_rows, m_rows, wsend.at[d], wrecv.at[d], {"prow": (prow + d) % 8}).start()

    def last():
        for d in range(1, 8):
            remote(m_rows, m_rows, wsend.at[d], wrecv.at[d], {"prow": (prow + d) % 8}).wait_recv()
        t, vct, linv = t_s[...], vct_s[...], linv_s[...]
        k = mm(t, mm(mraw[...], t), TN)
        b = mm(t, avt[...], TN) - mm(0.5 * (k + k.T), vct)
        b_ref[...] = b
        c_ref[...] = mm(linv, b, TN)
        d_ref[...] = mm(t, vct)
        sel = (iota((8, nb), 1) == iota((8, nb), 0) + 8 * pcol).astype(F32)
        kt = mm(sel, k, NT)
        l_ref[0:8, :] = kt
        l_ref[8:16, :] = mm(kt, linv)
        l_ref[16:24, :] = mm(sel, t, NT)

    gather(rows, out_ref, send, recv, (m_first, factor, m_second, m_third, m_fourth, last))

    gsum.flush()
    asum.flush()

    @pl.when(prow == 0)
    def _():
        for copy in handed:
            copy.wait_send()

    @pl.when(moves)
    def _():
        swap.wait_send()

    for dx in range(1, NX):
        along_x(mpart.at[pl.ds(0, 8)], mx.at[dx], xsend, xrecv, dx).wait_send()
        along_x(m_own, m_own, xgsend, xgrecv, dx).wait_send()
    for dz in range(1, NZ):
        remote(mown, mz.at[dz], zsend.at[dz], zrecv.at[dz], {"pcol": x * NZ + (z + dz) % NZ}).wait_send()
    for d in range(1, 8):
        remote(m_rows, m_rows, wsend.at[d], wrecv.at[d], {"prow": (prow + d) % 8}).wait_send()


def params(cid):
    return pltpu.CompilerParams(collective_id=cid, has_side_effects=True, vmem_limit_bytes=LIMIT)


def plain(**kw):
    return pltpu.CompilerParams(vmem_limit_bytes=LIMIT, **kw)


def shape(*dims):
    return jax.ShapeDtypeStruct(dims, F32)


def update_kernel(a_ref, pt_ref, av_ref, c_ref, d_ref, b_ref, l_ref, o_ref, w_ref, ch, cl, dh, dl):
    step = pl.program_id(0)

    @pl.when(step == 0)
    def _():
        ch[...], cl[...] = split(c_ref[...])
        dh[...], dl[...] = split(d_ref[...])

    p, v = pt_ref[...], av_ref[...]
    both = mm3(split(p), (ch[...], cl[...]), TN) + mm3(split(v), (dh[...], dl[...]))
    o_ref[...] = a_ref[...] - both
    w_ref[...] = mm(l_ref[16:24, :], v, NT) - 0.5 * mm(l_ref[8:16, :], p)

    @pl.when((lax.axis_index("prow") == 0) & (step == 0))
    def _():
        o_ref[...] += b_ref[...]
        w_ref[...] += 0.5 * l_ref[0:8, :]


def shards(trailing, panel):
    rows, cols = trailing.shape
    pt_own = panel.T
    nc = pt_own.shape[0]
    nb = nc * lax.axis_size("pcol")
    dma = pltpu.SemaphoreType.DMA
    buf = lambda *dims: pltpu.VMEM(dims, F32)

    pt, ae = pl.pallas_call(
        panel_kernel,
        out_shape=(shape(nb, rows), shape(nb, cols)),
        in_specs=[VMEM, ANY],
        out_specs=(VMEM, VMEM),
        scratch_shapes=[dma((NX, NZ)), dma((NX, NZ)), dma((NY + 1,)), dma((1,))],
        compiler_params=params(1),
    )(pt_own, trailing)

    h, q = nb // 2, nb // 8
    av, c, d, b, l = pl.pallas_call(
        main_kernel,
        out_shape=(shape(rows, nb),) + (shape(nb, cols),) * 3 + (shape(24, nb),),
        in_specs=[VMEM, VMEM, ANY],
        out_specs=(VMEM,) * 5,
        scratch_shapes=[
            buf(rows, cols),
            buf(nb, nb),
            buf(nb, 2 * nb),
            buf(h, nb),
            buf(NY, q, nb),
            buf(h, nb),
            buf(nb, cols),
            buf(nb, cols),
            buf(h, cols),
            buf(NY, q, cols),
            buf(h, cols),
            buf(cols, nb),
            buf(nb, cols),
            buf(nb, nb),
            buf(nb, nb),
            buf(nb, cols),
            buf(nb, cols),
            buf(q, nb),
            buf(NX, 8, nb),
            buf(NZ, 8, nb),
            buf(8, nb),
            buf(nb, nb),
            dma((1,)),
            dma((11,)),
            dma((11,)),
            dma((8,)),
            dma((1,)),
            dma((11,)),
            dma((11,)),
            dma((NY + 1,)),
            dma((1,)),
            dma((2,)),
            dma((NX, NZ)),
            dma((NX, NZ)),
            dma((NX,)),
            dma((NX,)),
            dma((NZ,)),
            dma((NZ,)),
            dma((NX,)),
            dma((NX,)),
            dma((8,)),
            dma((8,)),
        ],
        compiler_params=params(2),
    )(pt, ae, trailing)

    tile = nb
    whole = lambda *dims: pl.BlockSpec(dims, lambda i: (0, 0))
    updated, wt = pl.pallas_call(
        update_kernel,
        grid=(rows // tile,),
        out_shape=(shape(rows, cols), shape(nc, rows)),
        in_specs=[
            pl.BlockSpec((tile, cols), lambda i: (i, 0)),
            pl.BlockSpec((nb, tile), lambda i: (0, i)),
            pl.BlockSpec((tile, nb), lambda i: (i, 0)),
            whole(nb, cols),
            whole(nb, cols),
            whole(nb, cols),
            whole(24, nb),
        ],
        out_specs=(pl.BlockSpec((tile, cols), lambda i: (i, 0)), pl.BlockSpec((nc, tile), lambda i: (0, i))),
        scratch_shapes=[pltpu.VMEM((nb, cols), jnp.bfloat16)] * 4,
        compiler_params=plain(dimension_semantics=("arbitrary",)),
    )(trailing, pt, av, c, d, b, l)
    return updated, wt.T


def solution(mesh):
    in_specs = (P("prow", "pcol"), P("prow", "pcol"))
    out_specs = (P("prow", "pcol"), P("prow", "pcol"))
    return jax.shard_map(shards, mesh=mesh, in_specs=in_specs, out_specs=out_specs, check_vma=False)
```

```python
import jax
import jax.numpy as jnp
from jax import lax
from jax.experimental import pallas as pl
from jax.experimental.pallas import tpu as pltpu
from jax.sharding import PartitionSpec as P

HIGH = lax.Precision.HIGHEST
F32 = jnp.float32
NX, NZ, NY = 4, 8, 4
VMEM = pl.BlockSpec(memory_space=pltpu.VMEM)
ANY = pl.BlockSpec(memory_space=pl.ANY)
LIMIT = 48 << 20
NN, NT, TN = ((1,), (0,)), ((1,), (1,)), ((0,), (0,))


def mm(a, b, dims=NN):
    return lax.dot_general(a, b, (dims, ((), ())), precision=HIGH, preferred_element_type=F32)


def split(x):
    hi = x.astype(jnp.bfloat16)
    return hi, (x - hi.astype(F32)).astype(jnp.bfloat16)


def mm3(a, b, dims=NN):
    (ah, al), (bh, bl) = a, b

    def dot(l, r):
        return lax.dot_general(l, r, (dims, ((), ())), preferred_element_type=F32)

    return dot(ah, bh) + (dot(ah, bl) + dot(al, bh))


def iota(shape, dim):
    return lax.broadcasted_iota(jnp.int32, shape, dim)


BASE = 64


def base_inverse(block):
    n = BASE
    row = iota((8, 128), 0)
    eye = (iota((n, n), 0) == iota((n, n), 1)).astype(F32)
    x = jnp.concatenate([block, eye], axis=1)
    groups = [x[8 * g : 8 * g + 8, :] for g in range(n // 8)]
    zero = jnp.zeros((8, 128), F32)

    def column(vals):
        v = zero
        for i, e in enumerate(vals):
            if e is not None:
                v = jnp.where(row == i, e, v)
        return v

    out = []
    for k in range(n // 8):
        gk = groups[k]
        rows = [jnp.broadcast_to(gk[m : m + 1, :], (8, 128)) for m in range(8)]
        a = [[None] * 8 for _ in range(8)]
        for i in range(8):
            for j in range(i + 1):
                a[i][j] = jnp.broadcast_to(rows[j][:, 8 * k + i : 8 * k + i + 1], (8, 128))
        acols = {
            g: [jnp.broadcast_to(groups[g][:, 8 * k + m : 8 * k + m + 1], (8, 128)) for m in range(8)]
            for g in range(k + 1, n // 8)
        }
        l = [[None] * 8 for _ in range(8)]
        r = [None] * 8
        for j in range(8):
            r[j] = lax.rsqrt(a[j][j])
            for i in range(j + 1, 8):
                l[i][j] = a[i][j] * r[j]
            for i in range(j + 1, 8):
                for c in range(j + 1, i + 1):
                    a[i][c] = a[i][c] - l[i][j] * l[c][j]
        w = [[None] * 8 for _ in range(8)]
        for j in range(8):
            w[j][j] = r[j]
            for i in range(j + 1, 8):
                s = l[i][j] * w[j][j]
                for c in range(j + 1, i):
                    s = s + l[i][c] * w[c][j]
                w[i][j] = -(s * r[i])
        cols = [column([w[i][m] for i in range(8)]) for m in range(8)]
        u = cols[0] * rows[0]
        for m in range(1, 8):
            u = u + cols[m] * rows[m]
        out.append(u)
        if k + 1 < n // 8:
            cols_t = [column([w[j][m] for m in range(8)]) for j in range(8)]
            z = cols_t[0] * jnp.broadcast_to(u[0:1, :], (8, 128))
            for j in range(1, 8):
                z = z + cols_t[j] * jnp.broadcast_to(u[j : j + 1, :], (8, 128))
            z_rows = [jnp.broadcast_to(z[m : m + 1, :], (8, 128)) for m in range(8)]
            for g in range(k + 1, n // 8):
                s = acols[g][0] * z_rows[0]
                for m in range(1, 8):
                    s = s + acols[g][m] * z_rows[m]
                groups[g] = groups[g] - s
    inv = jnp.concatenate(out, axis=0)[:, n:]
    return jnp.where(iota((n, n), 1) <= iota((n, n), 0), inv, 0.0)


def lower_inverse(gram, hook):
    size = gram.shape[0]
    if size == BASE:
        inv = base_inverse(gram)
        hook()
        return inv
    h = size // 2
    i_top = lower_inverse(gram[:h, :h], hook)
    l_side = mm(gram[h:, :h], i_top, NT)
    i_bot = lower_inverse(gram[h:, h:] - mm(l_side, l_side, NT), hook)
    i_side = -mm(i_bot, mm(l_side, i_top))
    top = jnp.concatenate([i_top, jnp.zeros((h, h), F32)], 1)
    return jnp.concatenate([top, jnp.concatenate([i_side, i_bot], 1)], 0)


def upper_base(y):
    n = y.shape[0]
    r, c = iota((n, n), 0), iota((n, n), 1)
    inv = jnp.where(r == c, 1.0 / y, 0.0)
    s = 1
    while s < n:
        off = (r // (2 * s) == c // (2 * s)) & (r // s != c // s) & (r < c)
        inv = inv - mm(inv, mm(jnp.where(off, y, 0.0), inv))
        s *= 2
    return inv


def remote(src, dst, send, recv, peer):
    return pltpu.make_async_remote_copy(
        src_ref=src, dst_ref=dst, send_sem=send, recv_sem=recv, device_id=peer, device_id_type=pl.DeviceIdType.MESH
    )


def place():
    prow, pcol = lax.axis_index("prow"), lax.axis_index("pcol")
    return prow // 2, prow % 2, pcol // NZ, pcol % NZ


ORDER = (1, 7, 2, 6, 3, 5, 4)


def gather(at, send, recv, hooks=()):
    _, core, x, z = place()

    def slab(xx, zz):
        return at(xx % NX, (zz + 2 * NZ) % NZ)

    def along_z(dx, dist):
        step = 1 if dist <= NZ // 2 else -1
        piece = slab(x + dx, z + step - dist)
        return remote(piece, piece, send.at[dx, dist], recv.at[dx, dist], {"pcol": x * NZ + (z + step + NZ) % NZ})

    def along_x(dx, dist):
        piece = slab(x, z - dist)
        return remote(piece, piece, send.at[dx, dist], recv.at[dx, dist], {"pcol": (x + NX - dx) % NX * NZ + z})

    def arrived(dx, dist):
        piece = slab(x + dx, z - dist)
        remote(piece, piece, send.at[dx, dist], recv.at[dx, dist], {"pcol": x * NZ + (z + 1) % NZ}).wait_recv()

    def passed_on(dx, dist):
        if dist < NZ // 2:
            along_z(dx, dist + 1).start()
        elif dist > NZ // 2 + 1:
            along_z(dx, dist - 1).start()

    @pl.when(core == 0)
    def _():
        along_z(0, 1).start()
        along_z(0, NZ - 1).start()
        for dx in range(1, NX):
            along_x(dx, 0).start()

    @pl.when(core == 1)
    def _():
        for dx in range(1, NX):
            along_x(dx, 0).start()
        along_z(0, 1).start()
        along_z(0, NZ - 1).start()
        for dx in range(1, NX):
            arrived(dx, 0)
            along_z(dx, 1).start()
            along_z(dx, NZ - 1).start()

    for i, dist in enumerate(ORDER):

        @pl.when(core == 0)
        def _():
            arrived(0, dist)
            passed_on(0, dist)
            for dx in range(1, NX):
                along_x(dx, dist).start()
            for dx in range(1, NX):
                arrived(dx, ORDER[i - 1] if i else 0)

        @pl.when(core == 1)
        def _():
            for dx in range(NX):
                arrived(dx, dist)
                passed_on(dx, dist)

        if i < len(hooks):
            hooks[i]()

    @pl.when(core == 0)
    def _():
        for dx in range(1, NX):
            arrived(dx, ORDER[-1])

    def flush():
        for dx in range(NX):
            for dist in range(NZ):
                if dx or dist:
                    piece = slab(x, z)
                    remote(piece, piece, send.at[dx, dist], recv.at[dx, dist], {"pcol": x * NZ + (z + 1) % NZ}).wait_send()

    return flush


class Broadcast:
    def __init__(self, y0, core0, src, out, send, recv):
        y, core, _, _ = place()
        self.owner = (y == y0) & (core == core0)
        self.relay = (y != y0) & (core == core0)
        self.leaf = core != core0
        self.along = [
            remote(src, out, send.at[dy], recv.at[0], {"prow": (y + dy) % NY * 2 + core}) for dy in range(1, NY)
        ]
        self.own = remote(src, out, send.at[0], recv.at[0], {"prow": y * 2 + 1 - core})
        self.pass_on = remote(out, out, send.at[0], recv.at[0], {"prow": y * 2 + 1 - core})
        self.keep = pltpu.make_async_copy(src, out, send.at[NY])

    def start(self):
        @pl.when(self.owner)
        def _():
            for copy in self.along:
                copy.start()
            self.own.start()
            self.keep.start()

    def forward(self):
        @pl.when(self.relay)
        def _():
            self.pass_on.wait_recv()
            self.pass_on.start()

    def finish(self):
        @pl.when(self.relay)
        def _():
            self.pass_on.wait_send()

        @pl.when(self.leaf)
        def _():
            self.pass_on.wait_recv()

        @pl.when(self.owner)
        def _():
            for copy in self.along:
                copy.wait_send()
            self.own.wait_send()
            self.keep.wait()


class Parts:
    def __init__(self, y0, core0, src, window, out, send, recv):
        y, core, _, z = place()
        self.owner = (y == y0) & (core == core0)
        self.relay = (y != y0) & (core == core0)
        self.leaf = core != core0
        self.src, self.window, self.out, self.send, self.recv, self.y, self.core, self.z = src, window, out, send, recv, y, core, z

    def rows(self, dist):
        return pl.ds(pl.multiple_of((self.z + NZ - dist) % NZ * 8, 8), 8)

    def copy(self, dist, dy, passed=False):
        rows = self.rows(dist)
        dst = self.out.at[:, rows]
        src = dst if passed else self.src.at[:, rows, self.window]
        peer = (self.y + dy) % NY * 2 + self.core if dy else self.y * 2 + 1 - self.core
        return remote(src, dst, self.send.at[dist, dy], self.recv.at[dist], {"prow": peer})

    def start(self, dist):
        @pl.when(self.owner)
        def _():
            for dy in (1, 3, 2, 0):
                self.copy(dist, dy).start()

    def forward(self, dist):
        @pl.when(self.relay)
        def _():
            self.copy(dist, 0, True).wait_recv()
            self.copy(dist, 0, True).start()

    def finish(self):
        @pl.when(self.owner)
        def _():
            self.out[...] = self.src[:, :, self.window]

        @pl.when(self.leaf)
        def _():
            for dist in range(NZ):
                self.copy(dist, 0, True).wait_recv()

    def flush(self):
        @pl.when(self.owner)
        def _():
            for dist in range(NZ):
                for dy in range(NY):
                    self.copy(dist, dy).wait_send()

        @pl.when(self.relay)
        def _():
            for dist in range(NZ):
                self.copy(dist, 0, True).wait_send()


class Sum:
    def __init__(self, s, out, half, quarter, acc, send, recv):
        y, core, _, _ = place()
        self.s, self.out, self.half, self.quarter, self.acc, self.send, self.recv = s, out, half, quarter, acc, send, recv
        self.y, self.core = y, core
        self.width = s.shape[1]
        self.q = s.shape[0] // 8
        self.h = 4 * self.q
        self.mate = {"prow": y * 2 + 1 - core}
        self.own = self.rows(core * self.h + y * self.q, self.q)
        self.sent = []

    def rows(self, start, n):
        return pl.ds(pl.multiple_of(start, n), n)

    def copy(self, src, dst, i, peer):
        return remote(src, dst, self.send.at[i], self.recv.at[i], peer)

    def go(self, *args):
        copy = self.copy(*args)
        copy.start()
        self.sent.append(copy)
        return copy

    def along(self, dy):
        return {"prow": (self.y + dy) % NY * 2 + self.core}

    def exchange(self):
        self.first = self.go(self.s.at[self.rows((1 - self.core) * self.h, self.h)], self.half, 0, self.mate)

    def quarters(self):
        self.first.wait_recv()
        self.acc[...] = self.s[self.rows(self.core * self.h, self.h), :] + self.half[...]
        for dy in range(1, NY):
            piece = self.rows((self.y + dy) % NY * self.q, self.q)
            self.go(self.acc.at[piece], self.quarter.at[dy], dy, self.along(dy))

    def total(self):
        total = self.acc[self.rows(self.y * self.q, self.q), :]
        for dy in range(1, NY):
            self.copy(self.quarter.at[dy], self.quarter.at[dy], dy, self.mate).wait_recv()
            total = total + self.quarter[dy]
        self.out[self.own, pl.ds(0, self.width)] = total

    def spread(self):
        piece = self.out.at[self.own]
        for dy in range(1, NY):
            self.go(piece, piece, 3 + dy, self.along(dy))
        self.go(piece, piece, 7, self.mate)

    def forward(self):
        for dy in range(1, NY):
            piece = self.out.at[self.rows(self.core * self.h + (self.y + NY - dy) % NY * self.q, self.q)]
            self.copy(piece, piece, 3 + dy, self.mate).wait_recv()
            self.go(piece, piece, 7 + dy, self.mate)

    def finish(self):
        for dy in range(NY):
            piece = self.out.at[self.rows((1 - self.core) * self.h + (self.y + NY - dy) % NY * self.q, self.q)]
            self.copy(piece, piece, 7 + dy, self.mate).wait_recv()

    def flush(self):
        for copy in self.sent:
            copy.wait_send()


def main_kernel(
    slab_ref,
    a_ref,
    pt_ref,
    out_ref,
    c_ref,
    d_ref,
    b_ref,
    l_ref,
    a_buf,
    a_hi,
    a_lo,
    ae,
    gram,
    gtop,
    ghalf,
    gquarter,
    gacc,
    aps,
    apt,
    ahalf,
    aquarter,
    aacc,
    av,
    avt,
    linv_s,
    t_s,
    vct_s,
    pct,
    mpart,
    mx,
    mz,
    mown,
    mraw,
    acopy,
    panel_send,
    panel_recv,
    esend,
    erecv,
    gsend,
    grecv,
    hsend,
    hrecv,
    asend,
    arecv,
    psend,
    precv,
    fsem,
    send,
    recv,
    xsend,
    xrecv,
    zsend,
    zrecv,
    xgsend,
    xgrecv,
    wsend,
    wrecv,
):
    y, core, x, z = place()
    prow, pcol = y * 2 + core, x * NZ + z
    nb = out_ref.shape[1]
    cols = ae.shape[1]
    h, q = nb // 2, nb // 8
    rows = cols // 8
    wide = slab_ref.shape[1]

    load = pltpu.make_async_copy(a_ref, a_buf, acopy.at[0])
    load.start()

    to_row, to_col = pcol // 4, pcol % 4 * 8 + prow
    from_col, from_row = prow * 4 + pcol // 8, pcol % 8
    stays = (to_row == prow) & (to_col == pcol)
    moves = jnp.logical_not(stays)
    target = {"prow": to_row, "pcol": to_col}
    source = {"prow": from_row, "pcol": from_col}
    barrier = pltpu.get_barrier_semaphore()
    peers = [{"prow": (prow + d) % 8} for d in range(1, 8)]
    peers += [{"pcol": (x + dx) % NX * NZ + z} for dx in range(1, NX)]
    peers += [{"pcol": x * NZ + (z + dz) % NZ} for dz in range(1, NZ)]

    def greet(peer):
        pl.semaphore_signal(barrier, inc=1, device_id=peer, device_id_type=pl.DeviceIdType.MESH)

    for peer in peers:
        greet(peer)

    @pl.when(moves)
    def _():
        greet(target)
        greet(source)

    pt_ref[x, pl.ds(pl.multiple_of(z * 8, 8), 8), :] = slab_ref[...]

    @pl.when(moves)
    def _():
        pl.semaphore_wait(barrier, len(peers) + 2)

    @pl.when(stays)
    def _():
        pl.semaphore_wait(barrier, len(peers))

    top = Broadcast(0, 0, a_ref.at[pl.ds(0, nb)], ae, esend, erecv)
    top.start()
    window = pl.ds(pl.multiple_of(pcol % 4 * cols, cols), cols)
    part = Parts(x, z // 4, pt_ref, window, pct, psend, precv)

    def split_a():
        load.wait()
        a_hi[...], a_lo[...] = split(a_buf[...])

    def step(i):
        def run():
            part.start(((0,) + ORDER)[i])
            if i:
                part.forward(((0,) + ORDER)[i - 1])
            if i == 1:
                split_a()
            if i == 4:
                top.forward()

        return run

    panel_flush = gather(
        lambda xx, zz: pt_ref.at[xx, pl.ds(pl.multiple_of(zz * 8, 8), 8)],
        panel_send,
        panel_recv,
        [step(i) for i in range(7)],
    )
    part.start(ORDER[6])
    part.forward(ORDER[5])
    panel = pt_ref[...].reshape(nb, wide)
    gram[...] = mm(panel, panel, NT)

    gsum = Sum(gram, gtop, ghalf, gquarter, gacc, gsend, grecv)
    asum = Sum(aps, apt, ahalf, aquarter, aacc, asend, arecv)
    gsum.exchange()
    handed = []
    for r in range(1, 8):
        piece = pl.ds(r % 2 * h + r // 2 * q, q)
        src = pt_ref.at[(r % 2 * h + r // 2 * q) // 64, pl.ds((r % 2 * h + r // 2 * q) % 64, q), pl.ds(0, nb)]
        dst = gtop.at[piece, pl.ds(nb, nb)]
        handed.append(remote(src, dst, hsend.at[r], hrecv.at[0], {"prow": r}))

    @pl.when(prow == 0)
    def _():
        for copy in handed:
            copy.start()
        gtop[pl.ds(0, q), pl.ds(nb, nb)] = pt_ref[0, pl.ds(0, q), pl.ds(0, nb)]

    def product(half):
        mine = pt_ref[pl.ds(half * 2, 2)].reshape(h, wide)
        aps[gsum.rows(half * h, h), :] = mm3(split(mine), (a_hi[...], a_lo[...]))

    product(1 - core)
    asum.exchange()
    gsum.quarters()
    product(core)
    gsum.total()

    @pl.when(prow != 0)
    def _():
        piece = gtop.at[gsum.own, pl.ds(nb, nb)]
        remote(piece, piece, hsend.at[0], hrecv.at[0], gsum.mate).wait_recv()

    gsum.spread()
    asum.quarters()
    gsum.forward()
    gsum.finish()

    def first():
        asum.total()
        asum.spread()

    def second():
        asum.forward()
        part.forward(ORDER[6])

    def third():
        asum.finish()
        part.finish()

    stages = iter([first, second, third, top.finish])
    linv = lower_inverse(gtop[:, 0:nb], lambda: next(stages)())
    linv_s[...] = linv
    avt[...] = mm(linv, apt[...]) - ae[...]
    av[...] = avt[...].T

    mine = pl.ds(pl.multiple_of(prow * rows, rows), rows)
    swap = remote(
        av.at[mine], out_ref.at[pl.ds(pl.multiple_of(to_col * rows, rows), rows)], fsem.at[0], fsem.at[1], target
    )

    @pl.when(moves)
    def _():
        swap.start()

    @pl.when(stays)
    def _():
        out_ref[pl.ds(pl.multiple_of(pcol * rows, rows), rows), :] = av[mine, :]

    @pl.when(moves)
    def _():
        swap.wait_recv()

    def along_x(src, dst, sends, recvs, dx):
        return remote(src, dst, sends.at[dx], recvs.at[dx], {"pcol": (x + dx) % NX * NZ + z})

    def m_first():
        e = (iota((nb, cols), 0) == iota((nb, cols), 1)) & (pcol == 0)
        vct_s[...] = mm(linv_s[...], pct[...].reshape(nb, cols)) - e.astype(F32)
        mpart[...] = mm(vct_s[pl.ds(pl.multiple_of(prow * q, q), q), :], av[...])
        for dx in range(1, NX):
            piece = pl.ds(pl.multiple_of((x + dx) % NX * 8, 8), 8)
            along_x(mpart.at[piece], mx.at[dx], xsend, xrecv, dx).start()

    def factor_first():
        linv = linv_s[...]
        side = mm(linv, gtop[:, nb:])
        r, c = iota((nb, nb), 0), iota((nb, nb), 1)
        ygram = 2.0 * (r == c).astype(F32) - side - mm(gtop[:, nb:], linv, ((0,), (1,)))
        t_s[...] = jnp.where(r < c, ygram, jnp.where(r == c, 0.5 * ygram, 0.0))

    def factor_second():
        blocks = [slice(k * BASE, (k + 1) * BASE) for k in range(nb // BASE)]
        inverses = [upper_base(t_s[k, k]) for k in blocks]
        for k, inverse in zip(blocks, inverses):
            t_s[k, k] = inverse

    def merge(size):
        sides = []
        for k in range(0, nb, 2 * size):
            lo, hi = slice(k, k + size), slice(k + size, k + 2 * size)
            sides.append((lo, hi, -mm(t_s[lo, lo], mm(t_s[lo, hi], t_s[hi, hi]))))
        for lo, hi, side in sides:
            t_s[lo, hi] = side

    def m_second():
        total = mpart[pl.ds(pl.multiple_of(x * 8, 8), 8), :]
        for dx in range(1, NX):
            along_x(mx.at[dx], mx.at[dx], xsend, xrecv, dx).wait_recv()
            total = total + mx[dx]
        mown[...] = total
        for dz in range(1, NZ):
            remote(mown, mz.at[dz], zsend.at[dz], zrecv.at[dz], {"pcol": x * NZ + (z + dz) % NZ}).start()

    m_own = mraw.at[pl.ds(pl.multiple_of(prow * q + x * 8, 8), 8)]
    m_rows = mraw.at[pl.ds(pl.multiple_of(prow * q, q), q)]

    def m_third():
        total = mown[...]
        for dz in range(1, NZ):
            remote(mown, mz.at[dz], zsend.at[dz], zrecv.at[dz], {"pcol": x * NZ + (z + dz) % NZ}).wait_recv()
            total = total + mz[dz]
        mraw[pl.ds(pl.multiple_of(prow * q + x * 8, 8), 8), :] = total
        for dx in range(1, NX):
            along_x(m_own, m_own, xgsend, xgrecv, dx).start()

    def m_fourth():
        for dx in range(1, NX):
            along_x(m_own, m_own, xgsend, xgrecv, dx).wait_recv()
        for d in range(1, 8):
            remote(m_rows, m_rows, wsend.at[d], wrecv.at[d], {"prow": (prow + d) % 8}).start()

    def last():
        for d in range(1, 8):
            remote(m_rows, m_rows, wsend.at[d], wrecv.at[d], {"prow": (prow + d) % 8}).wait_recv()
        t, vct, linv = t_s[...], vct_s[...], linv_s[...]
        k = mm(t, mm(mraw[...], t), TN)
        b = mm(t, avt[...], TN) - mm(0.5 * (k + k.T), vct)
        b_ref[...] = b
        c_ref[...] = mm(linv, b, TN)
        d_ref[...] = mm(t, vct)
        sel = (iota((8, nb), 1) == iota((8, nb), 0) + 8 * pcol).astype(F32)
        kt = mm(sel, k, NT)
        l_ref[0:8, :] = kt
        l_ref[8:16, :] = mm(kt, linv)
        l_ref[16:24, :] = mm(sel, t, NT)

    def fourth():
        merge(BASE)
        m_second()

    def fifth():
        merge(2 * BASE)
        m_third()

    flush = gather(
        lambda xx, zz: out_ref.at[pl.ds(pl.multiple_of((xx * NZ + zz) * rows, rows), rows)],
        send,
        recv,
        (m_first, factor_first, factor_second, fourth, fifth, m_fourth, last),
    )
    flush()
    panel_flush()
    part.flush()

    gsum.flush()
    asum.flush()

    @pl.when(prow == 0)
    def _():
        for copy in handed:
            copy.wait_send()

    @pl.when(moves)
    def _():
        swap.wait_send()

    for dx in range(1, NX):
        along_x(mpart.at[pl.ds(0, 8)], mx.at[dx], xsend, xrecv, dx).wait_send()
        along_x(m_own, m_own, xgsend, xgrecv, dx).wait_send()
    for dz in range(1, NZ):
        remote(mown, mz.at[dz], zsend.at[dz], zrecv.at[dz], {"pcol": x * NZ + (z + dz) % NZ}).wait_send()
    for d in range(1, 8):
        remote(m_rows, m_rows, wsend.at[d], wrecv.at[d], {"prow": (prow + d) % 8}).wait_send()


def params(cid):
    return pltpu.CompilerParams(collective_id=cid, has_side_effects=True, vmem_limit_bytes=LIMIT)


def plain(**kw):
    return pltpu.CompilerParams(vmem_limit_bytes=LIMIT, **kw)


def shape(*dims):
    return jax.ShapeDtypeStruct(dims, F32)


def update_kernel(a_ref, pt_ref, av_ref, c_ref, d_ref, b_ref, l_ref, o_ref, w_ref, ch, cl, dh, dl):
    step = pl.program_id(0)

    @pl.when(step == 0)
    def _():
        ch[...], cl[...] = split(c_ref[...])
        dh[...], dl[...] = split(d_ref[...])

    p, v = pt_ref[...], av_ref[...]
    ps, vs = split(p), split(v)
    both = mm3(ps, (ch[...], cl[...]), TN) + mm3(vs, (dh[...], dl[...]))
    o_ref[...] = a_ref[...] - both
    w_ref[...] = mm3(split(l_ref[16:24, :]), vs, NT) - 0.5 * mm3(split(l_ref[8:16, :]), ps)

    @pl.when((lax.axis_index("prow") == 0) & (step == 0))
    def _():
        nb = b_ref.shape[0]
        o_ref[0:nb, :] += b_ref[...]
        w_ref[:, 0:nb] += 0.5 * l_ref[0:8, :]


def shards(trailing, panel):
    rows, cols = trailing.shape
    pt_own = panel.T
    nc = pt_own.shape[0]
    nb = nc * lax.axis_size("pcol")
    dma = pltpu.SemaphoreType.DMA
    buf = lambda *dims: pltpu.VMEM(dims, F32)

    h, q = nb // 2, nb // 8
    pt, av, c, d, b, l = pl.pallas_call(
        main_kernel,
        out_shape=(shape(NX, nb // NX, rows), shape(rows, nb)) + (shape(nb, cols),) * 3 + (shape(24, nb),),
        in_specs=[VMEM, ANY],
        out_specs=(VMEM,) * 6,
        scratch_shapes=[
            buf(rows, cols),
            pltpu.VMEM((rows, cols), jnp.bfloat16),
            pltpu.VMEM((rows, cols), jnp.bfloat16),
            buf(nb, cols),
            buf(nb, nb),
            buf(nb, 2 * nb),
            buf(h, nb),
            buf(NY, q, nb),
            buf(h, nb),
            buf(nb, cols),
            buf(nb, cols),
            buf(h, cols),
            buf(NY, q, cols),
            buf(h, cols),
            buf(cols, nb),
            buf(nb, cols),
            buf(nb, nb),
            buf(nb, nb),
            buf(nb, cols),
            buf(NX, nb // NX, cols),
            buf(q, nb),
            buf(NX, 8, nb),
            buf(NZ, 8, nb),
            buf(8, nb),
            buf(nb, nb),
            dma((1,)),
            dma((NX, NZ)),
            dma((NX, NZ)),
            dma((NY + 1,)),
            dma((1,)),
            dma((11,)),
            dma((11,)),
            dma((8,)),
            dma((1,)),
            dma((11,)),
            dma((11,)),
            dma((NZ, NY)),
            dma((NZ,)),
            dma((2,)),
            dma((NX, NZ)),
            dma((NX, NZ)),
            dma((NX,)),
            dma((NX,)),
            dma((NZ,)),
            dma((NZ,)),
            dma((NX,)),
            dma((NX,)),
            dma((8,)),
            dma((8,)),
        ],
        compiler_params=params(2),
    )(pt_own, trailing)

    tile = 2 * nb
    whole = lambda *dims: pl.BlockSpec(dims, lambda i: (0, 0))
    updated, wt = pl.pallas_call(
        update_kernel,
        grid=(rows // tile,),
        out_shape=(shape(rows, cols), shape(nc, rows)),
        in_specs=[
            pl.BlockSpec((tile, cols), lambda i: (i, 0)),
            pl.BlockSpec((nb, tile), lambda i: (0, i)),
            pl.BlockSpec((tile, nb), lambda i: (i, 0)),
            whole(nb, cols),
            whole(nb, cols),
            whole(nb, cols),
            whole(24, nb),
        ],
        out_specs=(pl.BlockSpec((tile, cols), lambda i: (i, 0)), pl.BlockSpec((nc, tile), lambda i: (0, i))),
        scratch_shapes=[pltpu.VMEM((nb, cols), jnp.bfloat16)] * 4,
        compiler_params=plain(dimension_semantics=("arbitrary",)),
    )(trailing, pt.reshape(nb, rows), av, c, d, b, l)
    return updated, wt.T


def solution(mesh):
    in_specs = (P("prow", "pcol"), P("prow", "pcol"))
    out_specs = (P("prow", "pcol"), P("prow", "pcol"))
    return jax.shard_map(shards, mesh=mesh, in_specs=in_specs, out_specs=out_specs, check_vma=False)
```

```python
import jax
import jax.numpy as jnp
from jax import lax
from jax.experimental import pallas as pl
from jax.experimental.pallas import tpu as pltpu
from jax.sharding import PartitionSpec as P

HIGH = lax.Precision.HIGHEST
F32 = jnp.float32
NX, NZ, NY = 4, 8, 4
VMEM = pl.BlockSpec(memory_space=pltpu.VMEM)
ANY = pl.BlockSpec(memory_space=pl.ANY)
LIMIT = 48 << 20
NN, NT, TN = ((1,), (0,)), ((1,), (1,)), ((0,), (0,))


def mm(a, b, dims=NN):
    return lax.dot_general(a, b, (dims, ((), ())), precision=HIGH, preferred_element_type=F32)


def split(x):
    hi = x.astype(jnp.bfloat16)
    return hi, (x - hi.astype(F32)).astype(jnp.bfloat16)


def mm3(a, b, dims=NN):
    (ah, al), (bh, bl) = a, b

    def dot(l, r):
        return lax.dot_general(l, r, (dims, ((), ())), preferred_element_type=F32)

    return dot(ah, bh) + (dot(ah, bl) + dot(al, bh))


def iota(shape, dim):
    return lax.broadcasted_iota(jnp.int32, shape, dim)


BASE = 64


def base_inverse(block):
    n = BASE
    row = iota((8, 128), 0)
    eye = (iota((n, n), 0) == iota((n, n), 1)).astype(F32)
    x = jnp.concatenate([block, eye], axis=1)
    groups = [x[8 * g : 8 * g + 8, :] for g in range(n // 8)]
    zero = jnp.zeros((8, 128), F32)

    def column(vals):
        v = zero
        for i, e in enumerate(vals):
            if e is not None:
                v = jnp.where(row == i, e, v)
        return v

    out = []
    for k in range(n // 8):
        gk = groups[k]
        rows = [jnp.broadcast_to(gk[m : m + 1, :], (8, 128)) for m in range(8)]
        a = [[None] * 8 for _ in range(8)]
        for i in range(8):
            for j in range(i + 1):
                a[i][j] = jnp.broadcast_to(rows[j][:, 8 * k + i : 8 * k + i + 1], (8, 128))
        acols = {
            g: [jnp.broadcast_to(groups[g][:, 8 * k + m : 8 * k + m + 1], (8, 128)) for m in range(8)]
            for g in range(k + 1, n // 8)
        }
        l = [[None] * 8 for _ in range(8)]
        r = [None] * 8
        for j in range(8):
            r[j] = lax.rsqrt(a[j][j])
            for i in range(j + 1, 8):
                l[i][j] = a[i][j] * r[j]
            for i in range(j + 1, 8):
                for c in range(j + 1, i + 1):
                    a[i][c] = a[i][c] - l[i][j] * l[c][j]
        w = [[None] * 8 for _ in range(8)]
        for j in range(8):
            w[j][j] = r[j]
            for i in range(j + 1, 8):
                s = l[i][j] * w[j][j]
                for c in range(j + 1, i):
                    s = s + l[i][c] * w[c][j]
                w[i][j] = -(s * r[i])
        cols = [column([w[i][m] for i in range(8)]) for m in range(8)]
        u = cols[0] * rows[0]
        for m in range(1, 8):
            u = u + cols[m] * rows[m]
        out.append(u)
        if k + 1 < n // 8:
            cols_t = [column([w[j][m] for m in range(8)]) for j in range(8)]
            z = cols_t[0] * jnp.broadcast_to(u[0:1, :], (8, 128))
            for j in range(1, 8):
                z = z + cols_t[j] * jnp.broadcast_to(u[j : j + 1, :], (8, 128))
            z_rows = [jnp.broadcast_to(z[m : m + 1, :], (8, 128)) for m in range(8)]
            for g in range(k + 1, n // 8):
                s = acols[g][0] * z_rows[0]
                for m in range(1, 8):
                    s = s + acols[g][m] * z_rows[m]
                groups[g] = groups[g] - s
    inv = jnp.concatenate(out, axis=0)[:, n:]
    return jnp.where(iota((n, n), 1) <= iota((n, n), 0), inv, 0.0)


def lower_inverse(gram, hook):
    size = gram.shape[0]
    if size == BASE:
        inv = base_inverse(gram)
        hook()
        return inv
    h = size // 2
    i_top = lower_inverse(gram[:h, :h], hook)
    l_side = mm(gram[h:, :h], i_top, NT)
    i_bot = lower_inverse(gram[h:, h:] - mm(l_side, l_side, NT), hook)
    i_side = -mm(i_bot, mm(l_side, i_top))
    top = jnp.concatenate([i_top, jnp.zeros((h, h), F32)], 1)
    return jnp.concatenate([top, jnp.concatenate([i_side, i_bot], 1)], 0)


def upper_base(y):
    n = y.shape[0]
    r, c = iota((n, n), 0), iota((n, n), 1)
    inv = jnp.where(r == c, 1.0 / y, 0.0)
    s = 1
    while s < n:
        off = (r // (2 * s) == c // (2 * s)) & (r // s != c // s) & (r < c)
        inv = inv - mm(inv, mm(jnp.where(off, y, 0.0), inv))
        s *= 2
    return inv


def remote(src, dst, send, recv, peer):
    return pltpu.make_async_remote_copy(
        src_ref=src, dst_ref=dst, send_sem=send, recv_sem=recv, device_id=peer, device_id_type=pl.DeviceIdType.MESH
    )


def place():
    prow, pcol = lax.axis_index("prow"), lax.axis_index("pcol")
    return prow // 2, prow % 2, pcol // NZ, pcol % NZ


ORDER = (1, 7, 2, 6, 3, 5, 4)


def gather(at, send, recv, hooks=()):
    _, core, x, z = place()

    def slab(xx, zz):
        return at(xx % NX, (zz + 2 * NZ) % NZ)

    def along_z(dx, dist):
        step = 1 if dist <= NZ // 2 else -1
        piece = slab(x + dx, z + step - dist)
        return remote(piece, piece, send.at[dx, dist], recv.at[dx, dist], {"pcol": x * NZ + (z + step + NZ) % NZ})

    def along_x(dx, dist):
        piece = slab(x, z - dist)
        return remote(piece, piece, send.at[dx, dist], recv.at[dx, dist], {"pcol": (x + NX - dx) % NX * NZ + z})

    def arrived(dx, dist):
        piece = slab(x + dx, z - dist)
        remote(piece, piece, send.at[dx, dist], recv.at[dx, dist], {"pcol": x * NZ + (z + 1) % NZ}).wait_recv()

    def passed_on(dx, dist):
        if dist < NZ // 2:
            along_z(dx, dist + 1).start()
        elif dist > NZ // 2 + 1:
            along_z(dx, dist - 1).start()

    @pl.when(core == 0)
    def _():
        along_z(0, 1).start()
        along_z(0, NZ - 1).start()
        for dx in range(1, NX):
            along_x(dx, 0).start()

    @pl.when(core == 1)
    def _():
        for dx in range(1, NX):
            along_x(dx, 0).start()
        along_z(0, 1).start()
        along_z(0, NZ - 1).start()
        for dx in range(1, NX):
            arrived(dx, 0)
            along_z(dx, 1).start()
            along_z(dx, NZ - 1).start()

    for i, dist in enumerate(ORDER):

        @pl.when(core == 0)
        def _():
            arrived(0, dist)
            passed_on(0, dist)
            for dx in range(1, NX):
                along_x(dx, dist).start()
            for dx in range(1, NX):
                arrived(dx, ORDER[i - 1] if i else 0)

        @pl.when(core == 1)
        def _():
            for dx in range(NX):
                arrived(dx, dist)
                passed_on(dx, dist)

        if i < len(hooks):
            hooks[i]()

    @pl.when(core == 0)
    def _():
        for dx in range(1, NX):
            arrived(dx, ORDER[-1])

    def flush():
        for dx in range(NX):
            for dist in range(NZ):
                if dx or dist:
                    piece = slab(x, z)
                    remote(piece, piece, send.at[dx, dist], recv.at[dx, dist], {"pcol": x * NZ + (z + 1) % NZ}).wait_send()

    return flush


class Broadcast:
    def __init__(self, y0, core0, src, out, send, recv):
        y, core, _, _ = place()
        self.owner = (y == y0) & (core == core0)
        self.relay = (y != y0) & (core == core0)
        self.leaf = core != core0
        self.along = [
            remote(src, out, send.at[dy], recv.at[0], {"prow": (y + dy) % NY * 2 + core}) for dy in range(1, NY)
        ]
        self.own = remote(src, out, send.at[0], recv.at[0], {"prow": y * 2 + 1 - core})
        self.pass_on = remote(out, out, send.at[0], recv.at[0], {"prow": y * 2 + 1 - core})
        self.keep = pltpu.make_async_copy(src, out, send.at[NY])

    def start(self):
        @pl.when(self.owner)
        def _():
            for copy in self.along:
                copy.start()
            self.own.start()
            self.keep.start()

    def forward(self):
        @pl.when(self.relay)
        def _():
            self.pass_on.wait_recv()
            self.pass_on.start()

    def finish(self):
        @pl.when(self.relay)
        def _():
            self.pass_on.wait_send()

        @pl.when(self.leaf)
        def _():
            self.pass_on.wait_recv()

        @pl.when(self.owner)
        def _():
            for copy in self.along:
                copy.wait_send()
            self.own.wait_send()
            self.keep.wait()


class DirectSum:
    def __init__(self, s, out, parts, send, recv):
        y, core, _, _ = place()
        self.s, self.out, self.parts, self.send, self.recv = s, out, parts, send, recv
        self.prow = y * 2 + core
        self.q = s.shape[0] // 8

    def rows(self, d):
        return pl.ds(pl.multiple_of((self.prow + d) % 8 * self.q, self.q), self.q)

    def scatter(self, d):
        peer = {"prow": (self.prow + d) % 8}
        return remote(self.s.at[self.rows(d)], self.parts.at[d], self.send.at[0, d], self.recv.at[0, d], peer)

    def spread(self, d):
        mine = self.out.at[self.rows(0)]
        return remote(mine, mine, self.send.at[1, d], self.recv.at[1, d], {"prow": (self.prow + d) % 8})

    def start(self):
        for d in range(1, 8):
            self.scatter(d).start()

    def total(self):
        total = self.s[self.rows(0), :]
        for d in range(1, 8):
            self.scatter(d).wait_recv()
            total = total + self.parts[d]
        self.out[self.rows(0), :] = total
        for d in range(1, 8):
            self.spread(d).start()

    def finish(self):
        for d in range(1, 8):
            self.spread(d).wait_recv()

    def flush(self):
        for d in range(1, 8):
            self.scatter(d).wait_send()
            self.spread(d).wait_send()


class Sum:
    def __init__(self, s, out, half, quarter, acc, send, recv):
        y, core, _, _ = place()
        self.s, self.out, self.half, self.quarter, self.acc, self.send, self.recv = s, out, half, quarter, acc, send, recv
        self.y, self.core = y, core
        self.width = s.shape[1]
        self.q = s.shape[0] // 8
        self.h = 4 * self.q
        self.mate = {"prow": y * 2 + 1 - core}
        self.own = self.rows(core * self.h + y * self.q, self.q)
        self.sent = []

    def rows(self, start, n):
        return pl.ds(pl.multiple_of(start, n), n)

    def copy(self, src, dst, i, peer):
        return remote(src, dst, self.send.at[i], self.recv.at[i], peer)

    def go(self, *args):
        copy = self.copy(*args)
        copy.start()
        self.sent.append(copy)
        return copy

    def along(self, dy):
        return {"prow": (self.y + dy) % NY * 2 + self.core}

    def exchange(self):
        self.first = self.go(self.s.at[self.rows((1 - self.core) * self.h, self.h)], self.half, 0, self.mate)

    def quarters(self):
        self.first.wait_recv()
        self.acc[...] = self.s[self.rows(self.core * self.h, self.h), :] + self.half[...]
        for dy in range(1, NY):
            piece = self.rows((self.y + dy) % NY * self.q, self.q)
            self.go(self.acc.at[piece], self.quarter.at[dy], dy, self.along(dy))

    def total(self):
        total = self.acc[self.rows(self.y * self.q, self.q), :]
        for dy in range(1, NY):
            self.copy(self.quarter.at[dy], self.quarter.at[dy], dy, self.mate).wait_recv()
            total = total + self.quarter[dy]
        self.out[self.own, pl.ds(0, self.width)] = total

    def spread(self):
        piece = self.out.at[self.own]
        for dy in range(1, NY):
            self.go(piece, piece, 3 + dy, self.along(dy))
        self.go(piece, piece, 7, self.mate)

    def forward(self):
        for dy in range(1, NY):
            piece = self.out.at[self.rows(self.core * self.h + (self.y + NY - dy) % NY * self.q, self.q)]
            self.copy(piece, piece, 3 + dy, self.mate).wait_recv()
            self.go(piece, piece, 7 + dy, self.mate)

    def finish(self):
        for dy in range(NY):
            piece = self.out.at[self.rows((1 - self.core) * self.h + (self.y + NY - dy) % NY * self.q, self.q)]
            self.copy(piece, piece, 7 + dy, self.mate).wait_recv()

    def flush(self):
        for copy in self.sent:
            copy.wait_send()


def main_kernel(
    slab_ref,
    a_ref,
    pt_ref,
    out_ref,
    c_ref,
    d_ref,
    b_ref,
    l_ref,
    a_buf,
    a_hi,
    a_lo,
    ae,
    gram,
    gfull,
    gparts,
    aps,
    apt,
    ahalf,
    aquarter,
    aacc,
    av,
    avt,
    xct,
    linv_s,
    t_s,
    vct_s,
    pct,
    mpart,
    mx,
    mz,
    mown,
    mraw,
    acopy,
    panel_send,
    panel_recv,
    esend,
    erecv,
    gsend,
    grecv,
    hsend,
    hrecv,
    asend,
    arecv,
    psend,
    precv,
    fsem,
    send,
    recv,
    xsend,
    xrecv,
    zsend,
    zrecv,
    xgsend,
    xgrecv,
    wsend,
    wrecv,
):
    y, core, x, z = place()
    prow, pcol = y * 2 + core, x * NZ + z
    nb = out_ref.shape[1]
    cols = ae.shape[1]
    h, q = nb // 2, nb // 8
    rows = cols // 8
    wide = slab_ref.shape[1]

    load = pltpu.make_async_copy(a_ref, a_buf, acopy.at[0])
    load.start()

    to_row, to_col = pcol // 4, pcol % 4 * 8 + prow
    from_col, from_row = prow * 4 + pcol // 8, pcol % 8
    stays = (to_row == prow) & (to_col == pcol)
    moves = jnp.logical_not(stays)
    target = {"prow": to_row, "pcol": to_col}
    source = {"prow": from_row, "pcol": from_col}
    barrier = pltpu.get_barrier_semaphore()
    peers = [{"prow": (prow + d) % 8} for d in range(1, 8)]
    peers += [{"pcol": (x + dx) % NX * NZ + z} for dx in range(1, NX)]
    peers += [{"pcol": x * NZ + (z + dz) % NZ} for dz in range(1, NZ)]

    def greet(peer):
        pl.semaphore_signal(barrier, inc=1, device_id=peer, device_id_type=pl.DeviceIdType.MESH)

    for peer in peers:
        greet(peer)

    @pl.when(moves)
    def _():
        greet(target)
        greet(source)

    pt_ref[x, pl.ds(pl.multiple_of(z * 8, 8), 8), :] = slab_ref[...]

    @pl.when(moves)
    def _():
        pl.semaphore_wait(barrier, len(peers) + 2)

    @pl.when(stays)
    def _():
        pl.semaphore_wait(barrier, len(peers))

    top = Broadcast(0, 0, a_ref.at[pl.ds(0, nb)], ae, esend, erecv)
    top.start()
    window = pl.ds(pl.multiple_of(pcol % 4 * cols, cols), cols)
    part = Broadcast(x, z // 4, pt_ref.at[:, :, window], pct, psend, precv)

    def split_a():
        load.wait()
        a_hi[...], a_lo[...] = split(a_buf[...])

    panel_flush = gather(
        lambda xx, zz: pt_ref.at[xx, pl.ds(pl.multiple_of(zz * 8, 8), 8)],
        panel_send,
        panel_recv,
        (lambda: None, split_a),
    )
    top.forward()
    panel = pt_ref[...].reshape(nb, wide)
    gram[...] = mm(panel, panel, NT)

    gsum = DirectSum(gram, gfull, gparts, gsend, grecv)
    asum = Sum(aps, apt, ahalf, aquarter, aacc, asend, arecv)
    gsum.start()
    handed = []
    for r in range(1, 8):
        start = r % 2 * h + r // 2 * q
        src = pt_ref.at[start // 64, pl.ds(start % 64, q), pl.ds(0, nb)]
        handed.append(remote(src, apt.at[pl.ds(start, q), pl.ds(cols, nb)], hsend.at[r], hrecv.at[0], {"prow": r}))

    aps[...] = mm3(split(panel), (a_hi[...], a_lo[...]))
    asum.exchange()
    gsum.total()

    @pl.when(prow == 0)
    def _():
        for copy in handed:
            copy.start()
        apt[pl.ds(0, q), pl.ds(cols, nb)] = pt_ref[0, pl.ds(0, q), pl.ds(0, nb)]

    asum.quarters()
    part.start()
    gsum.finish()

    def first():
        asum.total()

        @pl.when(prow != 0)
        def _():
            piece = apt.at[asum.own, pl.ds(cols, nb)]
            remote(piece, piece, hsend.at[0], hrecv.at[0], asum.mate).wait_recv()

        asum.spread()

    stages = iter([first, asum.forward, lambda: None, part.forward])
    linv = lower_inverse(gfull[...], lambda: next(stages)())
    linv_s[...] = linv
    asum.finish()
    top.finish()
    avt[...] = mm(linv, apt[:, 0:cols]) - ae[...]
    av[...] = avt[...].T

    mine = pl.ds(pl.multiple_of(prow * rows, rows), rows)
    swap = remote(
        av.at[mine], out_ref.at[pl.ds(pl.multiple_of(to_col * rows, rows), rows)], fsem.at[0], fsem.at[1], target
    )

    @pl.when(moves)
    def _():
        swap.start()

    @pl.when(stays)
    def _():
        out_ref[pl.ds(pl.multiple_of(pcol * rows, rows), rows), :] = av[mine, :]

    def along_x(src, dst, sends, recvs, dx):
        return remote(src, dst, sends.at[dx], recvs.at[dx], {"pcol": (x + dx) % NX * NZ + z})

    def m_first():
        e = (iota((nb, cols), 0) == iota((nb, cols), 1)) & (pcol == 0)
        vct_s[...] = mm(linv_s[...], pct[...].reshape(nb, cols)) - e.astype(F32)
        mpart[...] = mm(vct_s[pl.ds(pl.multiple_of(prow * q, q), q), :], av[...])
        for dx in range(1, NX):
            piece = pl.ds(pl.multiple_of((x + dx) % NX * 8, 8), 8)
            along_x(mpart.at[piece], mx.at[dx], xsend, xrecv, dx).start()

    def factor_first():
        linv = linv_s[...]
        side = mm(linv, apt[:, cols:])
        r, c = iota((nb, nb), 0), iota((nb, nb), 1)
        ygram = 2.0 * (r == c).astype(F32) - side - mm(apt[:, cols:], linv, ((0,), (1,)))
        t_s[...] = jnp.where(r < c, ygram, jnp.where(r == c, 0.5 * ygram, 0.0))

    def factor_second():
        blocks = [slice(k * BASE, (k + 1) * BASE) for k in range(nb // BASE)]
        inverses = [upper_base(t_s[k, k]) for k in blocks]
        for k, inverse in zip(blocks, inverses):
            t_s[k, k] = inverse

    def merge(size):
        sides = []
        for k in range(0, nb, 2 * size):
            lo, hi = slice(k, k + size), slice(k + size, k + 2 * size)
            sides.append((lo, hi, -mm(t_s[lo, lo], mm(t_s[lo, hi], t_s[hi, hi]))))
        for lo, hi, side in sides:
            t_s[lo, hi] = side

    def m_second():
        total = mpart[pl.ds(pl.multiple_of(x * 8, 8), 8), :]
        for dx in range(1, NX):
            along_x(mx.at[dx], mx.at[dx], xsend, xrecv, dx).wait_recv()
            total = total + mx[dx]
        mown[...] = total
        for dz in range(1, NZ):
            remote(mown, mz.at[dz], zsend.at[dz], zrecv.at[dz], {"pcol": x * NZ + (z + dz) % NZ}).start()

    m_own = mraw.at[pl.ds(pl.multiple_of(prow * q + x * 8, 8), 8)]
    m_rows = mraw.at[pl.ds(pl.multiple_of(prow * q, q), q)]

    def m_third():
        total = mown[...]
        for dz in range(1, NZ):
            remote(mown, mz.at[dz], zsend.at[dz], zrecv.at[dz], {"pcol": x * NZ + (z + dz) % NZ}).wait_recv()
            total = total + mz[dz]
        mraw[pl.ds(pl.multiple_of(prow * q + x * 8, 8), 8), :] = total
        for dx in range(1, NX):
            along_x(m_own, m_own, xgsend, xgrecv, dx).start()

    def m_fourth():
        for dx in range(1, NX):
            along_x(m_own, m_own, xgsend, xgrecv, dx).wait_recv()
        for d in range(1, 8):
            remote(m_rows, m_rows, wsend.at[d], wrecv.at[d], {"prow": (prow + d) % 8}).start()

    def last():
        for d in range(1, 8):
            remote(m_rows, m_rows, wsend.at[d], wrecv.at[d], {"prow": (prow + d) % 8}).wait_recv()
        t, vct, linv = t_s[...], vct_s[...], linv_s[...]
        k = mm(t, mm(mraw[...], t), TN)
        b = xct[...] - mm(0.5 * (k + k.T), vct)
        b_ref[...] = b
        c_ref[...] = mm(linv, b, TN)
        sel = (iota((8, nb), 1) == iota((8, nb), 0) + 8 * pcol).astype(F32)
        kt = mm(sel, k, NT)
        l_ref[0:8, :] = kt
        l_ref[8:16, :] = mm(kt, linv)
        l_ref[16:24, :] = mm(sel, t, NT)

    def ready():
        t = t_s[...]
        xct[...] = mm(t, avt[...], TN)
        d_ref[...] = mm(t, vct_s[...])

    factor_first()
    factor_second()
    merge(BASE)
    merge(2 * BASE)
    part.finish()
    m_first()

    @pl.when(moves)
    def _():
        swap.wait_recv()

    flush = gather(
        lambda xx, zz: out_ref.at[pl.ds(pl.multiple_of((xx * NZ + zz) * rows, rows), rows)],
        send,
        recv,
        (ready, m_second, lambda: None, m_third, lambda: None, m_fourth),
    )
    last()
    flush()
    panel_flush()

    gsum.flush()
    asum.flush()

    @pl.when(prow == 0)
    def _():
        for copy in handed:
            copy.wait_send()

    @pl.when(moves)
    def _():
        swap.wait_send()

    for dx in range(1, NX):
        along_x(mpart.at[pl.ds(0, 8)], mx.at[dx], xsend, xrecv, dx).wait_send()
        along_x(m_own, m_own, xgsend, xgrecv, dx).wait_send()
    for dz in range(1, NZ):
        remote(mown, mz.at[dz], zsend.at[dz], zrecv.at[dz], {"pcol": x * NZ + (z + dz) % NZ}).wait_send()
    for d in range(1, 8):
        remote(m_rows, m_rows, wsend.at[d], wrecv.at[d], {"prow": (prow + d) % 8}).wait_send()


def params(cid):
    return pltpu.CompilerParams(collective_id=cid, has_side_effects=True, vmem_limit_bytes=LIMIT)


def plain(**kw):
    return pltpu.CompilerParams(vmem_limit_bytes=LIMIT, **kw)


def shape(*dims):
    return jax.ShapeDtypeStruct(dims, F32)


def update_kernel(a_ref, pt_ref, av_ref, c_ref, d_ref, b_ref, l_ref, o_ref, w_ref, ch, cl, dh, dl):
    step = pl.program_id(0)

    @pl.when(step == 0)
    def _():
        ch[...], cl[...] = split(c_ref[...])
        dh[...], dl[...] = split(d_ref[...])

    p, v = pt_ref[...], av_ref[...]
    ps, vs = split(p), split(v)
    both = mm3(ps, (ch[...], cl[...]), TN) + mm3(vs, (dh[...], dl[...]))
    o_ref[...] = a_ref[...] - both
    w_ref[...] = mm3(split(l_ref[16:24, :]), vs, NT) - 0.5 * mm3(split(l_ref[8:16, :]), ps)

    @pl.when((lax.axis_index("prow") == 0) & (step == 0))
    def _():
        nb = b_ref.shape[0]
        o_ref[0:nb, :] += b_ref[...]
        w_ref[:, 0:nb] += 0.5 * l_ref[0:8, :]


def shards(trailing, panel):
    rows, cols = trailing.shape
    pt_own = panel.T
    nc = pt_own.shape[0]
    nb = nc * lax.axis_size("pcol")
    dma = pltpu.SemaphoreType.DMA
    buf = lambda *dims: pltpu.VMEM(dims, F32)

    h, q = nb // 2, nb // 8
    pt, av, c, d, b, l = pl.pallas_call(
        main_kernel,
        out_shape=(shape(NX, nb // NX, rows), shape(rows, nb)) + (shape(nb, cols),) * 3 + (shape(24, nb),),
        in_specs=[VMEM, ANY],
        out_specs=(VMEM,) * 6,
        scratch_shapes=[
            buf(rows, cols),
            pltpu.VMEM((rows, cols), jnp.bfloat16),
            pltpu.VMEM((rows, cols), jnp.bfloat16),
            buf(nb, cols),
            buf(nb, nb),
            buf(nb, nb),
            buf(8, q, nb),
            buf(nb, cols),
            buf(nb, cols + nb),
            buf(h, cols),
            buf(NY, q, cols),
            buf(h, cols),
            buf(cols, nb),
            buf(nb, cols),
            buf(nb, cols),
            buf(nb, nb),
            buf(nb, nb),
            buf(nb, cols),
            buf(NX, nb // NX, cols),
            buf(q, nb),
            buf(NX, 8, nb),
            buf(NZ, 8, nb),
            buf(8, nb),
            buf(nb, nb),
            dma((1,)),
            dma((NX, NZ)),
            dma((NX, NZ)),
            dma((NY + 1,)),
            dma((1,)),
            dma((2, 8)),
            dma((2, 8)),
            dma((8,)),
            dma((1,)),
            dma((11,)),
            dma((11,)),
            dma((NY + 1,)),
            dma((1,)),
            dma((2,)),
            dma((NX, NZ)),
            dma((NX, NZ)),
            dma((NX,)),
            dma((NX,)),
            dma((NZ,)),
            dma((NZ,)),
            dma((NX,)),
            dma((NX,)),
            dma((8,)),
            dma((8,)),
        ],
        compiler_params=params(2),
    )(pt_own, trailing)

    tile = 2 * nb
    whole = lambda *dims: pl.BlockSpec(dims, lambda i: (0, 0))
    updated, wt = pl.pallas_call(
        update_kernel,
        grid=(rows // tile,),
        out_shape=(shape(rows, cols), shape(nc, rows)),
        in_specs=[
            pl.BlockSpec((tile, cols), lambda i: (i, 0)),
            pl.BlockSpec((nb, tile), lambda i: (0, i)),
            pl.BlockSpec((tile, nb), lambda i: (i, 0)),
            whole(nb, cols),
            whole(nb, cols),
            whole(nb, cols),
            whole(24, nb),
        ],
        out_specs=(pl.BlockSpec((tile, cols), lambda i: (i, 0)), pl.BlockSpec((nc, tile), lambda i: (0, i))),
        scratch_shapes=[pltpu.VMEM((nb, cols), jnp.bfloat16)] * 4,
        compiler_params=plain(dimension_semantics=("arbitrary",)),
    )(trailing, pt.reshape(nb, rows), av, c, d, b, l)
    return updated, wt.T


def solution(mesh):
    in_specs = (P("prow", "pcol"), P("prow", "pcol"))
    out_specs = (P("prow", "pcol"), P("prow", "pcol"))
    return jax.shard_map(shards, mesh=mesh, in_specs=in_specs, out_specs=out_specs, check_vma=False)
```

```python
import jax
import jax.numpy as jnp
from jax import lax
from jax.experimental import pallas as pl
from jax.experimental.pallas import tpu as pltpu
from jax.sharding import PartitionSpec as P

HIGH = lax.Precision.HIGHEST
F32 = jnp.float32
NX, NZ, NY = 4, 8, 4
VMEM = pl.BlockSpec(memory_space=pltpu.VMEM)
ANY = pl.BlockSpec(memory_space=pl.ANY)
LIMIT = 48 << 20
NN, NT, TN = ((1,), (0,)), ((1,), (1,)), ((0,), (0,))


def mm(a, b, dims=NN):
    return lax.dot_general(a, b, (dims, ((), ())), precision=HIGH, preferred_element_type=F32)


def split(x):
    hi = x.astype(jnp.bfloat16)
    return hi, (x - hi.astype(F32)).astype(jnp.bfloat16)


def mm3(a, b, dims=NN):
    (ah, al), (bh, bl) = a, b

    def dot(l, r):
        return lax.dot_general(l, r, (dims, ((), ())), preferred_element_type=F32)

    return dot(ah, bh) + (dot(ah, bl) + dot(al, bh))


def iota(shape, dim):
    return lax.broadcasted_iota(jnp.int32, shape, dim)


BASE = 64


def base_inverse(block):
    n = BASE
    row = iota((8, 128), 0)
    eye = (iota((n, n), 0) == iota((n, n), 1)).astype(F32)
    x = jnp.concatenate([block, eye], axis=1)
    groups = [x[8 * g : 8 * g + 8, :] for g in range(n // 8)]
    zero = jnp.zeros((8, 128), F32)

    def column(vals):
        v = zero
        for i, e in enumerate(vals):
            if e is not None:
                v = jnp.where(row == i, e, v)
        return v

    out = []
    for k in range(n // 8):
        gk = groups[k]
        rows = [jnp.broadcast_to(gk[m : m + 1, :], (8, 128)) for m in range(8)]
        a = [[None] * 8 for _ in range(8)]
        for i in range(8):
            for j in range(i + 1):
                a[i][j] = jnp.broadcast_to(rows[j][:, 8 * k + i : 8 * k + i + 1], (8, 128))
        acols = {
            g: [jnp.broadcast_to(groups[g][:, 8 * k + m : 8 * k + m + 1], (8, 128)) for m in range(8)]
            for g in range(k + 1, n // 8)
        }
        l = [[None] * 8 for _ in range(8)]
        r = [None] * 8
        for j in range(8):
            r[j] = lax.rsqrt(a[j][j])
            for i in range(j + 1, 8):
                l[i][j] = a[i][j] * r[j]
            for i in range(j + 1, 8):
                for c in range(j + 1, i + 1):
                    a[i][c] = a[i][c] - l[i][j] * l[c][j]
        w = [[None] * 8 for _ in range(8)]
        for j in range(8):
            w[j][j] = r[j]
            for i in range(j + 1, 8):
                s = l[i][j] * w[j][j]
                for c in range(j + 1, i):
                    s = s + l[i][c] * w[c][j]
                w[i][j] = -(s * r[i])
        cols = [column([w[i][m] for i in range(8)]) for m in range(8)]
        u = cols[0] * rows[0]
        for m in range(1, 8):
            u = u + cols[m] * rows[m]
        out.append(u)
        if k + 1 < n // 8:
            cols_t = [column([w[j][m] for m in range(8)]) for j in range(8)]
            z = cols_t[0] * jnp.broadcast_to(u[0:1, :], (8, 128))
            for j in range(1, 8):
                z = z + cols_t[j] * jnp.broadcast_to(u[j : j + 1, :], (8, 128))
            z_rows = [jnp.broadcast_to(z[m : m + 1, :], (8, 128)) for m in range(8)]
            for g in range(k + 1, n // 8):
                s = acols[g][0] * z_rows[0]
                for m in range(1, 8):
                    s = s + acols[g][m] * z_rows[m]
                groups[g] = groups[g] - s
    inv = jnp.concatenate(out, axis=0)[:, n:]
    return jnp.where(iota((n, n), 1) <= iota((n, n), 0), inv, 0.0)


def lower_inverse(gram, hook):
    size = gram.shape[0]
    if size == BASE:
        inv = base_inverse(gram)
        hook()
        return inv
    h = size // 2
    i_top = lower_inverse(gram[:h, :h], hook)
    l_side = mm(gram[h:, :h], i_top, NT)
    i_bot = lower_inverse(gram[h:, h:] - mm(l_side, l_side, NT), hook)
    i_side = -mm(i_bot, mm(l_side, i_top))
    top = jnp.concatenate([i_top, jnp.zeros((h, h), F32)], 1)
    return jnp.concatenate([top, jnp.concatenate([i_side, i_bot], 1)], 0)


def upper_base(y):
    n = y.shape[0]
    r, c = iota((n, n), 0), iota((n, n), 1)
    inv = jnp.where(r == c, 1.0 / y, 0.0)
    s = 1
    while s < n:
        off = (r // (2 * s) == c // (2 * s)) & (r // s != c // s) & (r < c)
        inv = inv - mm(inv, mm(jnp.where(off, y, 0.0), inv))
        s *= 2
    return inv


def remote(src, dst, send, recv, peer):
    return pltpu.make_async_remote_copy(
        src_ref=src, dst_ref=dst, send_sem=send, recv_sem=recv, device_id=peer, device_id_type=pl.DeviceIdType.MESH
    )


def place():
    prow, pcol = lax.axis_index("prow"), lax.axis_index("pcol")
    return prow // 2, prow % 2, pcol // NZ, pcol % NZ


ORDER = (1, 7, 2, 6, 3, 5, 4)


def gather(at, send, recv, before=None, hooks=()):
    _, core, x, z = place()

    def slab(xx, zz):
        return at(xx % NX, (zz + 2 * NZ) % NZ)

    def along_z(dx, dist):
        step = 1 if dist <= NZ // 2 else -1
        piece = slab(x + dx, z + step - dist)
        return remote(piece, piece, send.at[dx, dist], recv.at[dx, dist], {"pcol": x * NZ + (z + step + NZ) % NZ})

    def along_x(dx, dist):
        piece = slab(x, z - dist)
        return remote(piece, piece, send.at[dx, dist], recv.at[dx, dist], {"pcol": (x + NX - dx) % NX * NZ + z})

    def arrived(dx, dist):
        piece = slab(x + dx, z - dist)
        remote(piece, piece, send.at[dx, dist], recv.at[dx, dist], {"pcol": x * NZ + (z + 1) % NZ}).wait_recv()

    def passed_on(dx, dist):
        if dist < NZ // 2:
            along_z(dx, dist + 1).start()
        elif dist > NZ // 2 + 1:
            along_z(dx, dist - 1).start()

    @pl.when(core == 0)
    def _():
        along_z(0, 1).start()
        along_z(0, NZ - 1).start()
        for dx in range(1, NX):
            along_x(dx, 0).start()

    @pl.when(core == 1)
    def _():
        for dx in range(1, NX):
            along_x(dx, 0).start()
        along_z(0, 1).start()
        along_z(0, NZ - 1).start()

    if before:
        before()

    @pl.when(core == 1)
    def _():
        for dx in range(1, NX):
            arrived(dx, 0)
            along_z(dx, 1).start()
            along_z(dx, NZ - 1).start()

    for i, dist in enumerate(ORDER):

        @pl.when(core == 0)
        def _():
            arrived(0, dist)
            passed_on(0, dist)
            for dx in range(1, NX):
                along_x(dx, dist).start()
            for dx in range(1, NX):
                arrived(dx, ORDER[i - 1] if i else 0)

        @pl.when(core == 1)
        def _():
            for dx in range(NX):
                arrived(dx, dist)
                passed_on(dx, dist)

        if i < len(hooks):
            hooks[i]()

    @pl.when(core == 0)
    def _():
        for dx in range(1, NX):
            arrived(dx, ORDER[-1])

    def flush():
        for dx in range(NX):
            for dist in range(NZ):
                if dx or dist:
                    piece = slab(x, z)
                    remote(piece, piece, send.at[dx, dist], recv.at[dx, dist], {"pcol": x * NZ + (z + 1) % NZ}).wait_send()

    return flush


class Broadcast:
    def __init__(self, y0, core0, src, out, send, recv):
        y, core, _, _ = place()
        away = (y + NY - y0) % NY
        self.owner = (away == 0) & (core == core0)
        self.next = (away == 1) & (core == core0)
        self.last = (away == 3) & (core == core0)
        self.far_one = (away == 2) & (core == core0)
        self.relay = (away != 0) & (core == core0)
        self.leaf = core != core0
        mate = {"prow": y * 2 + 1 - core}
        up, down = {"prow": (y + 1) % NY * 2 + core}, {"prow": (y + 3) % NY * 2 + core}
        self.up = remote(src, out, send.at[1], recv.at[0], up)
        self.down = remote(src, out, send.at[2], recv.at[0], down)
        self.own = remote(src, out, send.at[0], recv.at[0], mate)
        self.on = remote(out, out, send.at[1], recv.at[0], up)
        self.pass_on = remote(out, out, send.at[0], recv.at[0], mate)
        self.keep = pltpu.make_async_copy(src, out, send.at[3])

    def start(self):
        @pl.when(self.owner)
        def _():
            self.up.start()
            self.down.start()
            self.own.start()
            self.keep.start()

    def near(self):
        @pl.when(self.next)
        def _():
            self.on.wait_recv()
            self.on.start()
            self.pass_on.start()

        @pl.when(self.last)
        def _():
            self.pass_on.wait_recv()
            self.pass_on.start()

    def far(self):
        @pl.when(self.far_one)
        def _():
            self.pass_on.wait_recv()
            self.pass_on.start()

    def finish(self):
        @pl.when(self.relay)
        def _():
            self.pass_on.wait_send()

        @pl.when(self.next)
        def _():
            self.on.wait_send()

        @pl.when(self.leaf)
        def _():
            self.pass_on.wait_recv()

        @pl.when(self.owner)
        def _():
            self.up.wait_send()
            self.down.wait_send()
            self.own.wait_send()
            self.keep.wait()


class DirectSum:
    def __init__(self, s, out, parts, send, recv):
        y, core, _, _ = place()
        self.s, self.out, self.parts, self.send, self.recv = s, out, parts, send, recv
        self.prow = y * 2 + core
        self.q = s.shape[0] // 8

    def rows(self, d):
        return pl.ds(pl.multiple_of((self.prow + d) % 8 * self.q, self.q), self.q)

    def scatter(self, d):
        peer = {"prow": (self.prow + d) % 8}
        return remote(self.s.at[self.rows(d)], self.parts.at[d], self.send.at[0, d], self.recv.at[0, d], peer)

    def spread(self, d):
        mine = self.out.at[self.rows(0)]
        return remote(mine, mine, self.send.at[1, d], self.recv.at[1, d], {"prow": (self.prow + d) % 8})

    def start(self):
        for d in range(1, 8):
            self.scatter(d).start()

    def total(self):
        total = self.s[self.rows(0), :]
        for d in range(1, 8):
            self.scatter(d).wait_recv()
            total = total + self.parts[d]
        return total

    def share(self):
        for d in range(1, 8):
            self.spread(d).start()

    def finish(self):
        for d in range(1, 8):
            self.spread(d).wait_recv()

    def flush(self):
        for d in range(1, 8):
            self.scatter(d).wait_send()
            self.spread(d).wait_send()


class Sum:
    def __init__(self, s, out, half, quarter, acc, send, recv):
        y, core, _, _ = place()
        self.s, self.out, self.half, self.quarter, self.acc, self.send, self.recv = s, out, half, quarter, acc, send, recv
        self.y, self.core = y, core
        self.width = s.shape[1]
        self.q = s.shape[0] // 8
        self.h = 4 * self.q
        self.mate = {"prow": y * 2 + 1 - core}
        self.own = self.rows(core * self.h + y * self.q, self.q)
        self.sent = []

    def rows(self, start, n):
        return pl.ds(pl.multiple_of(start, n), n)

    def copy(self, src, dst, i, peer):
        return remote(src, dst, self.send.at[i], self.recv.at[i], peer)

    def go(self, *args):
        copy = self.copy(*args)
        copy.start()
        self.sent.append(copy)
        return copy

    def along(self, dy):
        return {"prow": (self.y + dy) % NY * 2 + self.core}

    def exchange(self):
        self.first = self.go(self.s.at[self.rows((1 - self.core) * self.h, self.h)], self.half, 0, self.mate)

    def quarters(self):
        self.first.wait_recv()
        self.acc[...] = self.s[self.rows(self.core * self.h, self.h), :] + self.half[...]
        for dy in range(1, NY):
            piece = self.rows((self.y + dy) % NY * self.q, self.q)
            self.go(self.acc.at[piece], self.quarter.at[dy], dy, self.along(dy))

    def total(self):
        total = self.acc[self.rows(self.y * self.q, self.q), :]
        for dy in range(1, NY):
            self.copy(self.quarter.at[dy], self.quarter.at[dy], dy, self.mate).wait_recv()
            total = total + self.quarter[dy]
        self.out[self.own, pl.ds(0, self.width)] = total

    def spread(self):
        piece = self.out.at[self.own]
        for dy in range(1, NY):
            self.go(piece, piece, 3 + dy, self.along(dy))
        self.go(piece, piece, 7, self.mate)

    def forward(self):
        for dy in range(1, NY):
            piece = self.out.at[self.rows(self.core * self.h + (self.y + NY - dy) % NY * self.q, self.q)]
            self.copy(piece, piece, 3 + dy, self.mate).wait_recv()
            self.go(piece, piece, 7 + dy, self.mate)

    def finish(self):
        for dy in range(NY):
            piece = self.out.at[self.rows((1 - self.core) * self.h + (self.y + NY - dy) % NY * self.q, self.q)]
            self.copy(piece, piece, 7 + dy, self.mate).wait_recv()

    def flush(self):
        for copy in self.sent:
            copy.wait_send()


def main_kernel(
    slab_ref,
    a_ref,
    pt_ref,
    out_ref,
    c_ref,
    d_ref,
    b_ref,
    l_ref,
    a_buf,
    a_hi,
    a_lo,
    ae,
    aet,
    ae64,
    ap64,
    gram,
    gfull,
    gparts,
    aps,
    apt,
    ahalf,
    aquarter,
    aacc,
    ptop,
    pct,
    linv_s,
    t_s,
    mpart,
    mparts,
    mq,
    mx,
    mz,
    mown,
    mraw,
    acopy,
    panel_send,
    panel_recv,
    esend,
    erecv,
    gsend,
    grecv,
    hsend,
    hrecv,
    asend,
    arecv,
    psend,
    precv,
    fsend,
    frecv,
    ksend,
    krecv,
    send,
    recv,
    xsend,
    xrecv,
    zsend,
    zrecv,
    xgsend,
    xgrecv,
    wsend,
    wrecv,
):
    y, core, x, z = place()
    prow, pcol = y * 2 + core, x * NZ + z
    nb = out_ref.shape[1]
    cols = ae.shape[1]
    rows = cols // 8
    q = nb // 8
    wide = slab_ref.shape[1]

    load = pltpu.make_async_copy(a_ref, a_buf, acopy.at[0])
    load.start()

    to_row, to_col = pcol // 4, pcol % 4 * 8 + core * NY + y
    source_col, j = prow * 4 + pcol // 8, pcol % 8
    stays = (to_row == prow) & (to_col == pcol)
    moves = jnp.logical_not(stays)
    corner = (prow == 0) & (pcol == 0)
    source = {"prow": j % NY * 2 + j // NY, "pcol": source_col}
    barrier = pltpu.get_barrier_semaphore()
    peers = [{"prow": (prow + d) % 8} for d in range(1, 8)]
    peers += [{"pcol": (x + dx) % NX * NZ + z} for dx in range(1, NX)]
    peers += [{"pcol": x * NZ + (z + dz) % NZ} for dz in range(1, NZ)]

    def greet(peer):
        pl.semaphore_signal(barrier, inc=1, device_id=peer, device_id_type=pl.DeviceIdType.MESH)

    for peer in peers:
        greet(peer)

    @pl.when(moves)
    def _():
        greet(source)

    @pl.when(jnp.logical_not(corner))
    def _():
        greet({"prow": 0, "pcol": source_col})

    pt_ref[x, pl.ds(pl.multiple_of(z * 8, 8), 8), :] = slab_ref[...]
    extra = jnp.where(moves, 1, 0) + jnp.where(prow == 0, 8, 0) - jnp.where(corner, 1, 0)
    pl.semaphore_wait(barrier, len(peers) + extra)

    top = Broadcast(0, 0, a_ref.at[pl.ds(0, nb)], ae, esend, erecv)
    window = pl.ds(pl.multiple_of(pcol % 4 * cols, cols), cols)
    part = Broadcast(x, z // 4, pt_ref.at[:, :, window], pct, psend, precv)
    head = Broadcast(0, 0, pt_ref.at[:, :, pl.ds(0, nb)], ptop, hsend, hrecv)

    def top_piece(k):
        peer = {"prow": pcol // 4, "pcol": pcol % 4 * 8 + k}
        return remote(aet.at[pl.ds(k * rows, rows)], ae64, ksend.at[k], krecv.at[0], peer)

    def take_a():
        load.wait()
        a_hi[...], a_lo[...] = split(a_buf[...])

        @pl.when(prow == 0)
        def _():
            aet[...] = a_buf[0:nb, :].T
            for k in range(1, 8):
                top_piece(k).start()

        @pl.when((prow == 0) & (pcol != 0))
        def _():
            top_piece(0).start()

        @pl.when(corner)
        def _():
            ae64[...] = aet[0:rows, :]

    panel_flush = gather(
        lambda xx, zz: pt_ref.at[xx, pl.ds(pl.multiple_of(zz * 8, 8), 8)],
        panel_send,
        panel_recv,
        top.start,
        (lambda: None, take_a),
    )
    panel = pt_ref[...].reshape(nb, wide)
    gram[...] = mm(panel, panel, NT)

    gsum = DirectSum(gram, gfull, gparts, gsend, grecv)
    asum = Sum(aps, apt, ahalf, aquarter, aacc, asend, arecv)
    msum = DirectSum(mpart, mraw, mparts, wsend, wrecv)
    gsum.start()
    aps[...] = mm3(split(panel), (a_hi[...], a_lo[...])).T
    asum.exchange()
    gfull[gsum.rows(0), :] = gsum.total()
    gsum.share()
    asum.quarters()
    head.start()
    gsum.finish()

    swap = remote(apt.at[asum.own], ap64, fsend.at[0], frecv.at[0], {"prow": to_row, "pcol": to_col})

    def hand_on():
        asum.total()

        @pl.when(moves)
        def _():
            swap.start()

        @pl.when(stays)
        def _():
            ap64[...] = apt[asum.own, :]

    def relay():
        head.far()
        top.near()

    stages = iter([hand_on, head.near, relay, lambda: None])
    linv = lower_inverse(gfull[...], lambda: next(stages)())
    linv_s[...] = linv

    @pl.when(moves)
    def _():
        swap.wait_recv()

    @pl.when(jnp.logical_not(corner))
    def _():
        top_piece(0).wait_recv()

    out_ref[pl.ds(pl.multiple_of(pcol * rows, rows), rows), :] = mm(ap64[...], linv, NT) - ae64[...]

    def along_x(src, dst, sends, recvs, dx):
        return remote(src, dst, sends.at[dx], recvs.at[dx], {"pcol": (x + dx) % NX * NZ + z})

    def along_z(dz):
        return remote(mown, mz.at[dz], zsend.at[dz], zrecv.at[dz], {"pcol": x * NZ + (z + dz) % NZ})

    def m_scatter():
        lanes = 2 * rows
        block = pcol // 2 * lanes
        p = pt_ref[:, :, pl.ds(pl.multiple_of(block, lanes), lanes)].reshape(nb, lanes)
        row, lane = iota((nb, lanes), 0), iota((nb, lanes), 1)
        v = mm(linv_s[...], p) - (row == lane + block + prow * wide).astype(F32)
        v = jnp.where(lane // rows == pcol % 2, v, 0.0)
        av = out_ref[pl.ds(pl.multiple_of(pcol * rows, rows), rows), :]
        mpart[...] = mm(v, jnp.concatenate([av, av], 0))
        msum.start()

    def m_x():
        mq[...] = msum.total()
        for dx in range(1, NX):
            piece = pl.ds(pl.multiple_of((x + dx) % NX * 8, 8), 8)
            along_x(mq.at[piece], mx.at[dx], xsend, xrecv, dx).start()

    def m_z():
        total = mq[pl.ds(pl.multiple_of(x * 8, 8), 8), :]
        for dx in range(1, NX):
            along_x(mx.at[dx], mx.at[dx], xsend, xrecv, dx).wait_recv()
            total = total + mx[dx]
        mown[...] = total
        for dz in range(1, NZ):
            along_z(dz).start()

    m_rows = pl.ds(pl.multiple_of(prow * q + x * 8, 8), 8)
    m_own = mraw.at[m_rows]

    def m_back():
        total = mown[...]
        for dz in range(1, NZ):
            along_z(dz).wait_recv()
            total = total + mz[dz]
        mraw[m_rows, :] = total
        for dx in range(1, NX):
            along_x(m_own, m_own, xgsend, xgrecv, dx).start()

    def m_share():
        for dx in range(1, NX):
            along_x(m_own, m_own, xgsend, xgrecv, dx).wait_recv()
        msum.share()

    def factor_first():
        linv = linv_s[...]
        first = ptop[...].reshape(nb, nb)
        side = mm(linv, first)
        r, c = iota((nb, nb), 0), iota((nb, nb), 1)
        ygram = 2.0 * (r == c).astype(F32) - side - mm(first, linv, ((0,), (1,)))
        t_s[...] = jnp.where(r < c, ygram, jnp.where(r == c, 0.5 * ygram, 0.0))

    def factor_second():
        blocks = [slice(k * BASE, (k + 1) * BASE) for k in range(nb // BASE)]
        inverses = [upper_base(t_s[k, k]) for k in blocks]
        for k, inverse in zip(blocks, inverses):
            t_s[k, k] = inverse

    def merge(size):
        sides = []
        for k in range(0, nb, 2 * size):
            lo, hi = slice(k, k + size), slice(k + size, k + 2 * size)
            sides.append((lo, hi, -mm(t_s[lo, lo], mm(t_s[lo, hi], t_s[hi, hi]))))
        for lo, hi, side in sides:
            t_s[lo, hi] = side

    def before():
        asum.spread()
        part.start()
        m_scatter()
        head.finish()

    def first():
        factor_first()
        top.far()

    def second():
        m_x()
        asum.forward()

    def fourth():
        m_z()
        part.near()

    def fifth():
        merge(BASE)
        merge(2 * BASE)
        part.far()

    flush = gather(
        lambda xx, zz: out_ref.at[pl.ds(pl.multiple_of((xx * NZ + zz) * rows, rows), rows)],
        send,
        recv,
        before,
        (first, second, factor_second, fourth, fifth, m_back, m_share),
    )

    asum.finish()
    top.finish()
    part.finish()
    linv, t = linv_s[...], t_s[...]
    e = (iota((nb, cols), 0) == iota((nb, cols), 1)) & (pcol == 0)
    vct = mm(linv, pct[...].reshape(nb, cols)) - e.astype(F32)
    xc = mm(t, mm(linv, apt[...], NT) - ae[...], TN)
    d_ref[...] = mm(t, vct)
    msum.finish()
    k = mm(t, mm(mraw[...], t), TN)
    b = xc - mm(0.5 * (k + k.T), vct)
    b_ref[...] = b
    c_ref[...] = mm(linv, b, TN)
    sel = (iota((8, nb), 1) == iota((8, nb), 0) + 8 * pcol).astype(F32)
    kt = mm(sel, k, NT)
    l_ref[0:8, :] = kt
    l_ref[8:16, :] = mm(kt, linv)
    l_ref[16:24, :] = mm(sel, t, NT)

    flush()
    panel_flush()
    gsum.flush()
    asum.flush()
    msum.flush()

    @pl.when(prow == 0)
    def _():
        for k in range(1, 8):
            top_piece(k).wait_send()

    @pl.when((prow == 0) & (pcol != 0))
    def _():
        top_piece(0).wait_send()

    @pl.when(moves)
    def _():
        swap.wait_send()

    for dx in range(1, NX):
        along_x(mq.at[pl.ds(0, 8)], mx.at[dx], xsend, xrecv, dx).wait_send()
        along_x(m_own, m_own, xgsend, xgrecv, dx).wait_send()
    for dz in range(1, NZ):
        along_z(dz).wait_send()


def params(cid):
    return pltpu.CompilerParams(collective_id=cid, has_side_effects=True, vmem_limit_bytes=LIMIT)


def plain(**kw):
    return pltpu.CompilerParams(vmem_limit_bytes=LIMIT, **kw)


def shape(*dims):
    return jax.ShapeDtypeStruct(dims, F32)


def update_kernel(a_ref, pt_ref, av_ref, c_ref, d_ref, b_ref, l_ref, o_ref, w_ref, ch, cl, dh, dl):
    step = pl.program_id(0)

    @pl.when(step == 0)
    def _():
        ch[...], cl[...] = split(c_ref[...])
        dh[...], dl[...] = split(d_ref[...])

    p, v = pt_ref[...], av_ref[...]
    ps, vs = split(p), split(v)
    both = mm3(ps, (ch[...], cl[...]), TN) + mm3(vs, (dh[...], dl[...]))
    o_ref[...] = a_ref[...] - both
    w_ref[...] = mm3(split(l_ref[16:24, :]), vs, NT) - 0.5 * mm3(split(l_ref[8:16, :]), ps)

    @pl.when((lax.axis_index("prow") == 0) & (step == 0))
    def _():
        nb = b_ref.shape[0]
        o_ref[0:nb, :] += b_ref[...]
        w_ref[:, 0:nb] += 0.5 * l_ref[0:8, :]


def shards(trailing, panel):
    rows, cols = trailing.shape
    pt_own = panel.T
    nc = pt_own.shape[0]
    nb = nc * lax.axis_size("pcol")
    dma = pltpu.SemaphoreType.DMA
    buf = lambda *dims: pltpu.VMEM(dims, F32)

    q = nb // 8
    pt, av, c, d, b, l = pl.pallas_call(
        main_kernel,
        out_shape=(shape(NX, nb // NX, rows), shape(rows, nb)) + (shape(nb, cols),) * 3 + (shape(24, nb),),
        in_specs=[VMEM, ANY],
        out_specs=(VMEM,) * 6,
        scratch_shapes=[
            buf(rows, cols),
            pltpu.VMEM((rows, cols), jnp.bfloat16),
            pltpu.VMEM((rows, cols), jnp.bfloat16),
            buf(nb, cols),
            buf(cols, nb),
            buf(cols // 8, nb),
            buf(cols // 8, nb),
            buf(nb, nb),
            buf(nb, nb),
            buf(8, q, nb),
            buf(cols, nb),
            buf(cols, nb),
            buf(cols // 2, nb),
            buf(NY, cols // 8, nb),
            buf(cols // 2, nb),
            buf(NX, nb // NX, nb),
            buf(NX, nb // NX, cols),
            buf(nb, nb),
            buf(nb, nb),
            buf(nb, nb),
            buf(8, q, nb),
            buf(q, nb),
            buf(NX, 8, nb),
            buf(NZ, 8, nb),
            buf(8, nb),
            buf(nb, nb),
            dma((1,)),
            dma((NX, NZ)),
            dma((NX, NZ)),
            dma((4,)),
            dma((1,)),
            dma((2, 8)),
            dma((2, 8)),
            dma((4,)),
            dma((1,)),
            dma((11,)),
            dma((11,)),
            dma((4,)),
            dma((1,)),
            dma((1,)),
            dma((1,)),
            dma((8,)),
            dma((1,)),
            dma((NX, NZ)),
            dma((NX, NZ)),
            dma((NX,)),
            dma((NX,)),
            dma((NZ,)),
            dma((NZ,)),
            dma((NX,)),
            dma((NX,)),
            dma((2, 8)),
            dma((2, 8)),
        ],
        compiler_params=params(2),
    )(pt_own, trailing)

    tile = 2 * nb
    whole = lambda *dims: pl.BlockSpec(dims, lambda i: (0, 0))
    updated, wt = pl.pallas_call(
        update_kernel,
        grid=(rows // tile,),
        out_shape=(shape(rows, cols), shape(nc, rows)),
        in_specs=[
            pl.BlockSpec((tile, cols), lambda i: (i, 0)),
            pl.BlockSpec((nb, tile), lambda i: (0, i)),
            pl.BlockSpec((tile, nb), lambda i: (i, 0)),
            whole(nb, cols),
            whole(nb, cols),
            whole(nb, cols),
            whole(24, nb),
        ],
        out_specs=(pl.BlockSpec((tile, cols), lambda i: (i, 0)), pl.BlockSpec((nc, tile), lambda i: (0, i))),
        scratch_shapes=[pltpu.VMEM((nb, cols), jnp.bfloat16)] * 4,
        compiler_params=plain(dimension_semantics=("arbitrary",)),
    )(trailing, pt.reshape(nb, rows), av, c, d, b, l)
    return updated, wt.T


def solution(mesh):
    in_specs = (P("prow", "pcol"), P("prow", "pcol"))
    out_specs = (P("prow", "pcol"), P("prow", "pcol"))
    return jax.shard_map(shards, mesh=mesh, in_specs=in_specs, out_specs=out_specs, check_vma=False)
```

```python
import jax
import jax.numpy as jnp
from jax import lax
from jax.experimental import pallas as pl
from jax.experimental.pallas import tpu as pltpu
from jax.sharding import PartitionSpec as P

HIGH = lax.Precision.HIGHEST
F32 = jnp.float32
NX, NZ, NY = 4, 8, 4
VMEM = pl.BlockSpec(memory_space=pltpu.VMEM)
ANY = pl.BlockSpec(memory_space=pl.ANY)
LIMIT = 48 << 20
NN, NT, TN = ((1,), (0,)), ((1,), (1,)), ((0,), (0,))


def mm(a, b, dims=NN):
    return lax.dot_general(a, b, (dims, ((), ())), precision=HIGH, preferred_element_type=F32)


def split(x):
    hi = x.astype(jnp.bfloat16)
    return hi, (x - hi.astype(F32)).astype(jnp.bfloat16)


def mm3(a, b, dims=NN):
    (ah, al), (bh, bl) = a, b

    def dot(l, r):
        return lax.dot_general(l, r, (dims, ((), ())), preferred_element_type=F32)

    return dot(ah, bh) + (dot(ah, bl) + dot(al, bh))


def iota(shape, dim):
    return lax.broadcasted_iota(jnp.int32, shape, dim)


BASE = 64


def base_inverse(block):
    n = BASE
    row = iota((8, 128), 0)
    eye = (iota((n, n), 0) == iota((n, n), 1)).astype(F32)
    x = jnp.concatenate([block, eye], axis=1)
    groups = [x[8 * g : 8 * g + 8, :] for g in range(n // 8)]
    zero = jnp.zeros((8, 128), F32)

    def column(vals):
        v = zero
        for i, e in enumerate(vals):
            if e is not None:
                v = jnp.where(row == i, e, v)
        return v

    out = []
    for k in range(n // 8):
        gk = groups[k]
        rows = [jnp.broadcast_to(gk[m : m + 1, :], (8, 128)) for m in range(8)]
        a = [[None] * 8 for _ in range(8)]
        for i in range(8):
            for j in range(i + 1):
                a[i][j] = jnp.broadcast_to(rows[j][:, 8 * k + i : 8 * k + i + 1], (8, 128))
        acols = {
            g: [jnp.broadcast_to(groups[g][:, 8 * k + m : 8 * k + m + 1], (8, 128)) for m in range(8)]
            for g in range(k + 1, n // 8)
        }
        l = [[None] * 8 for _ in range(8)]
        r = [None] * 8
        for j in range(8):
            r[j] = lax.rsqrt(a[j][j])
            for i in range(j + 1, 8):
                l[i][j] = a[i][j] * r[j]
            for i in range(j + 1, 8):
                for c in range(j + 1, i + 1):
                    a[i][c] = a[i][c] - l[i][j] * l[c][j]
        w = [[None] * 8 for _ in range(8)]
        for j in range(8):
            w[j][j] = r[j]
            for i in range(j + 1, 8):
                s = l[i][j] * w[j][j]
                for c in range(j + 1, i):
                    s = s + l[i][c] * w[c][j]
                w[i][j] = -(s * r[i])
        cols = [column([w[i][m] for i in range(8)]) for m in range(8)]
        u = cols[0] * rows[0]
        for m in range(1, 8):
            u = u + cols[m] * rows[m]
        out.append(u)
        if k + 1 < n // 8:
            cols_t = [column([w[j][m] for m in range(8)]) for j in range(8)]
            z = cols_t[0] * jnp.broadcast_to(u[0:1, :], (8, 128))
            for j in range(1, 8):
                z = z + cols_t[j] * jnp.broadcast_to(u[j : j + 1, :], (8, 128))
            z_rows = [jnp.broadcast_to(z[m : m + 1, :], (8, 128)) for m in range(8)]
            for g in range(k + 1, n // 8):
                s = acols[g][0] * z_rows[0]
                for m in range(1, 8):
                    s = s + acols[g][m] * z_rows[m]
                groups[g] = groups[g] - s
    inv = jnp.concatenate(out, axis=0)[:, n:]
    return jnp.where(iota((n, n), 1) <= iota((n, n), 0), inv, 0.0)


def lower_inverse(gram, hook):
    size = gram.shape[0]
    if size == BASE:
        inv = base_inverse(gram)
        hook()
        return inv
    h = size // 2
    i_top = lower_inverse(gram[:h, :h], hook)
    l_side = mm(gram[h:, :h], i_top, NT)
    i_bot = lower_inverse(gram[h:, h:] - mm(l_side, l_side, NT), hook)
    i_side = -mm(i_bot, mm(l_side, i_top))
    top = jnp.concatenate([i_top, jnp.zeros((h, h), F32)], 1)
    return jnp.concatenate([top, jnp.concatenate([i_side, i_bot], 1)], 0)


def upper_base(y):
    n = y.shape[0]
    r, c = iota((n, n), 0), iota((n, n), 1)
    inv = jnp.where(r == c, 1.0 / y, 0.0)
    s = 1
    while s < n:
        off = (r // (2 * s) == c // (2 * s)) & (r // s != c // s) & (r < c)
        inv = inv - mm(inv, mm(jnp.where(off, y, 0.0), inv))
        s *= 2
    return inv


def remote(src, dst, send, recv, peer):
    return pltpu.make_async_remote_copy(
        src_ref=src, dst_ref=dst, send_sem=send, recv_sem=recv, device_id=peer, device_id_type=pl.DeviceIdType.MESH
    )


def place():
    prow, pcol = lax.axis_index("prow"), lax.axis_index("pcol")
    return prow // 2, prow % 2, pcol // NZ, pcol % NZ


ORDER = (1, 7, 2, 6, 3, 5, 4)


class Gather:
    def __init__(self, at, send, recv):
        _, self.core, self.x, self.z = place()
        self.at, self.send, self.recv = at, send, recv

    def slab(self, xx, zz):
        return self.at(xx % NX, (zz + 2 * NZ) % NZ)

    def copy(self, piece, dx, dist, x, z):
        return remote(piece, piece, self.send.at[dx, dist], self.recv.at[dx, dist], {"pcol": x % NX * NZ + (z + NZ) % NZ})

    def along_z(self, dx, dist):
        step = 1 if dist <= NZ // 2 else -1
        return self.copy(self.slab(self.x + dx, self.z + step - dist), dx, dist, self.x, self.z + step)

    def along_x(self, dx, dist):
        return self.copy(self.slab(self.x, self.z - dist), dx, dist, self.x + NX - dx, self.z)

    def arrived(self, dx, dist):
        self.copy(self.slab(self.x + dx, self.z - dist), dx, dist, self.x, self.z + 1).wait_recv()

    def passed_on(self, dx, dist):
        if dist < NZ // 2:
            self.along_z(dx, dist + 1).start()
        elif dist > NZ // 2 + 1:
            self.along_z(dx, dist - 1).start()

    def start(self):
        @pl.when(self.core == 0)
        def _():
            self.along_z(0, 1).start()
            self.along_z(0, NZ - 1).start()
            for dx in range(1, NX):
                self.along_x(dx, 0).start()

        @pl.when(self.core == 1)
        def _():
            for dx in range(1, NX):
                self.along_x(dx, 0).start()
            self.along_z(0, 1).start()
            self.along_z(0, NZ - 1).start()

    def enter(self):
        @pl.when(self.core == 1)
        def _():
            for dx in range(1, NX):
                self.arrived(dx, 0)
                self.along_z(dx, 1).start()
                self.along_z(dx, NZ - 1).start()

    def step(self, i):
        dist = ORDER[i]

        @pl.when(self.core == 0)
        def _():
            self.arrived(0, dist)
            self.passed_on(0, dist)
            for dx in range(1, NX):
                self.along_x(dx, dist).start()
            for dx in range(1, NX):
                self.arrived(dx, ORDER[i - 1] if i else 0)

        @pl.when(self.core == 1)
        def _():
            for dx in range(NX):
                self.arrived(dx, dist)
                self.passed_on(dx, dist)

    def end(self):
        @pl.when(self.core == 0)
        def _():
            for dx in range(1, NX):
                self.arrived(dx, ORDER[-1])

    def flush(self):
        for dx in range(NX):
            for dist in range(NZ):
                if dx or dist:
                    self.copy(self.slab(self.x, self.z), dx, dist, self.x, self.z + 1).wait_send()


class Broadcast:
    def __init__(self, y0, core0, src, out, send, recv):
        y, core, _, _ = place()
        away = (y + NY - y0) % NY
        self.owner = (away == 0) & (core == core0)
        self.next = (away == 1) & (core == core0)
        self.last = (away == 3) & (core == core0)
        self.far_one = (away == 2) & (core == core0)
        self.relay = (away != 0) & (core == core0)
        self.leaf = core != core0
        mate = {"prow": y * 2 + 1 - core}
        up, down = {"prow": (y + 1) % NY * 2 + core}, {"prow": (y + 3) % NY * 2 + core}
        self.up = remote(src, out, send.at[1], recv.at[0], up)
        self.down = remote(src, out, send.at[2], recv.at[0], down)
        self.own = remote(src, out, send.at[0], recv.at[0], mate)
        self.on = remote(out, out, send.at[1], recv.at[0], up)
        self.pass_on = remote(out, out, send.at[0], recv.at[0], mate)
        self.keep = pltpu.make_async_copy(src, out, send.at[3])

    def start(self):
        @pl.when(self.owner)
        def _():
            self.up.start()
            self.down.start()
            self.own.start()
            self.keep.start()

    def near(self):
        @pl.when(self.next)
        def _():
            self.on.wait_recv()
            self.on.start()
            self.pass_on.start()

        @pl.when(self.last)
        def _():
            self.pass_on.wait_recv()
            self.pass_on.start()

    def far(self):
        @pl.when(self.far_one)
        def _():
            self.pass_on.wait_recv()
            self.pass_on.start()

    def finish(self):
        @pl.when(self.relay)
        def _():
            self.pass_on.wait_send()

        @pl.when(self.next)
        def _():
            self.on.wait_send()

        @pl.when(self.leaf)
        def _():
            self.pass_on.wait_recv()

        @pl.when(self.owner)
        def _():
            self.up.wait_send()
            self.down.wait_send()
            self.own.wait_send()
            self.keep.wait()


class DirectSum:
    def __init__(self, s, out, parts, send, recv):
        y, core, _, _ = place()
        self.s, self.out, self.parts, self.send, self.recv = s, out, parts, send, recv
        self.prow = y * 2 + core
        self.q = s.shape[0] // 8

    def rows(self, d):
        return pl.ds(pl.multiple_of((self.prow + d) % 8 * self.q, self.q), self.q)

    def scatter(self, d):
        peer = {"prow": (self.prow + d) % 8}
        return remote(self.s.at[self.rows(d)], self.parts.at[d], self.send.at[0, d], self.recv.at[0, d], peer)

    def spread(self, d):
        mine = self.out.at[self.rows(0)]
        return remote(mine, mine, self.send.at[1, d], self.recv.at[1, d], {"prow": (self.prow + d) % 8})

    def start(self):
        for d in range(1, 8):
            self.scatter(d).start()

    def total(self):
        total = self.s[self.rows(0), :]
        for d in range(1, 8):
            self.scatter(d).wait_recv()
            total = total + self.parts[d]
        return total

    def share(self):
        for d in range(1, 8):
            self.spread(d).start()

    def finish(self):
        for d in range(1, 8):
            self.spread(d).wait_recv()

    def flush(self):
        for d in range(1, 8):
            self.scatter(d).wait_send()
            self.spread(d).wait_send()


class Sum:
    def __init__(self, s, out, half, quarter, acc, send, recv):
        y, core, _, _ = place()
        self.s, self.out, self.half, self.quarter, self.acc, self.send, self.recv = s, out, half, quarter, acc, send, recv
        self.y, self.core = y, core
        self.width = s.shape[1]
        self.q = s.shape[0] // 8
        self.h = 4 * self.q
        self.mate = {"prow": y * 2 + 1 - core}
        self.own = self.rows(core * self.h + y * self.q, self.q)
        self.sent = []

    def rows(self, start, n):
        return pl.ds(pl.multiple_of(start, n), n)

    def copy(self, src, dst, i, peer):
        return remote(src, dst, self.send.at[i], self.recv.at[i], peer)

    def go(self, *args):
        copy = self.copy(*args)
        copy.start()
        self.sent.append(copy)
        return copy

    def along(self, dy):
        return {"prow": (self.y + dy) % NY * 2 + self.core}

    def exchange(self):
        self.first = self.go(self.s.at[self.rows((1 - self.core) * self.h, self.h)], self.half, 0, self.mate)

    def quarters(self):
        self.first.wait_recv()
        self.acc[...] = self.s[self.rows(self.core * self.h, self.h), :] + self.half[...]
        for dy in range(1, NY):
            piece = self.rows((self.y + dy) % NY * self.q, self.q)
            self.go(self.acc.at[piece], self.quarter.at[dy], dy, self.along(dy))

    def total(self):
        total = self.acc[self.rows(self.y * self.q, self.q), :]
        for dy in range(1, NY):
            self.copy(self.quarter.at[dy], self.quarter.at[dy], dy, self.mate).wait_recv()
            total = total + self.quarter[dy]
        self.out[self.own, pl.ds(0, self.width)] = total

    def spread(self):
        piece = self.out.at[self.own]
        for dy in range(1, NY):
            self.go(piece, piece, 3 + dy, self.along(dy))
        self.go(piece, piece, 7, self.mate)

    def forward(self):
        for dy in range(1, NY):
            piece = self.out.at[self.rows(self.core * self.h + (self.y + NY - dy) % NY * self.q, self.q)]
            self.copy(piece, piece, 3 + dy, self.mate).wait_recv()
            self.go(piece, piece, 7 + dy, self.mate)

    def finish(self):
        for dy in range(NY):
            piece = self.out.at[self.rows((1 - self.core) * self.h + (self.y + NY - dy) % NY * self.q, self.q)]
            self.copy(piece, piece, 7 + dy, self.mate).wait_recv()

    def flush(self):
        for copy in self.sent:
            copy.wait_send()


def main_kernel(
    slab_ref,
    a_ref,
    pt_out,
    ap_out,
    ae_out,
    c_ref,
    d_ref,
    e_ref,
    b_ref,
    l_ref,
    pt_ref,
    apr,
    aer,
    a_buf,
    a_hi,
    a_lo,
    ae,
    aet,
    gram,
    gfull,
    gparts,
    aps,
    apt,
    ahalf,
    aquarter,
    aacc,
    ptop,
    pct,
    linv_s,
    t_s,
    mpart,
    mparts,
    mq,
    mx,
    mz,
    mown,
    mraw,
    acopy,
    panel_send,
    panel_recv,
    esend,
    erecv,
    gsend,
    grecv,
    hsend,
    hrecv,
    asend,
    arecv,
    psend,
    precv,
    fsend,
    frecv,
    ksend,
    krecv,
    rsend,
    rrecv,
    send,
    recv,
    xsend,
    xrecv,
    zsend,
    zrecv,
    xgsend,
    xgrecv,
    wsend,
    wrecv,
):
    y, core, x, z = place()
    prow, pcol = y * 2 + core, x * NZ + z
    nb = apr.shape[1]
    cols = ae.shape[1]
    rows = cols // 8
    q = nb // 8
    wide = slab_ref.shape[1]

    load = pltpu.make_async_copy(a_ref, a_buf, acopy.at[0])
    load.start()
    own_slab = pt_ref.at[x, pl.ds(pl.multiple_of(z * 8, 8), 8)]
    take = pltpu.make_async_copy(slab_ref, own_slab, acopy.at[1])
    take.start()

    to_row, to_col = pcol // 4, pcol % 4 * 8 + core * NY + y
    source_col, j = prow * 4 + pcol // 8, pcol % 8
    stays = (to_row == prow) & (to_col == pcol)
    moves = jnp.logical_not(stays)
    corner = (prow == 0) & (pcol == 0)
    source = {"prow": j % NY * 2 + j // NY, "pcol": source_col}
    barrier = pltpu.get_barrier_semaphore()
    peers = [{"prow": (prow + d) % 8} for d in range(1, 8)]
    peers += [{"pcol": (x + dx) % NX * NZ + z} for dx in range(1, NX)]
    peers += [{"pcol": x * NZ + (z + dz) % NZ} for dz in range(1, NZ)]

    def greet(peer):
        pl.semaphore_signal(barrier, inc=1, device_id=peer, device_id_type=pl.DeviceIdType.MESH)

    for peer in peers:
        greet(peer)

    @pl.when(moves)
    def _():
        greet(source)

    @pl.when(jnp.logical_not(corner))
    def _():
        greet({"prow": 0, "pcol": source_col})

    extra = jnp.where(moves, 1, 0) + jnp.where(prow == 0, 8, 0) - jnp.where(corner, 1, 0)
    pl.semaphore_wait(barrier, len(peers) + extra)
    take.wait()

    def slab_rows(c):
        return pl.ds(pl.multiple_of(c * rows, rows), rows)

    def slabs(ref):
        return lambda xx, zz: ref.at[slab_rows(xx * NZ + zz)]

    top = Broadcast(0, 0, a_ref.at[pl.ds(0, nb)], ae, esend, erecv)
    window = pl.ds(pl.multiple_of(pcol % 4 * cols, cols), cols)
    part = Broadcast(x, z // 4, pt_ref.at[:, :, window], pct, psend, precv)
    head = Broadcast(0, 0, pt_ref.at[:, :, pl.ds(0, nb)], ptop, hsend, hrecv)

    def top_piece(k):
        peer = {"prow": pcol // 4, "pcol": pcol % 4 * 8 + k}
        dst = aer.at[slab_rows(pcol % 4 * 8 + k)]
        return remote(aet.at[pl.ds(k * rows, rows)], dst, ksend.at[k], krecv.at[0], peer)

    def take_a():
        load.wait()
        a_hi[...], a_lo[...] = split(a_buf[...])

        @pl.when(prow == 0)
        def _():
            aet[...] = a_buf[0:nb, :].T
            for k in range(1, 8):
                top_piece(k).start()

        @pl.when((prow == 0) & (pcol != 0))
        def _():
            top_piece(0).start()

        @pl.when(corner)
        def _():
            aer[0:rows, :] = aet[0:rows, :]

    pgather = Gather(
        lambda xx, zz: pt_ref.at[xx, pl.ds(pl.multiple_of(zz * 8, 8), 8)], panel_send, panel_recv
    )
    egather = Gather(slabs(aer), rsend, rrecv)
    agather = Gather(slabs(apr), send, recv)
    pgather.start()
    top.start()
    pgather.enter()
    for i in range(7):
        pgather.step(i)
        if i == 1:
            take_a()
    pgather.end()
    keep_p = pltpu.make_async_copy(pt_ref, pt_out, acopy.at[2])
    keep_a = pltpu.make_async_copy(apr, ap_out, acopy.at[3])
    keep_e = pltpu.make_async_copy(aer, ae_out, acopy.at[4])
    keep_p.start()

    @pl.when(jnp.logical_not(corner))
    def _():
        top_piece(0).wait_recv()

    egather.start()
    panel = pt_ref[...].reshape(nb, wide)
    gram[...] = mm(panel, panel, NT)

    gsum = DirectSum(gram, gfull, gparts, gsend, grecv)
    asum = Sum(aps, apt, ahalf, aquarter, aacc, asend, arecv)
    msum = DirectSum(mpart, mraw, mparts, wsend, wrecv)
    gsum.start()
    aps[...] = mm3(split(panel), (a_hi[...], a_lo[...])).T
    asum.exchange()
    egather.enter()
    gfull[gsum.rows(0), :] = gsum.total()
    gsum.share()
    egather.step(0)
    asum.quarters()
    head.start()
    gsum.finish()

    swap = remote(apt.at[asum.own], apr.at[slab_rows(to_col)], fsend.at[0], frecv.at[0], {"prow": to_row, "pcol": to_col})

    def chol_first():
        asum.total()

        @pl.when(moves)
        def _():
            swap.start()

        @pl.when(stays)
        def _():
            apr[slab_rows(pcol), :] = apt[asum.own, :]

        egather.step(1)

    def chol_second():
        head.near()
        egather.step(2)
        egather.step(3)
        asum.spread()

    def chol_third():
        @pl.when(moves)
        def _():
            swap.wait_recv()

        agather.start()
        top.near()
        egather.step(4)

    def chol_fourth():
        head.far()
        egather.step(5)
        agather.enter()

    stages = iter([chol_first, chol_second, chol_third, chol_fourth])
    linv = lower_inverse(gfull[...], lambda: next(stages)())
    linv_s[...] = linv

    def along_x(src, dst, sends, recvs, dx):
        return remote(src, dst, sends.at[dx], recvs.at[dx], {"pcol": (x + dx) % NX * NZ + z})

    def along_z(dz):
        return remote(mown, mz.at[dz], zsend.at[dz], zrecv.at[dz], {"pcol": x * NZ + (z + dz) % NZ})

    def m_scatter():
        lanes = 2 * rows
        block = pcol // 2 * lanes
        p = pt_ref[:, :, pl.ds(pl.multiple_of(block, lanes), lanes)].reshape(nb, lanes)
        row, lane = iota((nb, lanes), 0), iota((nb, lanes), 1)
        v = mm(linv_s[...], p) - (row == lane + block + prow * wide).astype(F32)
        v = jnp.where(lane // rows == pcol % 2, v, 0.0)
        av = mm(apr[slab_rows(pcol), :], linv_s[...], NT) - aer[slab_rows(pcol), :]
        mpart[...] = mm(v, jnp.concatenate([av, av], 0))
        msum.start()

    def m_x():
        mq[...] = msum.total()
        for dx in range(1, NX):
            piece = pl.ds(pl.multiple_of((x + dx) % NX * 8, 8), 8)
            along_x(mq.at[piece], mx.at[dx], xsend, xrecv, dx).start()

    def m_z():
        total = mq[pl.ds(pl.multiple_of(x * 8, 8), 8), :]
        for dx in range(1, NX):
            along_x(mx.at[dx], mx.at[dx], xsend, xrecv, dx).wait_recv()
            total = total + mx[dx]
        mown[...] = total
        for dz in range(1, NZ):
            along_z(dz).start()

    m_rows = pl.ds(pl.multiple_of(prow * q + x * 8, 8), 8)
    m_own = mraw.at[m_rows]

    def m_back():
        total = mown[...]
        for dz in range(1, NZ):
            along_z(dz).wait_recv()
            total = total + mz[dz]
        mraw[m_rows, :] = total
        for dx in range(1, NX):
            along_x(m_own, m_own, xgsend, xgrecv, dx).start()

    def m_share():
        for dx in range(1, NX):
            along_x(m_own, m_own, xgsend, xgrecv, dx).wait_recv()
        msum.share()

    def factor_first():
        linv = linv_s[...]
        first = ptop[...].reshape(nb, nb)
        side = mm(linv, first)
        r, c = iota((nb, nb), 0), iota((nb, nb), 1)
        ygram = 2.0 * (r == c).astype(F32) - side - mm(first, linv, ((0,), (1,)))
        t_s[...] = jnp.where(r < c, ygram, jnp.where(r == c, 0.5 * ygram, 0.0))

    def factor_second():
        blocks = [slice(k * BASE, (k + 1) * BASE) for k in range(nb // BASE)]
        inverses = [upper_base(t_s[k, k]) for k in blocks]
        for k, inverse in zip(blocks, inverses):
            t_s[k, k] = inverse

    def merge(size):
        sides = []
        for k in range(0, nb, 2 * size):
            lo, hi = slice(k, k + size), slice(k + size, k + 2 * size)
            sides.append((lo, hi, -mm(t_s[lo, lo], mm(t_s[lo, hi], t_s[hi, hi]))))
        for lo, hi, side in sides:
            t_s[lo, hi] = side

    m_scatter()
    part.start()
    egather.step(6)
    agather.step(0)
    egather.end()
    keep_e.start()
    head.finish()
    factor_first()
    asum.forward()
    top.far()
    agather.step(1)
    m_x()
    agather.step(2)
    factor_second()
    agather.step(3)
    m_z()
    part.near()
    merge(BASE)
    agather.step(4)
    merge(2 * BASE)
    m_back()
    part.far()
    agather.step(5)
    m_share()
    agather.step(6)
    asum.finish()
    top.finish()
    part.finish()
    linv, t = linv_s[...], t_s[...]
    e = (iota((nb, cols), 0) == iota((nb, cols), 1)) & (pcol == 0)
    vct = mm(linv, pct[...].reshape(nb, cols)) - e.astype(F32)
    xc = mm(t, mm(linv, apt[...], NT) - ae[...], TN)
    d = mm(t, vct)
    e_ref[...] = d
    d_ref[...] = mm(linv, d, TN)
    agather.end()
    keep_a.start()
    msum.finish()
    k = mm(t, mm(mraw[...], t), TN)
    b = xc - mm(0.5 * (k + k.T), vct)
    b_ref[...] = b
    c_ref[...] = mm(linv, b, TN)
    sel = (iota((8, nb), 1) == iota((8, nb), 0) + 8 * pcol).astype(F32)
    kt = mm(sel, k, NT)
    l_ref[0:8, :] = kt
    l_ref[8:16, :] = mm(kt, linv)
    ts = mm(sel, t, NT)
    l_ref[16:24, :] = mm(ts, linv)
    l_ref[24:32, :] = ts

    pgather.flush()
    egather.flush()
    agather.flush()
    keep_p.wait()
    keep_e.wait()
    keep_a.wait()
    gsum.flush()
    asum.flush()
    msum.flush()

    @pl.when(prow == 0)
    def _():
        for k in range(1, 8):
            top_piece(k).wait_send()

    @pl.when((prow == 0) & (pcol != 0))
    def _():
        top_piece(0).wait_send()

    @pl.when(moves)
    def _():
        swap.wait_send()

    for dx in range(1, NX):
        along_x(mq.at[pl.ds(0, 8)], mx.at[dx], xsend, xrecv, dx).wait_send()
        along_x(m_own, m_own, xgsend, xgrecv, dx).wait_send()
    for dz in range(1, NZ):
        along_z(dz).wait_send()


def params(cid):
    return pltpu.CompilerParams(collective_id=cid, has_side_effects=True, vmem_limit_bytes=LIMIT)


def plain(**kw):
    return pltpu.CompilerParams(vmem_limit_bytes=LIMIT, **kw)


def shape(*dims):
    return jax.ShapeDtypeStruct(dims, F32)


def update_kernel(a_ref, pt_ref, ap_ref, ae_ref, c_ref, d_ref, e_ref, b_ref, l_ref, o_ref, w_ref, ch, cl, dh, dl, eh, el):
    step = pl.program_id(0)

    @pl.when(step == 0)
    def _():
        ch[...], cl[...] = split(c_ref[...])
        dh[...], dl[...] = split(d_ref[...])
        eh[...], el[...] = split(-e_ref[...])

    ps, vs, es = split(pt_ref[...]), split(ap_ref[...]), split(ae_ref[...])
    both = mm3(ps, (ch[...], cl[...]), TN) + mm3(vs, (dh[...], dl[...])) + mm3(es, (eh[...], el[...]))
    o_ref[...] = a_ref[...] - both
    w = mm3(split(l_ref[16:24, :]), vs, NT) - mm3(split(l_ref[24:32, :]), es, NT)
    w_ref[...] = w - 0.5 * mm3(split(l_ref[8:16, :]), ps)

    @pl.when((lax.axis_index("prow") == 0) & (step == 0))
    def _():
        nb = b_ref.shape[0]
        o_ref[0:nb, :] += b_ref[...]
        w_ref[:, 0:nb] += 0.5 * l_ref[0:8, :]


def shards(trailing, panel):
    rows, cols = trailing.shape
    pt_own = panel.T
    nc = pt_own.shape[0]
    nb = nc * lax.axis_size("pcol")
    dma = pltpu.SemaphoreType.DMA
    buf = lambda *dims: pltpu.VMEM(dims, F32)

    q = nb // 8
    pt, ap, ae, c, d, e, b, l = pl.pallas_call(
        main_kernel,
        out_shape=(shape(NX, nb // NX, rows),) + (shape(rows, nb),) * 2 + (shape(nb, cols),) * 4 + (shape(32, nb),),
        in_specs=[ANY, ANY],
        out_specs=(ANY,) * 3 + (VMEM,) * 5,
        scratch_shapes=[
            buf(NX, nb // NX, rows),
            buf(rows, nb),
            buf(rows, nb),
            buf(rows, cols),
            pltpu.VMEM((rows, cols), jnp.bfloat16),
            pltpu.VMEM((rows, cols), jnp.bfloat16),
            buf(nb, cols),
            buf(cols, nb),
            buf(nb, nb),
            buf(nb, nb),
            buf(8, q, nb),
            buf(cols, nb),
            buf(cols, nb),
            buf(cols // 2, nb),
            buf(NY, cols // 8, nb),
            buf(cols // 2, nb),
            buf(NX, nb // NX, nb),
            buf(NX, nb // NX, cols),
            buf(nb, nb),
            buf(nb, nb),
            buf(nb, nb),
            buf(8, q, nb),
            buf(q, nb),
            buf(NX, 8, nb),
            buf(NZ, 8, nb),
            buf(8, nb),
            buf(nb, nb),
            dma((5,)),
            dma((NX, NZ)),
            dma((NX, NZ)),
            dma((4,)),
            dma((1,)),
            dma((2, 8)),
            dma((2, 8)),
            dma((4,)),
            dma((1,)),
            dma((11,)),
            dma((11,)),
            dma((4,)),
            dma((1,)),
            dma((1,)),
            dma((1,)),
            dma((8,)),
            dma((1,)),
            dma((NX, NZ)),
            dma((NX, NZ)),
            dma((NX, NZ)),
            dma((NX, NZ)),
            dma((NX,)),
            dma((NX,)),
            dma((NZ,)),
            dma((NZ,)),
            dma((NX,)),
            dma((NX,)),
            dma((2, 8)),
            dma((2, 8)),
        ],
        compiler_params=params(2),
    )(pt_own, trailing)

    tile = 2 * nb
    whole = lambda *dims: pl.BlockSpec(dims, lambda i: (0, 0))
    updated, wt = pl.pallas_call(
        update_kernel,
        grid=(rows // tile,),
        out_shape=(shape(rows, cols), shape(nc, rows)),
        in_specs=[
            pl.BlockSpec((tile, cols), lambda i: (i, 0)),
            pl.BlockSpec((nb, tile), lambda i: (0, i)),
            pl.BlockSpec((tile, nb), lambda i: (i, 0)),
            pl.BlockSpec((tile, nb), lambda i: (i, 0)),
            whole(nb, cols),
            whole(nb, cols),
            whole(nb, cols),
            whole(nb, cols),
            whole(32, nb),
        ],
        out_specs=(pl.BlockSpec((tile, cols), lambda i: (i, 0)), pl.BlockSpec((nc, tile), lambda i: (0, i))),
        scratch_shapes=[pltpu.VMEM((nb, cols), jnp.bfloat16)] * 6,
        compiler_params=plain(dimension_semantics=("arbitrary",)),
    )(trailing, pt.reshape(nb, rows), ap, ae, c, d, e, b, l)
    return updated, wt.T


def solution(mesh):
    in_specs = (P("prow", "pcol"), P("prow", "pcol"))
    out_specs = (P("prow", "pcol"), P("prow", "pcol"))
    return jax.shard_map(shards, mesh=mesh, in_specs=in_specs, out_specs=out_specs, check_vma=False)
```

```python
import jax
import jax.numpy as jnp
from jax import lax
from jax.experimental import pallas as pl
from jax.experimental.pallas import tpu as pltpu
from jax.sharding import PartitionSpec as P

HIGH = lax.Precision.HIGHEST
F32 = jnp.float32
NX, NZ, NY = 4, 8, 4
VMEM = pl.BlockSpec(memory_space=pltpu.VMEM)
ANY = pl.BlockSpec(memory_space=pl.ANY)
LIMIT = 48 << 20
NN, NT, TN = ((1,), (0,)), ((1,), (1,)), ((0,), (0,))


def mm(a, b, dims=NN):
    return lax.dot_general(a, b, (dims, ((), ())), precision=HIGH, preferred_element_type=F32)


def split(x):
    hi = x.astype(jnp.bfloat16)
    return hi, (x - hi.astype(F32)).astype(jnp.bfloat16)


def mm3(a, b, dims=NN):
    (ah, al), (bh, bl) = a, b

    def dot(l, r):
        return lax.dot_general(l, r, (dims, ((), ())), preferred_element_type=F32)

    return dot(ah, bh) + (dot(ah, bl) + dot(al, bh))


def iota(shape, dim):
    return lax.broadcasted_iota(jnp.int32, shape, dim)


BASE = 64


def base_inverse(block):
    n = BASE
    row = iota((8, 128), 0)
    eye = (iota((n, n), 0) == iota((n, n), 1)).astype(F32)
    x = jnp.concatenate([block, eye], axis=1)
    groups = [x[8 * g : 8 * g + 8, :] for g in range(n // 8)]
    zero = jnp.zeros((8, 128), F32)

    def column(vals):
        v = zero
        for i, e in enumerate(vals):
            if e is not None:
                v = jnp.where(row == i, e, v)
        return v

    out = []
    for k in range(n // 8):
        gk = groups[k]
        rows = [jnp.broadcast_to(gk[m : m + 1, :], (8, 128)) for m in range(8)]
        a = [[None] * 8 for _ in range(8)]
        for i in range(8):
            for j in range(i + 1):
                a[i][j] = jnp.broadcast_to(rows[j][:, 8 * k + i : 8 * k + i + 1], (8, 128))
        acols = {
            g: [jnp.broadcast_to(groups[g][:, 8 * k + m : 8 * k + m + 1], (8, 128)) for m in range(8)]
            for g in range(k + 1, n // 8)
        }
        l = [[None] * 8 for _ in range(8)]
        r = [None] * 8
        for j in range(8):
            r[j] = lax.rsqrt(a[j][j])
            for i in range(j + 1, 8):
                l[i][j] = a[i][j] * r[j]
            for i in range(j + 1, 8):
                for c in range(j + 1, i + 1):
                    a[i][c] = a[i][c] - l[i][j] * l[c][j]
        w = [[None] * 8 for _ in range(8)]
        for j in range(8):
            w[j][j] = r[j]
            for i in range(j + 1, 8):
                s = l[i][j] * w[j][j]
                for c in range(j + 1, i):
                    s = s + l[i][c] * w[c][j]
                w[i][j] = -(s * r[i])
        cols = [column([w[i][m] for i in range(8)]) for m in range(8)]
        u = cols[0] * rows[0]
        for m in range(1, 8):
            u = u + cols[m] * rows[m]
        out.append(u)
        if k + 1 < n // 8:
            cols_t = [column([w[j][m] for m in range(8)]) for j in range(8)]
            z = cols_t[0] * jnp.broadcast_to(u[0:1, :], (8, 128))
            for j in range(1, 8):
                z = z + cols_t[j] * jnp.broadcast_to(u[j : j + 1, :], (8, 128))
            z_rows = [jnp.broadcast_to(z[m : m + 1, :], (8, 128)) for m in range(8)]
            for g in range(k + 1, n // 8):
                s = acols[g][0] * z_rows[0]
                for m in range(1, 8):
                    s = s + acols[g][m] * z_rows[m]
                groups[g] = groups[g] - s
    inv = jnp.concatenate(out, axis=0)[:, n:]
    return jnp.where(iota((n, n), 1) <= iota((n, n), 0), inv, 0.0)


def lower_inverse(gram, hook):
    size = gram.shape[0]
    if size == BASE:
        inv = base_inverse(gram)
        hook()
        return inv
    h = size // 2
    i_top = lower_inverse(gram[:h, :h], hook)
    l_side = mm(gram[h:, :h], i_top, NT)
    i_bot = lower_inverse(gram[h:, h:] - mm(l_side, l_side, NT), hook)
    i_side = -mm(i_bot, mm(l_side, i_top))
    top = jnp.concatenate([i_top, jnp.zeros((h, h), F32)], 1)
    return jnp.concatenate([top, jnp.concatenate([i_side, i_bot], 1)], 0)


def upper_base(y):
    n = y.shape[0]
    r, c = iota((n, n), 0), iota((n, n), 1)
    inv = jnp.where(r == c, 1.0 / y, 0.0)
    s = 1
    while s < n:
        off = (r // (2 * s) == c // (2 * s)) & (r // s != c // s) & (r < c)
        inv = inv - mm(inv, mm(jnp.where(off, y, 0.0), inv))
        s *= 2
    return inv


def remote(src, dst, send, recv, peer):
    return pltpu.make_async_remote_copy(
        src_ref=src, dst_ref=dst, send_sem=send, recv_sem=recv, device_id=peer, device_id_type=pl.DeviceIdType.MESH
    )


def place():
    prow, pcol = lax.axis_index("prow"), lax.axis_index("pcol")
    return prow // 2, prow % 2, pcol // NZ, pcol % NZ


ORDER = (1, 7, 2, 6, 3, 5, 4)


def gather(at, send, recv, before=None, hooks=()):
    _, core, x, z = place()

    def slab(xx, zz):
        return at(xx % NX, (zz + 2 * NZ) % NZ)

    def along_z(dx, dist):
        step = 1 if dist <= NZ // 2 else -1
        piece = slab(x + dx, z + step - dist)
        return remote(piece, piece, send.at[dx, dist], recv.at[dx, dist], {"pcol": x * NZ + (z + step + NZ) % NZ})

    def along_x(dx, dist):
        piece = slab(x, z - dist)
        return remote(piece, piece, send.at[dx, dist], recv.at[dx, dist], {"pcol": (x + NX - dx) % NX * NZ + z})

    def arrived(dx, dist):
        piece = slab(x + dx, z - dist)
        remote(piece, piece, send.at[dx, dist], recv.at[dx, dist], {"pcol": x * NZ + (z + 1) % NZ}).wait_recv()

    def passed_on(dx, dist):
        if dist < NZ // 2:
            along_z(dx, dist + 1).start()
        elif dist > NZ // 2 + 1:
            along_z(dx, dist - 1).start()

    @pl.when(core == 0)
    def _():
        along_z(0, 1).start()
        along_z(0, NZ - 1).start()
        for dx in range(1, NX):
            along_x(dx, 0).start()

    @pl.when(core == 1)
    def _():
        for dx in range(1, NX):
            along_x(dx, 0).start()
        along_z(0, 1).start()
        along_z(0, NZ - 1).start()

    if before:
        before()

    @pl.when(core == 1)
    def _():
        for dx in range(1, NX):
            arrived(dx, 0)
            along_z(dx, 1).start()
            along_z(dx, NZ - 1).start()

    for i, dist in enumerate(ORDER):

        @pl.when(core == 0)
        def _():
            arrived(0, dist)
            passed_on(0, dist)
            for dx in range(1, NX):
                along_x(dx, dist).start()
            for dx in range(1, NX):
                arrived(dx, ORDER[i - 1] if i else 0)

        @pl.when(core == 1)
        def _():
            for dx in range(NX):
                arrived(dx, dist)
                passed_on(dx, dist)

        if i < len(hooks):
            hooks[i]()

    @pl.when(core == 0)
    def _():
        for dx in range(1, NX):
            arrived(dx, ORDER[-1])

    def flush():
        for dx in range(NX):
            for dist in range(NZ):
                if dx or dist:
                    piece = slab(x, z)
                    remote(piece, piece, send.at[dx, dist], recv.at[dx, dist], {"pcol": x * NZ + (z + 1) % NZ}).wait_send()

    return flush


class Broadcast:
    def __init__(self, y0, core0, src, out, send, recv):
        y, core, _, _ = place()
        away = (y + NY - y0) % NY
        self.owner = (away == 0) & (core == core0)
        self.next = (away == 1) & (core == core0)
        self.last = (away == 3) & (core == core0)
        self.far_one = (away == 2) & (core == core0)
        self.relay = (away != 0) & (core == core0)
        self.leaf = core != core0
        mate = {"prow": y * 2 + 1 - core}
        up, down = {"prow": (y + 1) % NY * 2 + core}, {"prow": (y + 3) % NY * 2 + core}
        self.up = remote(src, out, send.at[1], recv.at[0], up)
        self.down = remote(src, out, send.at[2], recv.at[0], down)
        self.own = remote(src, out, send.at[0], recv.at[0], mate)
        self.on = remote(out, out, send.at[1], recv.at[0], up)
        self.pass_on = remote(out, out, send.at[0], recv.at[0], mate)
        self.keep = pltpu.make_async_copy(src, out, send.at[3])

    def start(self):
        @pl.when(self.owner)
        def _():
            self.up.start()
            self.down.start()
            self.own.start()
            self.keep.start()

    def near(self):
        @pl.when(self.next)
        def _():
            self.on.wait_recv()
            self.on.start()
            self.pass_on.start()

        @pl.when(self.last)
        def _():
            self.pass_on.wait_recv()
            self.pass_on.start()

    def far(self):
        @pl.when(self.far_one)
        def _():
            self.pass_on.wait_recv()
            self.pass_on.start()

    def finish(self):
        @pl.when(self.relay)
        def _():
            self.pass_on.wait_send()

        @pl.when(self.next)
        def _():
            self.on.wait_send()

        @pl.when(self.leaf)
        def _():
            self.pass_on.wait_recv()

        @pl.when(self.owner)
        def _():
            self.up.wait_send()
            self.down.wait_send()
            self.own.wait_send()
            self.keep.wait()


class DirectSum:
    def __init__(self, s, out, parts, send, recv):
        y, core, _, _ = place()
        self.s, self.out, self.parts, self.send, self.recv = s, out, parts, send, recv
        self.prow = y * 2 + core
        self.q = s.shape[0] // 8

    def rows(self, d):
        return pl.ds(pl.multiple_of((self.prow + d) % 8 * self.q, self.q), self.q)

    def scatter(self, d):
        peer = {"prow": (self.prow + d) % 8}
        return remote(self.s.at[self.rows(d)], self.parts.at[d], self.send.at[0, d], self.recv.at[0, d], peer)

    def spread(self, d):
        mine = self.out.at[self.rows(0)]
        return remote(mine, mine, self.send.at[1, d], self.recv.at[1, d], {"prow": (self.prow + d) % 8})

    def start(self):
        for d in range(1, 8):
            self.scatter(d).start()

    def total(self):
        total = self.s[self.rows(0), :]
        for d in range(1, 8):
            self.scatter(d).wait_recv()
            total = total + self.parts[d]
        return total

    def share(self):
        for d in range(1, 8):
            self.spread(d).start()

    def finish(self):
        for d in range(1, 8):
            self.spread(d).wait_recv()

    def flush(self):
        for d in range(1, 8):
            self.scatter(d).wait_send()
            self.spread(d).wait_send()


class Sum:
    def __init__(self, s, out, half, quarter, acc, send, recv):
        y, core, _, _ = place()
        self.s, self.out, self.half, self.quarter, self.acc, self.send, self.recv = s, out, half, quarter, acc, send, recv
        self.y, self.core = y, core
        self.width = s.shape[1]
        self.q = s.shape[0] // 8
        self.h = 4 * self.q
        self.mate = {"prow": y * 2 + 1 - core}
        self.own = self.rows(core * self.h + y * self.q, self.q)
        self.sent = []

    def rows(self, start, n):
        return pl.ds(pl.multiple_of(start, n), n)

    def copy(self, src, dst, i, peer):
        return remote(src, dst, self.send.at[i], self.recv.at[i], peer)

    def go(self, *args):
        copy = self.copy(*args)
        copy.start()
        self.sent.append(copy)
        return copy

    def along(self, dy):
        return {"prow": (self.y + dy) % NY * 2 + self.core}

    def exchange(self):
        self.first = self.go(self.s.at[self.rows((1 - self.core) * self.h, self.h)], self.half, 0, self.mate)

    def quarters(self):
        self.first.wait_recv()
        self.acc[...] = self.s[self.rows(self.core * self.h, self.h), :] + self.half[...]
        for dy in range(1, NY):
            piece = self.rows((self.y + dy) % NY * self.q, self.q)
            self.go(self.acc.at[piece], self.quarter.at[dy], dy, self.along(dy))

    def total(self):
        total = self.acc[self.rows(self.y * self.q, self.q), :]
        for dy in range(1, NY):
            self.copy(self.quarter.at[dy], self.quarter.at[dy], dy, self.mate).wait_recv()
            total = total + self.quarter[dy]
        self.out[self.own, pl.ds(0, self.width)] = total

    def spread(self):
        piece = self.out.at[self.own]
        for dy in range(1, NY):
            self.go(piece, piece, 3 + dy, self.along(dy))
        self.go(piece, piece, 7, self.mate)

    def forward(self):
        for dy in range(1, NY):
            piece = self.out.at[self.rows(self.core * self.h + (self.y + NY - dy) % NY * self.q, self.q)]
            self.copy(piece, piece, 3 + dy, self.mate).wait_recv()
            self.go(piece, piece, 7 + dy, self.mate)

    def finish(self):
        for dy in range(NY):
            piece = self.out.at[self.rows((1 - self.core) * self.h + (self.y + NY - dy) % NY * self.q, self.q)]
            self.copy(piece, piece, 7 + dy, self.mate).wait_recv()

    def flush(self):
        for copy in self.sent:
            copy.wait_send()


def main_kernel(
    slab_ref,
    a_ref,
    pt_out,
    out_ref,
    c_ref,
    d_ref,
    b_ref,
    l_ref,
    pt_ref,
    a_buf,
    a_hi,
    a_lo,
    ae,
    aet,
    ae64,
    ap64,
    gram,
    gfull,
    gparts,
    aps,
    apt,
    ahalf,
    aquarter,
    aacc,
    ptop,
    pct,
    linv_s,
    t_s,
    mpart,
    mparts,
    mq,
    mx,
    mz,
    mown,
    mraw,
    acopy,
    panel_send,
    panel_recv,
    esend,
    erecv,
    gsend,
    grecv,
    hsend,
    hrecv,
    asend,
    arecv,
    psend,
    precv,
    fsend,
    frecv,
    ksend,
    krecv,
    send,
    recv,
    xsend,
    xrecv,
    zsend,
    zrecv,
    xgsend,
    xgrecv,
    wsend,
    wrecv,
):
    y, core, x, z = place()
    prow, pcol = y * 2 + core, x * NZ + z
    nb = out_ref.shape[1]
    cols = ae.shape[1]
    rows = cols // 8
    q = nb // 8
    wide = slab_ref.shape[1]

    load = pltpu.make_async_copy(a_ref, a_buf, acopy.at[0])
    load.start()
    take = pltpu.make_async_copy(slab_ref, pt_ref.at[x, pl.ds(pl.multiple_of(z * 8, 8), 8)], acopy.at[1])
    take.start()

    to_row, to_col = pcol // 4, pcol % 4 * 8 + core * NY + y
    source_col, j = prow * 4 + pcol // 8, pcol % 8
    stays = (to_row == prow) & (to_col == pcol)
    moves = jnp.logical_not(stays)
    corner = (prow == 0) & (pcol == 0)
    source = {"prow": j % NY * 2 + j // NY, "pcol": source_col}
    barrier = pltpu.get_barrier_semaphore()
    peers = [{"prow": (prow + d) % 8} for d in range(1, 8)]
    peers += [{"pcol": (x + dx) % NX * NZ + z} for dx in range(1, NX)]
    peers += [{"pcol": x * NZ + (z + dz) % NZ} for dz in range(1, NZ)]

    def greet(peer):
        pl.semaphore_signal(barrier, inc=1, device_id=peer, device_id_type=pl.DeviceIdType.MESH)

    for peer in peers:
        greet(peer)

    @pl.when(moves)
    def _():
        greet(source)

    @pl.when(jnp.logical_not(corner))
    def _():
        greet({"prow": 0, "pcol": source_col})

    extra = jnp.where(moves, 1, 0) + jnp.where(prow == 0, 8, 0) - jnp.where(corner, 1, 0)
    pl.semaphore_wait(barrier, len(peers) + extra)
    take.wait()

    top = Broadcast(0, 0, a_ref.at[pl.ds(0, nb)], ae, esend, erecv)
    window = pl.ds(pl.multiple_of(pcol % 4 * cols, cols), cols)
    part = Broadcast(x, z // 4, pt_ref.at[:, :, window], pct, psend, precv)
    head = Broadcast(0, 0, pt_ref.at[:, :, pl.ds(0, nb)], ptop, hsend, hrecv)

    def top_piece(k):
        peer = {"prow": pcol // 4, "pcol": pcol % 4 * 8 + k}
        return remote(aet.at[pl.ds(k * rows, rows)], ae64, ksend.at[k], krecv.at[0], peer)

    def take_a():
        load.wait()
        a_hi[...], a_lo[...] = split(a_buf[...])

        @pl.when(prow == 0)
        def _():
            aet[...] = a_buf[0:nb, :].T
            for k in range(1, 8):
                top_piece(k).start()

        @pl.when((prow == 0) & (pcol != 0))
        def _():
            top_piece(0).start()

        @pl.when(corner)
        def _():
            ae64[...] = aet[0:rows, :]

    panel_flush = gather(
        lambda xx, zz: pt_ref.at[xx, pl.ds(pl.multiple_of(zz * 8, 8), 8)],
        panel_send,
        panel_recv,
        None,
        (lambda: None, take_a),
    )
    keep = pltpu.make_async_copy(pt_ref, pt_out, acopy.at[2])
    keep.start()
    panel = pt_ref[...].reshape(nb, wide)
    gram[...] = mm(panel, panel, NT)

    gsum = DirectSum(gram, gfull, gparts, gsend, grecv)
    asum = Sum(aps, apt, ahalf, aquarter, aacc, asend, arecv)
    msum = DirectSum(mpart, mraw, mparts, wsend, wrecv)
    gsum.start()
    aps[...] = mm3(split(panel), (a_hi[...], a_lo[...])).T
    asum.exchange()
    gfull[gsum.rows(0), :] = gsum.total()
    gsum.share()
    asum.quarters()
    head.start()
    gsum.finish()
    top.start()

    swap = remote(apt.at[asum.own], ap64, fsend.at[0], frecv.at[0], {"prow": to_row, "pcol": to_col})

    def hand_on():
        asum.total()

        @pl.when(moves)
        def _():
            swap.start()

        @pl.when(stays)
        def _():
            ap64[...] = apt[asum.own, :]

    def relay():
        top.near()
        part.start()

    stages = iter([hand_on, head.near, head.far, relay])
    linv = lower_inverse(gfull[...], lambda: next(stages)())
    linv_s[...] = linv

    @pl.when(moves)
    def _():
        swap.wait_recv()

    @pl.when(jnp.logical_not(corner))
    def _():
        top_piece(0).wait_recv()

    out_ref[pl.ds(pl.multiple_of(pcol * rows, rows), rows), :] = mm(ap64[...], linv, NT) - ae64[...]

    def along_x(src, dst, sends, recvs, dx):
        return remote(src, dst, sends.at[dx], recvs.at[dx], {"pcol": (x + dx) % NX * NZ + z})

    def along_z(dz):
        return remote(mown, mz.at[dz], zsend.at[dz], zrecv.at[dz], {"pcol": x * NZ + (z + dz) % NZ})

    def m_scatter():
        lanes = 2 * rows
        block = pcol // 2 * lanes
        p = pt_ref[:, :, pl.ds(pl.multiple_of(block, lanes), lanes)].reshape(nb, lanes)
        row, lane = iota((nb, lanes), 0), iota((nb, lanes), 1)
        v = mm(linv_s[...], p) - (row == lane + block + prow * wide).astype(F32)
        v = jnp.where(lane // rows == pcol % 2, v, 0.0)
        av = out_ref[pl.ds(pl.multiple_of(pcol * rows, rows), rows), :]
        mpart[...] = mm(v, jnp.concatenate([av, av], 0))
        msum.start()

    def m_x():
        mq[...] = msum.total()
        for dx in range(1, NX):
            piece = pl.ds(pl.multiple_of((x + dx) % NX * 8, 8), 8)
            along_x(mq.at[piece], mx.at[dx], xsend, xrecv, dx).start()

    def m_z():
        total = mq[pl.ds(pl.multiple_of(x * 8, 8), 8), :]
        for dx in range(1, NX):
            along_x(mx.at[dx], mx.at[dx], xsend, xrecv, dx).wait_recv()
            total = total + mx[dx]
        mown[...] = total
        for dz in range(1, NZ):
            along_z(dz).start()

    m_rows = pl.ds(pl.multiple_of(prow * q + x * 8, 8), 8)
    m_own = mraw.at[m_rows]

    def m_back():
        total = mown[...]
        for dz in range(1, NZ):
            along_z(dz).wait_recv()
            total = total + mz[dz]
        mraw[m_rows, :] = total
        for dx in range(1, NX):
            along_x(m_own, m_own, xgsend, xgrecv, dx).start()

    def m_share():
        for dx in range(1, NX):
            along_x(m_own, m_own, xgsend, xgrecv, dx).wait_recv()
        msum.share()

    def factor_first():
        linv = linv_s[...]
        first = ptop[...].reshape(nb, nb)
        side = mm(linv, first)
        r, c = iota((nb, nb), 0), iota((nb, nb), 1)
        ygram = 2.0 * (r == c).astype(F32) - side - mm(first, linv, ((0,), (1,)))
        t_s[...] = jnp.where(r < c, ygram, jnp.where(r == c, 0.5 * ygram, 0.0))

    def factor_second():
        blocks = [slice(k * BASE, (k + 1) * BASE) for k in range(nb // BASE)]
        inverses = [upper_base(t_s[k, k]) for k in blocks]
        for k, inverse in zip(blocks, inverses):
            t_s[k, k] = inverse

    def merge(size):
        sides = []
        for k in range(0, nb, 2 * size):
            lo, hi = slice(k, k + size), slice(k + size, k + 2 * size)
            sides.append((lo, hi, -mm(t_s[lo, lo], mm(t_s[lo, hi], t_s[hi, hi]))))
        for lo, hi, side in sides:
            t_s[lo, hi] = side

    def before():
        asum.spread()
        m_scatter()
        head.finish()

    def first():
        factor_first()
        top.far()

    def second():
        m_x()
        asum.forward()

    def third():
        factor_second()
        part.near()

    def fourth():
        m_z()

    def fifth():
        merge(BASE)
        merge(2 * BASE)

    def sixth():
        m_back()
        part.far()

    flush = gather(
        lambda xx, zz: out_ref.at[pl.ds(pl.multiple_of((xx * NZ + zz) * rows, rows), rows)],
        send,
        recv,
        before,
        (first, second, third, fourth, fifth, sixth, m_share),
    )

    asum.finish()
    top.finish()
    part.finish()
    linv, t = linv_s[...], t_s[...]
    e = (iota((nb, cols), 0) == iota((nb, cols), 1)) & (pcol == 0)
    ls, ts = split(linv), split(t)
    vct = mm3(ls, split(pct[...].reshape(nb, cols))) - e.astype(F32)
    vs = split(vct)
    xc = mm3(ts, split(mm3(ls, split(apt[...]), NT) - ae[...]), TN)
    d_ref[...] = mm3(ts, vs)
    msum.finish()
    k = mm3(ts, split(mm3(split(mraw[...]), ts)), TN)
    b = xc - mm3(split(0.5 * (k + k.T)), vs)
    b_ref[...] = b
    c_ref[...] = mm3(ls, split(b), TN)
    sel = (iota((8, nb), 1) == iota((8, nb), 0) + 8 * pcol).astype(F32)
    kt = mm(sel, k, NT)
    l_ref[0:8, :] = kt
    l_ref[8:16, :] = mm(kt, linv)
    l_ref[16:24, :] = mm(sel, t, NT)

    flush()
    panel_flush()
    keep.wait()
    gsum.flush()
    asum.flush()
    msum.flush()

    @pl.when(prow == 0)
    def _():
        for k in range(1, 8):
            top_piece(k).wait_send()

    @pl.when((prow == 0) & (pcol != 0))
    def _():
        top_piece(0).wait_send()

    @pl.when(moves)
    def _():
        swap.wait_send()

    for dx in range(1, NX):
        along_x(mq.at[pl.ds(0, 8)], mx.at[dx], xsend, xrecv, dx).wait_send()
        along_x(m_own, m_own, xgsend, xgrecv, dx).wait_send()
    for dz in range(1, NZ):
        along_z(dz).wait_send()


def params(cid):
    return pltpu.CompilerParams(collective_id=cid, has_side_effects=True, vmem_limit_bytes=LIMIT)


def plain(**kw):
    return pltpu.CompilerParams(vmem_limit_bytes=LIMIT, **kw)


def shape(*dims):
    return jax.ShapeDtypeStruct(dims, F32)


def update_kernel(a_ref, pt_ref, av_ref, c_ref, d_ref, b_ref, l_ref, o_ref, w_ref, ch, cl, dh, dl):
    step = pl.program_id(0)

    @pl.when(step == 0)
    def _():
        ch[...], cl[...] = split(c_ref[...])
        dh[...], dl[...] = split(d_ref[...])

    p, v = pt_ref[...], av_ref[...]
    ps, vs = split(p), split(v)
    both = mm3(ps, (ch[...], cl[...]), TN) + mm3(vs, (dh[...], dl[...]))
    o_ref[...] = a_ref[...] - both
    w_ref[...] = mm3(split(l_ref[16:24, :]), vs, NT) - 0.5 * mm3(split(l_ref[8:16, :]), ps)

    @pl.when((lax.axis_index("prow") == 0) & (step == 0))
    def _():
        nb = b_ref.shape[0]
        o_ref[0:nb, :] += b_ref[...]
        w_ref[:, 0:nb] += 0.5 * l_ref[0:8, :]


def shards(trailing, panel):
    rows, cols = trailing.shape
    pt_own = panel.T
    nc = pt_own.shape[0]
    nb = nc * lax.axis_size("pcol")
    dma = pltpu.SemaphoreType.DMA
    buf = lambda *dims: pltpu.VMEM(dims, F32)

    q = nb // 8
    pt, av, c, d, b, l = pl.pallas_call(
        main_kernel,
        out_shape=(shape(NX, nb // NX, rows), shape(rows, nb)) + (shape(nb, cols),) * 3 + (shape(24, nb),),
        in_specs=[ANY, ANY],
        out_specs=(ANY,) + (VMEM,) * 5,
        scratch_shapes=[
            buf(NX, nb // NX, rows),
            buf(rows, cols),
            pltpu.VMEM((rows, cols), jnp.bfloat16),
            pltpu.VMEM((rows, cols), jnp.bfloat16),
            buf(nb, cols),
            buf(cols, nb),
            buf(cols // 8, nb),
            buf(cols // 8, nb),
            buf(nb, nb),
            buf(nb, nb),
            buf(8, q, nb),
            buf(cols, nb),
            buf(cols, nb),
            buf(cols // 2, nb),
            buf(NY, cols // 8, nb),
            buf(cols // 2, nb),
            buf(NX, nb // NX, nb),
            buf(NX, nb // NX, cols),
            buf(nb, nb),
            buf(nb, nb),
            buf(nb, nb),
            buf(8, q, nb),
            buf(q, nb),
            buf(NX, 8, nb),
            buf(NZ, 8, nb),
            buf(8, nb),
            buf(nb, nb),
            dma((3,)),
            dma((NX, NZ)),
            dma((NX, NZ)),
            dma((4,)),
            dma((1,)),
            dma((2, 8)),
            dma((2, 8)),
            dma((4,)),
            dma((1,)),
            dma((11,)),
            dma((11,)),
            dma((4,)),
            dma((1,)),
            dma((1,)),
            dma((1,)),
            dma((8,)),
            dma((1,)),
            dma((NX, NZ)),
            dma((NX, NZ)),
            dma((NX,)),
            dma((NX,)),
            dma((NZ,)),
            dma((NZ,)),
            dma((NX,)),
            dma((NX,)),
            dma((2, 8)),
            dma((2, 8)),
        ],
        compiler_params=params(2),
    )(pt_own, trailing)

    tile = 2 * nb
    whole = lambda *dims: pl.BlockSpec(dims, lambda i: (0, 0))
    updated, wt = pl.pallas_call(
        update_kernel,
        grid=(rows // tile,),
        out_shape=(shape(rows, cols), shape(nc, rows)),
        in_specs=[
            pl.BlockSpec((tile, cols), lambda i: (i, 0)),
            pl.BlockSpec((nb, tile), lambda i: (0, i)),
            pl.BlockSpec((tile, nb), lambda i: (i, 0)),
            whole(nb, cols),
            whole(nb, cols),
            whole(nb, cols),
            whole(24, nb),
        ],
        out_specs=(pl.BlockSpec((tile, cols), lambda i: (i, 0)), pl.BlockSpec((nc, tile), lambda i: (0, i))),
        scratch_shapes=[pltpu.VMEM((nb, cols), jnp.bfloat16)] * 4,
        compiler_params=plain(dimension_semantics=("arbitrary",)),
    )(trailing, pt.reshape(nb, rows), av, c, d, b, l)
    return updated, wt.T


def solution(mesh):
    in_specs = (P("prow", "pcol"), P("prow", "pcol"))
    out_specs = (P("prow", "pcol"), P("prow", "pcol"))
    return jax.shard_map(shards, mesh=mesh, in_specs=in_specs, out_specs=out_specs, check_vma=False)
```

```python
import jax
import jax.numpy as jnp
from jax import lax
from jax.experimental import pallas as pl
from jax.experimental.pallas import tpu as pltpu
from jax.sharding import PartitionSpec as P

HIGH = lax.Precision.HIGHEST
F32 = jnp.float32
NX, NZ, NY = 4, 8, 4
VMEM = pl.BlockSpec(memory_space=pltpu.VMEM)
ANY = pl.BlockSpec(memory_space=pl.ANY)
LIMIT = 48 << 20
NN, NT, TN = ((1,), (0,)), ((1,), (1,)), ((0,), (0,))


def mm(a, b, dims=NN):
    return lax.dot_general(a, b, (dims, ((), ())), precision=HIGH, preferred_element_type=F32)


def split(x):
    hi = x.astype(jnp.bfloat16)
    return hi, (x - hi.astype(F32)).astype(jnp.bfloat16)


def mm3(a, b, dims=NN):
    (ah, al), (bh, bl) = a, b

    def dot(l, r):
        return lax.dot_general(l, r, (dims, ((), ())), preferred_element_type=F32)

    return dot(ah, bh) + (dot(ah, bl) + dot(al, bh))


def iota(shape, dim):
    return lax.broadcasted_iota(jnp.int32, shape, dim)


BASE = 64


def base_inverse(block):
    n = BASE
    row = iota((8, 128), 0)
    eye = (iota((n, n), 0) == iota((n, n), 1)).astype(F32)
    x = jnp.concatenate([block, eye], axis=1)
    groups = [x[8 * g : 8 * g + 8, :] for g in range(n // 8)]
    zero = jnp.zeros((8, 128), F32)

    def column(vals):
        v = zero
        for i, e in enumerate(vals):
            if e is not None:
                v = jnp.where(row == i, e, v)
        return v

    out = []
    for k in range(n // 8):
        gk = groups[k]
        rows = [jnp.broadcast_to(gk[m : m + 1, :], (8, 128)) for m in range(8)]
        a = [[None] * 8 for _ in range(8)]
        for i in range(8):
            for j in range(i + 1):
                a[i][j] = jnp.broadcast_to(rows[j][:, 8 * k + i : 8 * k + i + 1], (8, 128))
        acols = {
            g: [jnp.broadcast_to(groups[g][:, 8 * k + m : 8 * k + m + 1], (8, 128)) for m in range(8)]
            for g in range(k + 1, n // 8)
        }
        l = [[None] * 8 for _ in range(8)]
        r = [None] * 8
        for j in range(8):
            r[j] = lax.rsqrt(a[j][j])
            for i in range(j + 1, 8):
                l[i][j] = a[i][j] * r[j]
            for i in range(j + 1, 8):
                for c in range(j + 1, i + 1):
                    a[i][c] = a[i][c] - l[i][j] * l[c][j]
        w = [[None] * 8 for _ in range(8)]
        for j in range(8):
            w[j][j] = r[j]
            for i in range(j + 1, 8):
                s = l[i][j] * w[j][j]
                for c in range(j + 1, i):
                    s = s + l[i][c] * w[c][j]
                w[i][j] = -(s * r[i])
        cols = [column([w[i][m] for i in range(8)]) for m in range(8)]
        u = cols[0] * rows[0]
        for m in range(1, 8):
            u = u + cols[m] * rows[m]
        out.append(u)
        if k + 1 < n // 8:
            cols_t = [column([w[j][m] for m in range(8)]) for j in range(8)]
            z = cols_t[0] * jnp.broadcast_to(u[0:1, :], (8, 128))
            for j in range(1, 8):
                z = z + cols_t[j] * jnp.broadcast_to(u[j : j + 1, :], (8, 128))
            z_rows = [jnp.broadcast_to(z[m : m + 1, :], (8, 128)) for m in range(8)]
            for g in range(k + 1, n // 8):
                s = acols[g][0] * z_rows[0]
                for m in range(1, 8):
                    s = s + acols[g][m] * z_rows[m]
                groups[g] = groups[g] - s
    inv = jnp.concatenate(out, axis=0)[:, n:]
    return jnp.where(iota((n, n), 1) <= iota((n, n), 0), inv, 0.0)


def lower_inverse(gram, hook):
    size = gram.shape[0]
    if size == BASE:
        inv = base_inverse(gram)
        hook()
        return inv
    h = size // 2
    i_top = lower_inverse(gram[:h, :h], hook)
    l_side = mm(gram[h:, :h], i_top, NT)
    i_bot = lower_inverse(gram[h:, h:] - mm(l_side, l_side, NT), hook)
    i_side = -mm(i_bot, mm(l_side, i_top))
    top = jnp.concatenate([i_top, jnp.zeros((h, h), F32)], 1)
    return jnp.concatenate([top, jnp.concatenate([i_side, i_bot], 1)], 0)


def upper_base(y):
    n = y.shape[0]
    r, c = iota((n, n), 0), iota((n, n), 1)
    inv = jnp.where(r == c, 1.0 / y, 0.0)
    s = 1
    while s < n:
        off = (r // (2 * s) == c // (2 * s)) & (r // s != c // s) & (r < c)
        inv = inv - mm(inv, mm(jnp.where(off, y, 0.0), inv))
        s *= 2
    return inv


def remote(src, dst, send, recv, peer):
    return pltpu.make_async_remote_copy(
        src_ref=src, dst_ref=dst, send_sem=send, recv_sem=recv, device_id=peer, device_id_type=pl.DeviceIdType.MESH
    )


def place():
    prow, pcol = lax.axis_index("prow"), lax.axis_index("pcol")
    return prow // 2, prow % 2, pcol // NZ, pcol % NZ


ORDER = (1, 7, 2, 6, 3, 5, 4)


def gather(at, send, recv, before=None, hooks=()):
    _, core, x, z = place()

    def slab(xx, zz):
        return at(xx % NX, (zz + 2 * NZ) % NZ)

    def along_z(dx, dist):
        step = 1 if dist <= NZ // 2 else -1
        piece = slab(x + dx, z + step - dist)
        return remote(piece, piece, send.at[dx, dist], recv.at[dx, dist], {"pcol": x * NZ + (z + step + NZ) % NZ})

    def along_x(dx, dist):
        piece = slab(x, z - dist)
        return remote(piece, piece, send.at[dx, dist], recv.at[dx, dist], {"pcol": (x + NX - dx) % NX * NZ + z})

    def arrived(dx, dist):
        piece = slab(x + dx, z - dist)
        remote(piece, piece, send.at[dx, dist], recv.at[dx, dist], {"pcol": x * NZ + (z + 1) % NZ}).wait_recv()

    def passed_on(dx, dist):
        if dist < NZ // 2:
            along_z(dx, dist + 1).start()
        elif dist > NZ // 2 + 1:
            along_z(dx, dist - 1).start()

    @pl.when(core == 0)
    def _():
        along_z(0, 1).start()
        along_z(0, NZ - 1).start()
        for dx in range(1, NX):
            along_x(dx, 0).start()

    @pl.when(core == 1)
    def _():
        for dx in range(1, NX):
            along_x(dx, 0).start()
        along_z(0, 1).start()
        along_z(0, NZ - 1).start()

    if before:
        before()

    @pl.when(core == 1)
    def _():
        for dx in range(1, NX):
            arrived(dx, 0)
            along_z(dx, 1).start()
            along_z(dx, NZ - 1).start()

    for i, dist in enumerate(ORDER):

        @pl.when(core == 0)
        def _():
            arrived(0, dist)
            passed_on(0, dist)
            for dx in range(1, NX):
                along_x(dx, dist).start()
            for dx in range(1, NX):
                arrived(dx, ORDER[i - 1] if i else 0)

        @pl.when(core == 1)
        def _():
            for dx in range(NX):
                arrived(dx, dist)
                passed_on(dx, dist)

        if i < len(hooks):
            hooks[i]()

    @pl.when(core == 0)
    def _():
        for dx in range(1, NX):
            arrived(dx, ORDER[-1])

    def flush():
        for dx in range(NX):
            for dist in range(NZ):
                if dx or dist:
                    piece = slab(x, z)
                    remote(piece, piece, send.at[dx, dist], recv.at[dx, dist], {"pcol": x * NZ + (z + 1) % NZ}).wait_send()

    return flush


class Broadcast:
    def __init__(self, y0, core0, src, out, send, recv):
        y, core, _, _ = place()
        away = (y + NY - y0) % NY
        self.owner = (away == 0) & (core == core0)
        self.next = (away == 1) & (core == core0)
        self.last = (away == 3) & (core == core0)
        self.far_one = (away == 2) & (core == core0)
        self.relay = (away != 0) & (core == core0)
        self.leaf = core != core0
        mate = {"prow": y * 2 + 1 - core}
        up, down = {"prow": (y + 1) % NY * 2 + core}, {"prow": (y + 3) % NY * 2 + core}
        self.up = remote(src, out, send.at[1], recv.at[0], up)
        self.down = remote(src, out, send.at[2], recv.at[0], down)
        self.own = remote(src, out, send.at[0], recv.at[0], mate)
        self.on = remote(out, out, send.at[1], recv.at[0], up)
        self.pass_on = remote(out, out, send.at[0], recv.at[0], mate)
        self.keep = pltpu.make_async_copy(src, out, send.at[3])

    def start(self):
        @pl.when(self.owner)
        def _():
            self.up.start()
            self.down.start()
            self.own.start()
            self.keep.start()

    def near(self):
        @pl.when(self.next)
        def _():
            self.on.wait_recv()
            self.on.start()
            self.pass_on.start()

        @pl.when(self.last)
        def _():
            self.pass_on.wait_recv()
            self.pass_on.start()

    def far(self):
        @pl.when(self.far_one)
        def _():
            self.pass_on.wait_recv()
            self.pass_on.start()

    def finish(self):
        @pl.when(self.relay)
        def _():
            self.pass_on.wait_send()

        @pl.when(self.next)
        def _():
            self.on.wait_send()

        @pl.when(self.leaf)
        def _():
            self.pass_on.wait_recv()

        @pl.when(self.owner)
        def _():
            self.up.wait_send()
            self.down.wait_send()
            self.own.wait_send()
            self.keep.wait()


class DirectSum:
    def __init__(self, s, out, parts, send, recv):
        y, core, _, _ = place()
        self.s, self.out, self.parts, self.send, self.recv = s, out, parts, send, recv
        self.prow = y * 2 + core
        self.q = s.shape[0] // 8

    def rows(self, d):
        return pl.ds(pl.multiple_of((self.prow + d) % 8 * self.q, self.q), self.q)

    def scatter(self, d):
        peer = {"prow": (self.prow + d) % 8}
        return remote(self.s.at[self.rows(d)], self.parts.at[d], self.send.at[0, d], self.recv.at[0, d], peer)

    def spread(self, d):
        mine = self.out.at[self.rows(0)]
        return remote(mine, mine, self.send.at[1, d], self.recv.at[1, d], {"prow": (self.prow + d) % 8})

    def start(self):
        for d in range(1, 8):
            self.scatter(d).start()

    def total(self):
        total = self.s[self.rows(0), :]
        for d in range(1, 8):
            self.scatter(d).wait_recv()
            total = total + self.parts[d]
        return total

    def share(self):
        for d in range(1, 8):
            self.spread(d).start()

    def finish(self):
        for d in range(1, 8):
            self.spread(d).wait_recv()

    def flush(self):
        for d in range(1, 8):
            self.scatter(d).wait_send()
            self.spread(d).wait_send()


class Sum:
    def __init__(self, s, out, half, quarter, acc, send, recv):
        y, core, _, _ = place()
        self.s, self.out, self.half, self.quarter, self.acc, self.send, self.recv = s, out, half, quarter, acc, send, recv
        self.y, self.core = y, core
        self.width = s.shape[1]
        self.q = s.shape[0] // 8
        self.h = 4 * self.q
        self.mate = {"prow": y * 2 + 1 - core}
        self.own = self.rows(core * self.h + y * self.q, self.q)
        self.sent = []

    def rows(self, start, n):
        return pl.ds(pl.multiple_of(start, n), n)

    def copy(self, src, dst, i, peer):
        return remote(src, dst, self.send.at[i], self.recv.at[i], peer)

    def go(self, *args):
        copy = self.copy(*args)
        copy.start()
        self.sent.append(copy)
        return copy

    def along(self, dy):
        return {"prow": (self.y + dy) % NY * 2 + self.core}

    def exchange(self):
        self.first = self.go(self.s.at[self.rows((1 - self.core) * self.h, self.h)], self.half, 0, self.mate)

    def quarters(self):
        self.first.wait_recv()
        self.acc[...] = self.s[self.rows(self.core * self.h, self.h), :] + self.half[...]
        for dy in range(1, NY):
            piece = self.rows((self.y + dy) % NY * self.q, self.q)
            self.go(self.acc.at[piece], self.quarter.at[dy], dy, self.along(dy))

    def total(self):
        total = self.acc[self.rows(self.y * self.q, self.q), :]
        for dy in range(1, NY):
            self.copy(self.quarter.at[dy], self.quarter.at[dy], dy, self.mate).wait_recv()
            total = total + self.quarter[dy]
        self.out[self.own, pl.ds(0, self.width)] = total

    def spread(self):
        piece = self.out.at[self.own]
        for dy in range(1, NY):
            self.go(piece, piece, 3 + dy, self.along(dy))
        self.go(piece, piece, 7, self.mate)

    def forward(self):
        for dy in range(1, NY):
            piece = self.out.at[self.rows(self.core * self.h + (self.y + NY - dy) % NY * self.q, self.q)]
            self.copy(piece, piece, 3 + dy, self.mate).wait_recv()
            self.go(piece, piece, 7 + dy, self.mate)

    def finish(self):
        for dy in range(NY):
            piece = self.out.at[self.rows((1 - self.core) * self.h + (self.y + NY - dy) % NY * self.q, self.q)]
            self.copy(piece, piece, 7 + dy, self.mate).wait_recv()

    def flush(self):
        for copy in self.sent:
            copy.wait_send()


def main_kernel(
    slab_ref,
    a_ref,
    pt_out,
    out_ref,
    c_ref,
    d_ref,
    b_ref,
    l_ref,
    pt_ref,
    a_buf,
    a_hi,
    a_lo,
    ae,
    aet,
    ae64,
    ap64,
    gram,
    gfull,
    gparts,
    aps,
    apt,
    ahalf,
    aquarter,
    aacc,
    ptop,
    pct,
    linv_s,
    t_s,
    mpart,
    mparts,
    mq,
    mx,
    mz,
    mown,
    mraw,
    acopy,
    panel_send,
    panel_recv,
    esend,
    erecv,
    gsend,
    grecv,
    hsend,
    hrecv,
    asend,
    arecv,
    psend,
    precv,
    fsend,
    frecv,
    ksend,
    krecv,
    send,
    recv,
    xsend,
    xrecv,
    zsend,
    zrecv,
    xgsend,
    xgrecv,
    wsend,
    wrecv,
):
    y, core, x, z = place()
    prow, pcol = y * 2 + core, x * NZ + z
    nb = out_ref.shape[1]
    cols = ae.shape[1]
    rows = cols // 8
    q = nb // 8
    wide = slab_ref.shape[1]

    load = pltpu.make_async_copy(a_ref, a_buf, acopy.at[0])
    load.start()
    take = pltpu.make_async_copy(slab_ref, pt_ref.at[x, pl.ds(pl.multiple_of(z * 8, 8), 8)], acopy.at[1])
    take.start()

    to_row, to_col = pcol // 4, pcol % 4 * 8 + core * NY + y
    source_col, j = prow * 4 + pcol // 8, pcol % 8
    stays = (to_row == prow) & (to_col == pcol)
    moves = jnp.logical_not(stays)
    corner = (prow == 0) & (pcol == 0)
    source = {"prow": j % NY * 2 + j // NY, "pcol": source_col}
    barrier = pltpu.get_barrier_semaphore()
    peers = [{"prow": (prow + d) % 8} for d in range(1, 8)]
    peers += [{"pcol": (x + dx) % NX * NZ + z} for dx in range(1, NX)]
    peers += [{"pcol": x * NZ + (z + dz) % NZ} for dz in range(1, NZ)]

    def greet(peer):
        pl.semaphore_signal(barrier, inc=1, device_id=peer, device_id_type=pl.DeviceIdType.MESH)

    for peer in peers:
        greet(peer)

    @pl.when(moves)
    def _():
        greet(source)

    @pl.when(jnp.logical_not(corner))
    def _():
        greet({"prow": 0, "pcol": source_col})

    extra = jnp.where(moves, 1, 0) + jnp.where(prow == 0, 8, 0) - jnp.where(corner, 1, 0)
    pl.semaphore_wait(barrier, len(peers) + extra)
    take.wait()

    top = Broadcast(0, 0, a_ref.at[pl.ds(0, nb)], ae, esend, erecv)
    window = pl.ds(pl.multiple_of(pcol % 4 * cols, cols), cols)
    part = Broadcast(x, z // 4, pt_ref.at[:, :, window], pct, psend, precv)
    head = Broadcast(0, 0, pt_ref.at[:, :, pl.ds(0, nb)], ptop, hsend, hrecv)

    def top_piece(k):
        peer = {"prow": pcol // 4, "pcol": pcol % 4 * 8 + k}
        return remote(aet.at[pl.ds(k * rows, rows)], ae64, ksend.at[k], krecv.at[0], peer)

    def take_a():
        load.wait()
        a_hi[...], a_lo[...] = split(a_buf[...])

        @pl.when(prow == 0)
        def _():
            aet[...] = a_buf[0:nb, :].T
            for k in range(1, 8):
                top_piece(k).start()

        @pl.when((prow == 0) & (pcol != 0))
        def _():
            top_piece(0).start()

        @pl.when(corner)
        def _():
            ae64[...] = aet[0:rows, :]

    def begin():
        top.start()
        take_a()

    panel_flush = gather(
        lambda xx, zz: pt_ref.at[xx, pl.ds(pl.multiple_of(zz * 8, 8), 8)],
        panel_send,
        panel_recv,
        begin,
        (),
    )
    keep = pltpu.make_async_copy(pt_ref, pt_out, acopy.at[2])
    keep.start()
    panel = pt_ref[...].reshape(nb, wide)
    gram[...] = mm(panel, panel, NT)

    gsum = DirectSum(gram, gfull, gparts, gsend, grecv)
    asum = Sum(aps, apt, ahalf, aquarter, aacc, asend, arecv)
    msum = DirectSum(mpart, mraw, mparts, wsend, wrecv)
    gsum.start()
    aps[...] = mm3(split(panel), (a_hi[...], a_lo[...])).T
    asum.exchange()
    gfull[gsum.rows(0), :] = gsum.total()
    gsum.share()
    asum.quarters()
    head.start()
    gsum.finish()

    swap = remote(apt.at[asum.own], ap64, fsend.at[0], frecv.at[0], {"prow": to_row, "pcol": to_col})

    def hand_on():
        asum.total()

        @pl.when(moves)
        def _():
            swap.start()

        @pl.when(stays)
        def _():
            ap64[...] = apt[asum.own, :]

    def relay():
        head.far()
        top.near()

    stages = iter([hand_on, head.near, relay, lambda: None])
    linv = lower_inverse(gfull[...], lambda: next(stages)())
    linv_s[...] = linv

    @pl.when(moves)
    def _():
        swap.wait_recv()

    @pl.when(jnp.logical_not(corner))
    def _():
        top_piece(0).wait_recv()

    out_ref[pl.ds(pl.multiple_of(pcol * rows, rows), rows), :] = mm(ap64[...], linv, NT) - ae64[...]

    def along_x(src, dst, sends, recvs, dx):
        return remote(src, dst, sends.at[dx], recvs.at[dx], {"pcol": (x + dx) % NX * NZ + z})

    def along_z(dz):
        return remote(mown, mz.at[dz], zsend.at[dz], zrecv.at[dz], {"pcol": x * NZ + (z + dz) % NZ})

    def m_scatter():
        lanes = 2 * rows
        block = pcol // 2 * lanes
        p = pt_ref[:, :, pl.ds(pl.multiple_of(block, lanes), lanes)].reshape(nb, lanes)
        row, lane = iota((nb, lanes), 0), iota((nb, lanes), 1)
        v = mm(linv_s[...], p) - (row == lane + block + prow * wide).astype(F32)
        v = jnp.where(lane // rows == pcol % 2, v, 0.0)
        av = out_ref[pl.ds(pl.multiple_of(pcol * rows, rows), rows), :]
        mpart[...] = mm(v, jnp.concatenate([av, av], 0))
        msum.start()

    def m_x():
        mq[...] = msum.total()
        for dx in range(1, NX):
            piece = pl.ds(pl.multiple_of((x + dx) % NX * 8, 8), 8)
            along_x(mq.at[piece], mx.at[dx], xsend, xrecv, dx).start()

    def m_z():
        total = mq[pl.ds(pl.multiple_of(x * 8, 8), 8), :]
        for dx in range(1, NX):
            along_x(mx.at[dx], mx.at[dx], xsend, xrecv, dx).wait_recv()
            total = total + mx[dx]
        mown[...] = total
        for dz in range(1, NZ):
            along_z(dz).start()

    m_rows = pl.ds(pl.multiple_of(prow * q + x * 8, 8), 8)
    m_own = mraw.at[m_rows]

    def m_back():
        total = mown[...]
        for dz in range(1, NZ):
            along_z(dz).wait_recv()
            total = total + mz[dz]
        mraw[m_rows, :] = total
        for dx in range(1, NX):
            along_x(m_own, m_own, xgsend, xgrecv, dx).start()

    def m_share():
        for dx in range(1, NX):
            along_x(m_own, m_own, xgsend, xgrecv, dx).wait_recv()
        msum.share()

    def factor_first():
        linv = linv_s[...]
        first = ptop[...].reshape(nb, nb)
        side = mm(linv, first)
        r, c = iota((nb, nb), 0), iota((nb, nb), 1)
        ygram = 2.0 * (r == c).astype(F32) - side - mm(first, linv, ((0,), (1,)))
        t_s[...] = jnp.where(r < c, ygram, jnp.where(r == c, 0.5 * ygram, 0.0))

    def factor_second():
        blocks = [slice(k * BASE, (k + 1) * BASE) for k in range(nb // BASE)]
        inverses = [upper_base(t_s[k, k]) for k in blocks]
        for k, inverse in zip(blocks, inverses):
            t_s[k, k] = inverse

    def merge(size):
        sides = []
        for k in range(0, nb, 2 * size):
            lo, hi = slice(k, k + size), slice(k + size, k + 2 * size)
            sides.append((lo, hi, -mm(t_s[lo, lo], mm(t_s[lo, hi], t_s[hi, hi]))))
        for lo, hi, side in sides:
            t_s[lo, hi] = side

    def before():
        asum.spread()
        part.start()
        m_scatter()
        head.finish()
        factor_first()
        factor_second()
        merge(BASE)
        merge(2 * BASE)

    def first():
        top.far()

    def second():
        m_x()
        asum.forward()

    def third():
        pass

    def fourth():
        m_z()
        part.near()

    def fifth():
        pass

    def sixth():
        m_back()
        part.far()

    flush = gather(
        lambda xx, zz: out_ref.at[pl.ds(pl.multiple_of((xx * NZ + zz) * rows, rows), rows)],
        send,
        recv,
        before,
        (first, second, third, fourth, fifth, sixth, m_share),
    )

    asum.finish()
    top.finish()
    part.finish()
    linv, t = linv_s[...], t_s[...]
    e = (iota((nb, cols), 0) == iota((nb, cols), 1)) & (pcol == 0)
    ls, ts = split(linv), split(t)
    vct = mm3(ls, split(pct[...].reshape(nb, cols))) - e.astype(F32)
    vs = split(vct)
    xc = mm3(ts, split(mm3(ls, split(apt[...]), NT) - ae[...]), TN)
    d_ref[...] = mm3(ts, vs)
    msum.finish()
    k = mm3(ts, split(mm3(split(mraw[...]), ts)), TN)
    b = xc - mm3(split(0.5 * (k + k.T)), vs)
    b_ref[...] = b
    c_ref[...] = mm3(ls, split(b), TN)
    sel = (iota((8, nb), 1) == iota((8, nb), 0) + 8 * pcol).astype(F32)
    kt = mm(sel, k, NT)
    l_ref[0:8, :] = kt
    l_ref[8:16, :] = mm(kt, linv)
    l_ref[16:24, :] = mm(sel, t, NT)

    flush()
    panel_flush()
    keep.wait()
    gsum.flush()
    asum.flush()
    msum.flush()

    @pl.when(prow == 0)
    def _():
        for k in range(1, 8):
            top_piece(k).wait_send()

    @pl.when((prow == 0) & (pcol != 0))
    def _():
        top_piece(0).wait_send()

    @pl.when(moves)
    def _():
        swap.wait_send()

    for dx in range(1, NX):
        along_x(mq.at[pl.ds(0, 8)], mx.at[dx], xsend, xrecv, dx).wait_send()
        along_x(m_own, m_own, xgsend, xgrecv, dx).wait_send()
    for dz in range(1, NZ):
        along_z(dz).wait_send()


def params(cid):
    return pltpu.CompilerParams(collective_id=cid, has_side_effects=True, vmem_limit_bytes=LIMIT)


def plain(**kw):
    return pltpu.CompilerParams(vmem_limit_bytes=LIMIT, **kw)


def shape(*dims):
    return jax.ShapeDtypeStruct(dims, F32)


def update_kernel(a_ref, pt_ref, av_ref, c_ref, d_ref, b_ref, l_ref, o_ref, w_ref, ch, cl, dh, dl):
    step = pl.program_id(0)

    @pl.when(step == 0)
    def _():
        ch[...], cl[...] = split(c_ref[...])
        dh[...], dl[...] = split(d_ref[...])

    p, v = pt_ref[...], av_ref[...]
    ps, vs = split(p), split(v)
    both = mm3(ps, (ch[...], cl[...]), TN) + mm3(vs, (dh[...], dl[...]))
    o_ref[...] = a_ref[...] - both
    w_ref[...] = mm3(split(l_ref[16:24, :]), vs, NT) - 0.5 * mm3(split(l_ref[8:16, :]), ps)

    @pl.when((lax.axis_index("prow") == 0) & (step == 0))
    def _():
        nb = b_ref.shape[0]
        o_ref[0:nb, :] += b_ref[...]
        w_ref[:, 0:nb] += 0.5 * l_ref[0:8, :]


def shards(trailing, panel):
    rows, cols = trailing.shape
    pt_own = panel.T
    nc = pt_own.shape[0]
    nb = nc * lax.axis_size("pcol")
    dma = pltpu.SemaphoreType.DMA
    buf = lambda *dims: pltpu.VMEM(dims, F32)

    q = nb // 8
    pt, av, c, d, b, l = pl.pallas_call(
        main_kernel,
        out_shape=(shape(NX, nb // NX, rows), shape(rows, nb)) + (shape(nb, cols),) * 3 + (shape(24, nb),),
        in_specs=[ANY, ANY],
        out_specs=(ANY,) + (VMEM,) * 5,
        scratch_shapes=[
            buf(NX, nb // NX, rows),
            buf(rows, cols),
            pltpu.VMEM((rows, cols), jnp.bfloat16),
            pltpu.VMEM((rows, cols), jnp.bfloat16),
            buf(nb, cols),
            buf(cols, nb),
            buf(cols // 8, nb),
            buf(cols // 8, nb),
            buf(nb, nb),
            buf(nb, nb),
            buf(8, q, nb),
            buf(cols, nb),
            buf(cols, nb),
            buf(cols // 2, nb),
            buf(NY, cols // 8, nb),
            buf(cols // 2, nb),
            buf(NX, nb // NX, nb),
            buf(NX, nb // NX, cols),
            buf(nb, nb),
            buf(nb, nb),
            buf(nb, nb),
            buf(8, q, nb),
            buf(q, nb),
            buf(NX, 8, nb),
            buf(NZ, 8, nb),
            buf(8, nb),
            buf(nb, nb),
            dma((3,)),
            dma((NX, NZ)),
            dma((NX, NZ)),
            dma((4,)),
            dma((1,)),
            dma((2, 8)),
            dma((2, 8)),
            dma((4,)),
            dma((1,)),
            dma((11,)),
            dma((11,)),
            dma((4,)),
            dma((1,)),
            dma((1,)),
            dma((1,)),
            dma((8,)),
            dma((1,)),
            dma((NX, NZ)),
            dma((NX, NZ)),
            dma((NX,)),
            dma((NX,)),
            dma((NZ,)),
            dma((NZ,)),
            dma((NX,)),
            dma((NX,)),
            dma((2, 8)),
            dma((2, 8)),
        ],
        compiler_params=params(2),
    )(pt_own, trailing)

    tile = 2 * nb
    whole = lambda *dims: pl.BlockSpec(dims, lambda i: (0, 0))
    updated, wt = pl.pallas_call(
        update_kernel,
        grid=(rows // tile,),
        out_shape=(shape(rows, cols), shape(nc, rows)),
        in_specs=[
            pl.BlockSpec((tile, cols), lambda i: (i, 0)),
            pl.BlockSpec((nb, tile), lambda i: (0, i)),
            pl.BlockSpec((tile, nb), lambda i: (i, 0)),
            whole(nb, cols),
            whole(nb, cols),
            whole(nb, cols),
            whole(24, nb),
        ],
        out_specs=(pl.BlockSpec((tile, cols), lambda i: (i, 0)), pl.BlockSpec((nc, tile), lambda i: (0, i))),
        scratch_shapes=[pltpu.VMEM((nb, cols), jnp.bfloat16)] * 4,
        compiler_params=plain(dimension_semantics=("arbitrary",)),
    )(trailing, pt.reshape(nb, rows), av, c, d, b, l)
    return updated, wt.T


def solution(mesh):
    in_specs = (P("prow", "pcol"), P("prow", "pcol"))
    out_specs = (P("prow", "pcol"), P("prow", "pcol"))
    return jax.shard_map(shards, mesh=mesh, in_specs=in_specs, out_specs=out_specs, check_vma=False)
```

```python
import jax
import jax.numpy as jnp
from jax import lax
from jax.experimental import pallas as pl
from jax.experimental.pallas import tpu as pltpu
from jax.sharding import PartitionSpec as P

HIGH = lax.Precision.HIGHEST
F32 = jnp.float32
NX, NZ, NY = 4, 8, 4
VMEM = pl.BlockSpec(memory_space=pltpu.VMEM)
ANY = pl.BlockSpec(memory_space=pl.ANY)
LIMIT = 48 << 20
NN, NT, TN = ((1,), (0,)), ((1,), (1,)), ((0,), (0,))


def mm(a, b, dims=NN):
    return lax.dot_general(a, b, (dims, ((), ())), precision=HIGH, preferred_element_type=F32)


def split(x):
    hi = x.astype(jnp.bfloat16)
    return hi, (x - hi.astype(F32)).astype(jnp.bfloat16)


def mm3(a, b, dims=NN):
    (ah, al), (bh, bl) = a, b

    def dot(l, r):
        return lax.dot_general(l, r, (dims, ((), ())), preferred_element_type=F32)

    return dot(ah, bh) + (dot(ah, bl) + dot(al, bh))


def iota(shape, dim):
    return lax.broadcasted_iota(jnp.int32, shape, dim)


BASE = 64


def base_inverse(block):
    n = BASE
    row = iota((8, 128), 0)
    eye = (iota((n, n), 0) == iota((n, n), 1)).astype(F32)
    x = jnp.concatenate([block, eye], axis=1)
    groups = [x[8 * g : 8 * g + 8, :] for g in range(n // 8)]
    zero = jnp.zeros((8, 128), F32)

    def column(vals):
        v = zero
        for i, e in enumerate(vals):
            if e is not None:
                v = jnp.where(row == i, e, v)
        return v

    out = []
    for k in range(n // 8):
        gk = groups[k]
        rows = [jnp.broadcast_to(gk[m : m + 1, :], (8, 128)) for m in range(8)]
        a = [[None] * 8 for _ in range(8)]
        for i in range(8):
            for j in range(i + 1):
                a[i][j] = jnp.broadcast_to(rows[j][:, 8 * k + i : 8 * k + i + 1], (8, 128))
        acols = {
            g: [jnp.broadcast_to(groups[g][:, 8 * k + m : 8 * k + m + 1], (8, 128)) for m in range(8)]
            for g in range(k + 1, n // 8)
        }
        l = [[None] * 8 for _ in range(8)]
        r = [None] * 8
        for j in range(8):
            r[j] = lax.rsqrt(a[j][j])
            for i in range(j + 1, 8):
                l[i][j] = a[i][j] * r[j]
            for i in range(j + 1, 8):
                for c in range(j + 1, i + 1):
                    a[i][c] = a[i][c] - l[i][j] * l[c][j]
        w = [[None] * 8 for _ in range(8)]
        for j in range(8):
            w[j][j] = r[j]
            for i in range(j + 1, 8):
                s = l[i][j] * w[j][j]
                for c in range(j + 1, i):
                    s = s + l[i][c] * w[c][j]
                w[i][j] = -(s * r[i])
        cols = [column([w[i][m] for i in range(8)]) for m in range(8)]
        u = cols[0] * rows[0]
        for m in range(1, 8):
            u = u + cols[m] * rows[m]
        out.append(u)
        if k + 1 < n // 8:
            cols_t = [column([w[j][m] for m in range(8)]) for j in range(8)]
            z = cols_t[0] * jnp.broadcast_to(u[0:1, :], (8, 128))
            for j in range(1, 8):
                z = z + cols_t[j] * jnp.broadcast_to(u[j : j + 1, :], (8, 128))
            z_rows = [jnp.broadcast_to(z[m : m + 1, :], (8, 128)) for m in range(8)]
            for g in range(k + 1, n // 8):
                s = acols[g][0] * z_rows[0]
                for m in range(1, 8):
                    s = s + acols[g][m] * z_rows[m]
                groups[g] = groups[g] - s
    inv = jnp.concatenate(out, axis=0)[:, n:]
    return jnp.where(iota((n, n), 1) <= iota((n, n), 0), inv, 0.0)


def lower_inverse(gram, hook):
    size = gram.shape[0]
    if size == BASE:
        inv = base_inverse(gram)
        hook()
        return inv
    h = size // 2
    i_top = lower_inverse(gram[:h, :h], hook)
    l_side = mm(gram[h:, :h], i_top, NT)
    i_bot = lower_inverse(gram[h:, h:] - mm(l_side, l_side, NT), hook)
    i_side = -mm(i_bot, mm(l_side, i_top))
    top = jnp.concatenate([i_top, jnp.zeros((h, h), F32)], 1)
    return jnp.concatenate([top, jnp.concatenate([i_side, i_bot], 1)], 0)


def upper_base(y):
    n = y.shape[0]
    r, c = iota((n, n), 0), iota((n, n), 1)
    inv = jnp.where(r == c, 1.0 / y, 0.0)
    s = 1
    while s < n:
        off = (r // (2 * s) == c // (2 * s)) & (r // s != c // s) & (r < c)
        inv = inv - mm(inv, mm(jnp.where(off, y, 0.0), inv))
        s *= 2
    return inv


def remote(src, dst, send, recv, peer):
    return pltpu.make_async_remote_copy(
        src_ref=src, dst_ref=dst, send_sem=send, recv_sem=recv, device_id=peer, device_id_type=pl.DeviceIdType.MESH
    )


def place():
    prow, pcol = lax.axis_index("prow"), lax.axis_index("pcol")
    return prow // 2, prow % 2, pcol // NZ, pcol % NZ


ORDER = (1, 7, 2, 6, 3, 5, 4)


def gather(at, send, recv, before=None, hooks=()):
    _, core, x, z = place()

    def slab(xx, zz):
        return at(xx % NX, (zz + 2 * NZ) % NZ)

    def along_z(dx, dist):
        step = 1 if dist <= NZ // 2 else -1
        piece = slab(x + dx, z + step - dist)
        return remote(piece, piece, send.at[dx, dist], recv.at[dx, dist], {"pcol": x * NZ + (z + step + NZ) % NZ})

    def along_x(dx, dist):
        piece = slab(x, z - dist)
        return remote(piece, piece, send.at[dx, dist], recv.at[dx, dist], {"pcol": (x + NX - dx) % NX * NZ + z})

    def arrived(dx, dist):
        piece = slab(x + dx, z - dist)
        remote(piece, piece, send.at[dx, dist], recv.at[dx, dist], {"pcol": x * NZ + (z + 1) % NZ}).wait_recv()

    def passed_on(dx, dist):
        if dist < NZ // 2:
            along_z(dx, dist + 1).start()
        elif dist > NZ // 2 + 1:
            along_z(dx, dist - 1).start()

    @pl.when(core == 0)
    def _():
        along_z(0, 1).start()
        along_z(0, NZ - 1).start()
        for dx in range(1, NX):
            along_x(dx, 0).start()

    @pl.when(core == 1)
    def _():
        for dx in range(1, NX):
            along_x(dx, 0).start()
        along_z(0, 1).start()
        along_z(0, NZ - 1).start()

    if before:
        before()

    @pl.when(core == 1)
    def _():
        for dx in range(1, NX):
            arrived(dx, 0)
            along_z(dx, 1).start()
            along_z(dx, NZ - 1).start()

    for i, dist in enumerate(ORDER):

        @pl.when(core == 0)
        def _():
            arrived(0, dist)
            passed_on(0, dist)
            for dx in range(1, NX):
                along_x(dx, dist).start()
            for dx in range(1, NX):
                arrived(dx, ORDER[i - 1] if i else 0)

        @pl.when(core == 1)
        def _():
            for dx in range(NX):
                arrived(dx, dist)
                passed_on(dx, dist)

        if i < len(hooks):
            hooks[i]()

    @pl.when(core == 0)
    def _():
        for dx in range(1, NX):
            arrived(dx, ORDER[-1])

    def flush():
        for dx in range(NX):
            for dist in range(NZ):
                if dx or dist:
                    piece = slab(x, z)
                    remote(piece, piece, send.at[dx, dist], recv.at[dx, dist], {"pcol": x * NZ + (z + 1) % NZ}).wait_send()

    return flush


class Broadcast:
    def __init__(self, y0, core0, src, out, send, recv):
        y, core, _, _ = place()
        away = (y + NY - y0) % NY
        self.owner = (away == 0) & (core == core0)
        self.next = (away == 1) & (core == core0)
        self.last = (away == 3) & (core == core0)
        self.far_one = (away == 2) & (core == core0)
        self.relay = (away != 0) & (core == core0)
        self.leaf = core != core0
        mate = {"prow": y * 2 + 1 - core}
        up, down = {"prow": (y + 1) % NY * 2 + core}, {"prow": (y + 3) % NY * 2 + core}
        self.up = remote(src, out, send.at[1], recv.at[0], up)
        self.down = remote(src, out, send.at[2], recv.at[0], down)
        self.own = remote(src, out, send.at[0], recv.at[0], mate)
        self.on = remote(out, out, send.at[1], recv.at[0], up)
        self.pass_on = remote(out, out, send.at[0], recv.at[0], mate)
        self.keep = pltpu.make_async_copy(src, out, send.at[3])

    def start(self):
        @pl.when(self.owner)
        def _():
            self.up.start()
            self.down.start()
            self.own.start()
            self.keep.start()

    def near(self):
        @pl.when(self.next)
        def _():
            self.on.wait_recv()
            self.on.start()
            self.pass_on.start()

        @pl.when(self.last)
        def _():
            self.pass_on.wait_recv()
            self.pass_on.start()

    def far(self):
        @pl.when(self.far_one)
        def _():
            self.pass_on.wait_recv()
            self.pass_on.start()

    def finish(self):
        @pl.when(self.relay)
        def _():
            self.pass_on.wait_send()

        @pl.when(self.next)
        def _():
            self.on.wait_send()

        @pl.when(self.leaf)
        def _():
            self.pass_on.wait_recv()

        @pl.when(self.owner)
        def _():
            self.up.wait_send()
            self.down.wait_send()
            self.own.wait_send()
            self.keep.wait()


class DirectSum:
    def __init__(self, s, out, parts, send, recv):
        y, core, _, _ = place()
        self.s, self.out, self.parts, self.send, self.recv = s, out, parts, send, recv
        self.prow = y * 2 + core
        self.q = s.shape[0] // 8

    def rows(self, d):
        return pl.ds(pl.multiple_of((self.prow + d) % 8 * self.q, self.q), self.q)

    def scatter(self, d):
        peer = {"prow": (self.prow + d) % 8}
        return remote(self.s.at[self.rows(d)], self.parts.at[d], self.send.at[0, d], self.recv.at[0, d], peer)

    def spread(self, d):
        mine = self.out.at[self.rows(0)]
        return remote(mine, mine, self.send.at[1, d], self.recv.at[1, d], {"prow": (self.prow + d) % 8})

    def start(self):
        for d in range(1, 8):
            self.scatter(d).start()

    def total(self):
        total = self.s[self.rows(0), :]
        for d in range(1, 8):
            self.scatter(d).wait_recv()
            total = total + self.parts[d]
        return total

    def share(self):
        for d in range(1, 8):
            self.spread(d).start()

    def finish(self):
        for d in range(1, 8):
            self.spread(d).wait_recv()

    def flush(self):
        for d in range(1, 8):
            self.scatter(d).wait_send()
            self.spread(d).wait_send()


class Sum:
    def __init__(self, s, out, half, quarter, acc, send, recv):
        y, core, _, _ = place()
        self.s, self.out, self.half, self.quarter, self.acc, self.send, self.recv = s, out, half, quarter, acc, send, recv
        self.y, self.core = y, core
        self.width = s.shape[1]
        self.q = s.shape[0] // 8
        self.h = 4 * self.q
        self.mate = {"prow": y * 2 + 1 - core}
        self.own = self.rows(core * self.h + y * self.q, self.q)
        self.sent = []

    def rows(self, start, n):
        return pl.ds(pl.multiple_of(start, n), n)

    def copy(self, src, dst, i, peer):
        return remote(src, dst, self.send.at[i], self.recv.at[i], peer)

    def go(self, *args):
        copy = self.copy(*args)
        copy.start()
        self.sent.append(copy)
        return copy

    def along(self, dy):
        return {"prow": (self.y + dy) % NY * 2 + self.core}

    def exchange(self):
        self.first = self.go(self.s.at[self.rows((1 - self.core) * self.h, self.h)], self.half, 0, self.mate)

    def quarters(self):
        self.first.wait_recv()
        self.acc[...] = self.s[self.rows(self.core * self.h, self.h), :] + self.half[...]
        for dy in range(1, NY):
            piece = self.rows((self.y + dy) % NY * self.q, self.q)
            self.go(self.acc.at[piece], self.quarter.at[dy], dy, self.along(dy))

    def total(self):
        total = self.acc[self.rows(self.y * self.q, self.q), :]
        for dy in range(1, NY):
            self.copy(self.quarter.at[dy], self.quarter.at[dy], dy, self.mate).wait_recv()
            total = total + self.quarter[dy]
        self.out[self.own, pl.ds(0, self.width)] = total

    def spread(self):
        piece = self.out.at[self.own]
        for dy in range(1, NY):
            self.go(piece, piece, 3 + dy, self.along(dy))
        self.go(piece, piece, 7, self.mate)

    def forward(self):
        for dy in range(1, NY):
            piece = self.out.at[self.rows(self.core * self.h + (self.y + NY - dy) % NY * self.q, self.q)]
            self.copy(piece, piece, 3 + dy, self.mate).wait_recv()
            self.go(piece, piece, 7 + dy, self.mate)

    def finish(self):
        for dy in range(NY):
            piece = self.out.at[self.rows((1 - self.core) * self.h + (self.y + NY - dy) % NY * self.q, self.q)]
            self.copy(piece, piece, 7 + dy, self.mate).wait_recv()

    def flush(self):
        for copy in self.sent:
            copy.wait_send()


def main_kernel(
    slab_ref,
    a_ref,
    pt_out,
    out_ref,
    c_ref,
    d_ref,
    b_ref,
    l_ref,
    pt_ref,
    a_buf,
    a_hi,
    a_lo,
    ae,
    aet,
    ae64,
    ap64,
    gram,
    gfull,
    gparts,
    aps,
    apt,
    ahalf,
    aquarter,
    aacc,
    ptop,
    pct,
    linv_s,
    t_s,
    mpart,
    mparts,
    mq,
    mx,
    mz,
    mown,
    mraw,
    acopy,
    panel_send,
    panel_recv,
    esend,
    erecv,
    gsend,
    grecv,
    hsend,
    hrecv,
    asend,
    arecv,
    psend,
    precv,
    fsend,
    frecv,
    ksend,
    krecv,
    send,
    recv,
    xsend,
    xrecv,
    zsend,
    zrecv,
    xgsend,
    xgrecv,
    wsend,
    wrecv,
):
    y, core, x, z = place()
    prow, pcol = y * 2 + core, x * NZ + z
    nb = out_ref.shape[1]
    cols = ae.shape[1]
    rows = cols // 8
    q = nb // 8
    wide = slab_ref.shape[1]

    load = pltpu.make_async_copy(a_ref, a_buf, acopy.at[0])
    load.start()
    take = pltpu.make_async_copy(slab_ref, pt_ref.at[x, pl.ds(pl.multiple_of(z * 8, 8), 8)], acopy.at[1])
    take.start()

    to_row, to_col = pcol // 4, pcol % 4 * 8 + core * NY + y
    source_col, j = prow * 4 + pcol // 8, pcol % 8
    stays = (to_row == prow) & (to_col == pcol)
    moves = jnp.logical_not(stays)
    corner = (prow == 0) & (pcol == 0)
    source = {"prow": j % NY * 2 + j // NY, "pcol": source_col}
    barrier = pltpu.get_barrier_semaphore()
    peers = [{"prow": (prow + d) % 8} for d in range(1, 8)]
    peers += [{"pcol": (x + dx) % NX * NZ + z} for dx in range(1, NX)]
    peers += [{"pcol": x * NZ + (z + dz) % NZ} for dz in range(1, NZ)]

    def greet(peer):
        pl.semaphore_signal(barrier, inc=1, device_id=peer, device_id_type=pl.DeviceIdType.MESH)

    for peer in peers:
        greet(peer)

    @pl.when(moves)
    def _():
        greet(source)

    @pl.when(jnp.logical_not(corner))
    def _():
        greet({"prow": 0, "pcol": source_col})

    extra = jnp.where(moves, 1, 0) + jnp.where(prow == 0, 8, 0) - jnp.where(corner, 1, 0)
    pl.semaphore_wait(barrier, len(peers) + extra)
    take.wait()

    top = Broadcast(0, 0, a_ref.at[pl.ds(0, nb)], ae, esend, erecv)
    window = pl.ds(pl.multiple_of(pcol % 4 * cols, cols), cols)
    part = Broadcast(x, z // 4, pt_ref.at[:, :, window], pct, psend, precv)
    head = Broadcast(0, 0, pt_ref.at[:, :, pl.ds(0, nb)], ptop, hsend, hrecv)

    def top_piece(k):
        peer = {"prow": pcol // 4, "pcol": pcol % 4 * 8 + k}
        return remote(aet.at[pl.ds(k * rows, rows)], ae64, ksend.at[k], krecv.at[0], peer)

    def take_a():
        load.wait()
        a_hi[...], a_lo[...] = split(a_buf[...])

        @pl.when(prow == 0)
        def _():
            aet[...] = a_buf[0:nb, :].T
            for k in range(1, 8):
                top_piece(k).start()

        @pl.when((prow == 0) & (pcol != 0))
        def _():
            top_piece(0).start()

        @pl.when(corner)
        def _():
            ae64[...] = aet[0:rows, :]

    def begin():
        top.start()
        take_a()

    panel_flush = gather(
        lambda xx, zz: pt_ref.at[xx, pl.ds(pl.multiple_of(zz * 8, 8), 8)],
        panel_send,
        panel_recv,
        begin,
        (),
    )
    keep = pltpu.make_async_copy(pt_ref, pt_out, acopy.at[2])
    keep.start()
    panel = pt_ref[...].reshape(nb, wide)
    gram[...] = mm(panel, panel, NT)

    gsum = DirectSum(gram, gfull, gparts, gsend, grecv)
    asum = Sum(aps, apt, ahalf, aquarter, aacc, asend, arecv)
    msum = DirectSum(mpart, mraw, mparts, wsend, wrecv)
    gsum.start()
    aps[...] = mm3(split(panel), (a_hi[...], a_lo[...])).T
    asum.exchange()
    gfull[gsum.rows(0), :] = gsum.total()
    gsum.share()
    asum.quarters()
    head.start()
    gsum.finish()

    swap = remote(apt.at[asum.own], ap64, fsend.at[0], frecv.at[0], {"prow": to_row, "pcol": to_col})

    def hand_on():
        asum.total()

        @pl.when(moves)
        def _():
            swap.start()

        @pl.when(stays)
        def _():
            ap64[...] = apt[asum.own, :]

    def relay():
        head.far()
        top.near()

    stages = iter([hand_on, head.near, relay, lambda: None])
    linv = lower_inverse(gfull[...], lambda: next(stages)())
    linv_s[...] = linv

    @pl.when(moves)
    def _():
        swap.wait_recv()

    @pl.when(jnp.logical_not(corner))
    def _():
        top_piece(0).wait_recv()

    out_ref[pl.ds(pl.multiple_of(pcol * rows, rows), rows), :] = mm(ap64[...], linv, NT) - ae64[...]

    def along_x(src, dst, sends, recvs, dx):
        return remote(src, dst, sends.at[dx], recvs.at[dx], {"pcol": (x + dx) % NX * NZ + z})

    def along_z(dz):
        return remote(mown, mz.at[dz], zsend.at[dz], zrecv.at[dz], {"pcol": x * NZ + (z + dz) % NZ})

    def m_scatter():
        lanes = 2 * rows
        block = pcol // 2 * lanes
        p = pt_ref[:, :, pl.ds(pl.multiple_of(block, lanes), lanes)].reshape(nb, lanes)
        row, lane = iota((nb, lanes), 0), iota((nb, lanes), 1)
        v = mm(linv_s[...], p) - (row == lane + block + prow * wide).astype(F32)
        v = jnp.where(lane // rows == pcol % 2, v, 0.0)
        av = out_ref[pl.ds(pl.multiple_of(pcol * rows, rows), rows), :]
        mpart[...] = mm(v, jnp.concatenate([av, av], 0))
        msum.start()

    def m_x():
        mq[...] = msum.total()
        for dx in range(1, NX):
            piece = pl.ds(pl.multiple_of((x + dx) % NX * 8, 8), 8)
            along_x(mq.at[piece], mx.at[dx], xsend, xrecv, dx).start()

    def m_z():
        total = mq[pl.ds(pl.multiple_of(x * 8, 8), 8), :]
        for dx in range(1, NX):
            along_x(mx.at[dx], mx.at[dx], xsend, xrecv, dx).wait_recv()
            total = total + mx[dx]
        mown[...] = total
        for dz in range(1, NZ):
            along_z(dz).start()

    m_rows = pl.ds(pl.multiple_of(prow * q + x * 8, 8), 8)
    m_own = mraw.at[m_rows]

    def m_back():
        total = mown[...]
        for dz in range(1, NZ):
            along_z(dz).wait_recv()
            total = total + mz[dz]
        mraw[m_rows, :] = total
        for dx in range(1, NX):
            along_x(m_own, m_own, xgsend, xgrecv, dx).start()

    def m_share():
        for dx in range(1, NX):
            along_x(m_own, m_own, xgsend, xgrecv, dx).wait_recv()
        msum.share()

    def factor_first():
        linv = linv_s[...]
        first = ptop[...].reshape(nb, nb)
        side = mm(linv, first)
        r, c = iota((nb, nb), 0), iota((nb, nb), 1)
        ygram = 2.0 * (r == c).astype(F32) - side - mm(first, linv, ((0,), (1,)))
        t_s[...] = jnp.where(r < c, ygram, jnp.where(r == c, 0.5 * ygram, 0.0))

    def factor_second():
        blocks = [slice(k * BASE, (k + 1) * BASE) for k in range(nb // BASE)]
        inverses = [upper_base(t_s[k, k]) for k in blocks]
        for k, inverse in zip(blocks, inverses):
            t_s[k, k] = inverse

    def merge(size):
        sides = []
        for k in range(0, nb, 2 * size):
            lo, hi = slice(k, k + size), slice(k + size, k + 2 * size)
            sides.append((lo, hi, -mm(t_s[lo, lo], mm(t_s[lo, hi], t_s[hi, hi]))))
        for lo, hi, side in sides:
            t_s[lo, hi] = side

    def before():
        asum.spread()
        part.start()
        m_scatter()
        head.finish()
        factor_first()
        factor_second()
        merge(BASE)
        merge(2 * BASE)

    def first():
        m_x()
        top.far()

    def second():
        asum.forward()
        m_z()

    def fourth():
        m_back()
        part.near()

    def fifth():
        m_share()

    def sixth():
        part.far()
        asum.finish()
        top.finish()

    def last():
        part.finish()
        matrices()

    def matrices():
        linv, t = linv_s[...], t_s[...]
        e = (iota((nb, cols), 0) == iota((nb, cols), 1)) & (pcol == 0)
        ls, ts = split(linv), split(t)
        vct = mm3(ls, split(pct[...].reshape(nb, cols))) - e.astype(F32)
        vs = split(vct)
        xc = mm3(ts, split(mm3(ls, split(apt[...]), NT) - ae[...]), TN)
        d_ref[...] = mm3(ts, vs)
        msum.finish()
        k = mm3(ts, split(mm3(split(mraw[...]), ts)), TN)
        b = xc - mm3(split(0.5 * (k + k.T)), vs)
        b_ref[...] = b
        c_ref[...] = mm3(ls, split(b), TN)
        sel = (iota((8, nb), 1) == iota((8, nb), 0) + 8 * pcol).astype(F32)
        kt = mm(sel, k, NT)
        l_ref[0:8, :] = kt
        l_ref[8:16, :] = mm(kt, linv)
        l_ref[16:24, :] = mm(sel, t, NT)
    flush = gather(
        lambda xx, zz: out_ref.at[pl.ds(pl.multiple_of((xx * NZ + zz) * rows, rows), rows)],
        send,
        recv,
        before,
        (first, second, lambda: None, fourth, fifth, sixth, last),
    )

    flush()
    panel_flush()
    keep.wait()
    gsum.flush()
    asum.flush()
    msum.flush()

    @pl.when(prow == 0)
    def _():
        for k in range(1, 8):
            top_piece(k).wait_send()

    @pl.when((prow == 0) & (pcol != 0))
    def _():
        top_piece(0).wait_send()

    @pl.when(moves)
    def _():
        swap.wait_send()

    for dx in range(1, NX):
        along_x(mq.at[pl.ds(0, 8)], mx.at[dx], xsend, xrecv, dx).wait_send()
        along_x(m_own, m_own, xgsend, xgrecv, dx).wait_send()
    for dz in range(1, NZ):
        along_z(dz).wait_send()


def params(cid):
    return pltpu.CompilerParams(collective_id=cid, has_side_effects=True, vmem_limit_bytes=LIMIT)


def plain(**kw):
    return pltpu.CompilerParams(vmem_limit_bytes=LIMIT, **kw)


def shape(*dims):
    return jax.ShapeDtypeStruct(dims, F32)


def update_kernel(a_ref, pt_ref, av_ref, c_ref, d_ref, b_ref, l_ref, o_ref, w_ref, ch, cl, dh, dl):
    step = pl.program_id(0)

    @pl.when(step == 0)
    def _():
        ch[...], cl[...] = split(c_ref[...])
        dh[...], dl[...] = split(d_ref[...])

    p, v = pt_ref[...], av_ref[...]
    ps, vs = split(p), split(v)
    both = mm3(ps, (ch[...], cl[...]), TN) + mm3(vs, (dh[...], dl[...]))
    o_ref[...] = a_ref[...] - both
    w_ref[...] = mm3(split(l_ref[16:24, :]), vs, NT) - 0.5 * mm3(split(l_ref[8:16, :]), ps)

    @pl.when((lax.axis_index("prow") == 0) & (step == 0))
    def _():
        nb = b_ref.shape[0]
        o_ref[0:nb, :] += b_ref[...]
        w_ref[:, 0:nb] += 0.5 * l_ref[0:8, :]


def shards(trailing, panel):
    rows, cols = trailing.shape
    pt_own = panel.T
    nc = pt_own.shape[0]
    nb = nc * lax.axis_size("pcol")
    dma = pltpu.SemaphoreType.DMA
    buf = lambda *dims: pltpu.VMEM(dims, F32)

    q = nb // 8
    pt, av, c, d, b, l = pl.pallas_call(
        main_kernel,
        out_shape=(shape(NX, nb // NX, rows), shape(rows, nb)) + (shape(nb, cols),) * 3 + (shape(24, nb),),
        in_specs=[ANY, ANY],
        out_specs=(ANY,) + (VMEM,) * 5,
        scratch_shapes=[
            buf(NX, nb // NX, rows),
            buf(rows, cols),
            pltpu.VMEM((rows, cols), jnp.bfloat16),
            pltpu.VMEM((rows, cols), jnp.bfloat16),
            buf(nb, cols),
            buf(cols, nb),
            buf(cols // 8, nb),
            buf(cols // 8, nb),
            buf(nb, nb),
            buf(nb, nb),
            buf(8, q, nb),
            buf(cols, nb),
            buf(cols, nb),
            buf(cols // 2, nb),
            buf(NY, cols // 8, nb),
            buf(cols // 2, nb),
            buf(NX, nb // NX, nb),
            buf(NX, nb // NX, cols),
            buf(nb, nb),
            buf(nb, nb),
            buf(nb, nb),
            buf(8, q, nb),
            buf(q, nb),
            buf(NX, 8, nb),
            buf(NZ, 8, nb),
            buf(8, nb),
            buf(nb, nb),
            dma((3,)),
            dma((NX, NZ)),
            dma((NX, NZ)),
            dma((4,)),
            dma((1,)),
            dma((2, 8)),
            dma((2, 8)),
            dma((4,)),
            dma((1,)),
            dma((11,)),
            dma((11,)),
            dma((4,)),
            dma((1,)),
            dma((1,)),
            dma((1,)),
            dma((8,)),
            dma((1,)),
            dma((NX, NZ)),
            dma((NX, NZ)),
            dma((NX,)),
            dma((NX,)),
            dma((NZ,)),
            dma((NZ,)),
            dma((NX,)),
            dma((NX,)),
            dma((2, 8)),
            dma((2, 8)),
        ],
        compiler_params=params(2),
    )(pt_own, trailing)

    tile = 2 * nb
    whole = lambda *dims: pl.BlockSpec(dims, lambda i: (0, 0))
    updated, wt = pl.pallas_call(
        update_kernel,
        grid=(rows // tile,),
        out_shape=(shape(rows, cols), shape(nc, rows)),
        in_specs=[
            pl.BlockSpec((tile, cols), lambda i: (i, 0)),
            pl.BlockSpec((nb, tile), lambda i: (0, i)),
            pl.BlockSpec((tile, nb), lambda i: (i, 0)),
            whole(nb, cols),
            whole(nb, cols),
            whole(nb, cols),
            whole(24, nb),
        ],
        out_specs=(pl.BlockSpec((tile, cols), lambda i: (i, 0)), pl.BlockSpec((nc, tile), lambda i: (0, i))),
        scratch_shapes=[pltpu.VMEM((nb, cols), jnp.bfloat16)] * 4,
        compiler_params=plain(dimension_semantics=("arbitrary",)),
    )(trailing, pt.reshape(nb, rows), av, c, d, b, l)
    return updated, wt.T


def solution(mesh):
    in_specs = (P("prow", "pcol"), P("prow", "pcol"))
    out_specs = (P("prow", "pcol"), P("prow", "pcol"))
    return jax.shard_map(shards, mesh=mesh, in_specs=in_specs, out_specs=out_specs, check_vma=False)
```
